32 devices in a mesh: section: 4 (over y, x), dp: 8 (over z, core).
Axes of the slice: x: 2, y: 2, z: 4, core: 2. Of those that a mesh axis runs over, the one named last changes fastest.
Arguments:
- patches: bfloat16 [2, 5120, 768], P(None, 'dp'), may hold values from -6 to 6
- positions: bfloat16 [878, 768], replicated, may hold values from -3 to 3
- image_sizes: int32 [2, 8, 6], P(None, 'dp'), may hold values from 0 to 3, as said below
- keep_masks: int32 [2, 8, 6, 4], P(None, 'dp'), may hold values 0 or 1
- output_grad: bfloat16 [2, 5120, 768], P(None, 'dp'), may hold values from -6 to 6
- vector_params: float32 [2, 12, 768], P(None, None, 'dp'), may hold values from -0.9 to 1.6, as said below
- attention_weights: float32 [2, 768, 3072], P(None, 'dp'), may hold values from -0.8660254 to 0.8660254
- feedforward_weights: float32 [2, 2, 768, 3072], P(None, None, 'dp'), may hold values from -0.108253175 to 0.108253175
- vector_first: float32 [2, 12, 768], P(None, None, 'dp'), may hold values from -6 to 6
- attention_first: float32 [2, 768, 3072], P(None, 'dp'), may hold values from -6 to 6
- feedforward_first: float32 [2, 2, 768, 3072], P(None, None, 'dp'), may hold values from -6 to 6
- vector_second: float32 [2, 12, 768], P(None, None, 'dp'), may hold values from 1 to 100
- attention_second: float32 [2, 768, 3072], P(None, 'dp'), may hold values from 1 to 100
- feedforward_second: float32 [2, 2, 768, 3072], P(None, None, 'dp'), may hold values from 1 to 100
- layer_rates: float32 [2], replicated, may hold values from 0.4 to 1
Outputs:
- block_out: bfloat16 [2, 5120, 768], P(None, 'dp', 'section')
- input_grad: float32 [2, 5120, 768], P(None, 'dp', 'section')
- vector_grad: float32 [2, 12, 768], P(None, None, 'dp')
- attention_grad: float32 [2, 768, 3072], P(None, 'dp')
- feedforward_grad: float32 [2, 2, 768, 3072], P(None, None, 'dp')
- vector_mean: float32 [2, 12, 768], P(None, None, 'dp')
- attention_mean: float32 [2, 768, 3072], P(None, 'dp')
- feedforward_mean: float32 [2, 2, 768, 3072], P(None, None, 'dp')
- vector_square: float32 [2, 12, 768], P(None, None, 'dp')
- attention_square: float32 [2, 768, 3072], P(None, 'dp')
- feedforward_square: float32 [2, 2, 768, 3072], P(None, None, 'dp')
- vector_step: float32 [2, 12, 768], P(None, None, 'dp')
- attention_step: float32 [2, 768, 3072], P(None, 'dp')
- feedforward_step: float32 [2, 2, 768, 3072], P(None, None, 'dp')
The draws below stay inside these ranges and needn't reach their ends.
Inputs may be any that keep to these rules, and one draw needn't show every extreme that they name: `image_sizes`: 3 marks an empty slot. The images of the used slots, in slot order, fill the first rows of their unit and fit within its 640 rows; the rest of the unit is padding. `vector_params`: rows 0 and 5 lie near 1, the others near 0.
All inputs are finite; a program needn't handle non-finite values. No bound on the sum of `keep_masks` on one device may be relied on, other than what follows from the above.
Results may differ from the reference program's by a relative error of at most 0.015.
The reference program's roundings to bfloat16 on the way count: a program that leaves them out, or rounds other values in their place, can miss the bound.
Values may be sent and summed in bfloat16 or wider, within the bound.
No kernel may reach another device: no remote copies, remote signals or barrier semaphores. Data moves between devices by JAX's collectives and lax.ppermute only.
A program may use at most 384 MiB of HBM per device.

```python
import math
import jax
import jax.numpy as jnp
from jax import lax

D = 768
H = 12
HD = 64
FF = 3072
GRID_S = 10
GRID_M = 14
GRID_L = 24
TOK_MB = 640
LAYERS = 2
MICRO = 2
SLOTS = 6
DPTOK = 5120
POS_ROWS = 878
N_SECTION = 4
N_DP = 8


def draw_image_sizes(key, part):
    small_len = GRID_S * GRID_S + 2
    middle_len = GRID_M * GRID_M + 2
    large_len = GRID_L * GRID_L + 2
    drawn_ids = jax.random.randint(key, (SLOTS, MICRO, N_DP), 0, 3).astype(jnp.int32)

    def place_slot(used_rows, slot_ids):
        lengths = jnp.where(slot_ids == 0, small_len, jnp.where(slot_ids == 1, middle_len, large_len)).astype(jnp.int32)
        fits_room = used_rows + lengths <= TOK_MB
        next_used = (used_rows + jnp.where(fits_room, lengths, 0)).astype(jnp.int32)
        return (next_used, jnp.where(fits_room, slot_ids, 3).astype(jnp.int32))
    used_rows, chosen = lax.scan(place_slot, jnp.zeros((MICRO, N_DP), jnp.int32), drawn_ids)
    return jnp.transpose(chosen, (1, 2, 0)).astype(jnp.int32)


def draw_vector_params(key, part):
    normal_draw = jnp.clip(jax.random.normal(key, (LAYERS, 12, D), jnp.float32), -3.0, 3.0)
    row_index = jnp.arange(12)
    gain_rows = (row_index == 0) | (row_index == 5)
    return jnp.where(gain_rows[None, :, None], 1.0 + 0.2 * normal_draw, 0.3 * normal_draw).astype(jnp.float32)


def draw_attention_weights(key, part):
    normal_draw = jnp.clip(jax.random.normal(key, (LAYERS, D, 4 * D), jnp.float32), -3.0, 3.0)
    column = jnp.arange(4 * D)
    column_scale = jnp.where(column < 3 * D, D ** (-0.5), (D / 64.0) ** (-0.5))
    return (normal_draw * column_scale[None, None, :]).astype(jnp.float32)


def draw_feedforward_weights(key, part):
    normal_draw = jnp.clip(jax.random.normal(key, (LAYERS, 2, D, FF), jnp.float32), -3.0, 3.0)
    matrix_scale = jnp.array([D ** (-0.5), FF ** (-0.5)], jnp.float32)
    return (normal_draw * matrix_scale[None, :, None, None]).astype(jnp.float32)


def with_ends(drawn, stream_key, smallest, high):
    longest = drawn.shape.index(max(drawn.shape))
    spots = []
    for shift in (0, 1):
        where = [jax.random.randint(jax.random.fold_in(stream_key, axis), (), 0, length) for axis, length in enumerate(drawn.shape)]
        where[longest] = (where[longest] + shift) % drawn.shape[longest]
        spots.append(tuple(where))
    return drawn.at[spots[0]].set(smallest).at[spots[1]].set(high)


def block_scale(stream_key, shape, pieces, low, largest):
    def one(position, blocks):
        draws = jax.random.uniform(jax.random.fold_in(jax.random.fold_in(stream_key, 6), position), (blocks,), jnp.float32, low / len(pieces), largest / len(pieces))
        return jnp.repeat(jnp.exp(draws), shape[position] // blocks).reshape((-1,) + (1,) * (len(shape) - position - 1))

    loudness = one(*pieces[0])
    for cut in pieces[1:]:
        loudness = loudness * one(*cut)
    return loudness


def gaussian(own_key, extent, width, limit, split=(), held_as=jnp.bfloat16):
    values = jax.random.normal(own_key, extent, jnp.float32) * width
    if len(split) > 0:
        values = block_scale(own_key, extent, split, -0.22, 0.18) * values
    return jnp.clip(values, min=-limit, max=limit).astype(held_as)


def setup_inputs(seed: int = 0) -> dict:
    seeds = jax.random.split(jax.random.key(seed), 16)
    return {
        "patches": gaussian(seeds[0], (MICRO, DPTOK, D), 1.0, 6.0, ((1, 8),)),
        "positions": gaussian(seeds[1], (POS_ROWS, D), 0.5, 3.0),
        "image_sizes": draw_image_sizes(jax.random.fold_in(seeds[15], 71), 0),
        "keep_masks": with_ends((jax.random.randint(seeds[3], (MICRO, N_DP, SLOTS, N_SECTION), 0, 10) < 9).astype(jnp.int32), jax.random.fold_in(seeds[3], 1), 0, 1),
        "output_grad": gaussian(seeds[4], (MICRO, DPTOK, D), 1.0, 6.0, ((1, 8),)),
        "vector_params": draw_vector_params(jax.random.fold_in(seeds[15], 71), 0),
        "attention_weights": draw_attention_weights(jax.random.fold_in(seeds[15], 71), 0),
        "feedforward_weights": draw_feedforward_weights(jax.random.fold_in(seeds[15], 71), 0),
        "vector_first": gaussian(seeds[8], (LAYERS, 12, D), 1.0, 6.0, ((2, 8),), jnp.float32),
        "attention_first": gaussian(seeds[9], (LAYERS, D, 4 * D), 1.0, 6.0, ((1, 8),), jnp.float32),
        "feedforward_first": gaussian(seeds[10], (LAYERS, 2, D, FF), 1.0, 6.0, ((2, 8),), jnp.float32),
        "vector_second": jnp.clip(jnp.exp(math.log(100.0) - 4.6051702 * jax.random.uniform(seeds[11], (LAYERS, 12, D), jnp.float32) ** block_scale(seeds[11], (LAYERS, 12, D), ((2, 8),), -0.2, 0.2)), 1.0, 100.0),
        "attention_second": jnp.clip(jnp.exp(math.log(100.0) - 4.6051702 * jax.random.uniform(seeds[12], (LAYERS, D, 4 * D), jnp.float32) ** block_scale(seeds[12], (LAYERS, D, 4 * D), ((1, 8),), -0.2, 0.2)), 1.0, 100.0),
        "feedforward_second": jnp.clip(jnp.exp(math.log(100.0) - 4.6051702 * jax.random.uniform(seeds[13], (LAYERS, 2, D, FF), jnp.float32) ** block_scale(seeds[13], (LAYERS, 2, D, FF), ((2, 8),), -0.2, 0.2)), 1.0, 100.0),
        "layer_rates": jnp.clip(jnp.exp(jax.random.uniform(seeds[14], (LAYERS,), jnp.float32, math.log(0.4), math.log(1.0))), 0.4, 1.0),
    }


@jax.custom_vjp
def low(v):
    return lax.optimization_barrier(v.astype(jnp.bfloat16)).astype(jnp.float32)

@jax.custom_vjp
def low_back(v):
    return v

def low_keep(v):
    return (low(v), None)

def low_pass(kept, grad):
    return (grad,)

def back_keep(v):
    return (v, None)

def back_low(kept, grad):
    return (low(grad),)
low.defvjp(low_keep, low_pass)
low_back.defvjp(back_keep, back_low)
highest = lax.Precision.HIGHEST
beta_one = 0.9
beta_two = 0.999
bias_one = 1.0 - 0.9 ** 10
bias_two = 1.0 - 0.999 ** 10
adam_eps = 1e-08
decay_rate = 0.05
drop_rate = 0.1
norm_eps = 1e-06
masked_score = -1e+30
root_half = 0.7071067811865476

def image_layout(image_ids, row_count):
    small_len = GRID_S * GRID_S + 2
    middle_len = GRID_M * GRID_M + 2
    large_len = GRID_L * GRID_L + 2
    lengths = jnp.where(image_ids == 0, small_len, jnp.where(image_ids == 1, middle_len, jnp.where(image_ids == 2, large_len, 0))).astype(jnp.int32)
    slot_ends = jnp.cumsum(lengths).astype(jnp.int32)
    slot_starts = (slot_ends - lengths).astype(jnp.int32)
    row_index = jnp.arange(row_count, dtype=jnp.int32)
    segment = lax.optimization_barrier(jnp.sum((row_index[:, None] >= slot_ends[None, :]).astype(jnp.int32), axis=1)).astype(jnp.int32)
    member = segment[:, None] == jnp.arange(image_ids.shape[0], dtype=jnp.int32)[None, :]
    first_row = lax.optimization_barrier(jnp.sum(jnp.where(member, slot_starts[None, :], 0), axis=1)).astype(jnp.int32)
    kind_row = lax.optimization_barrier(jnp.sum(jnp.where(member, image_ids[None, :], 0), axis=1)).astype(jnp.int32)
    table_start = jnp.where(kind_row == 0, 0, jnp.where(kind_row == 1, small_len, small_len + middle_len)).astype(jnp.int32)
    in_image = segment < image_ids.shape[0]
    table_row = jnp.where(in_image, table_start + row_index - first_row, 0).astype(jnp.int32)
    return (segment, member, in_image, table_row)

def branch_factor(keep_column, member, in_image):
    kept = lax.optimization_barrier(jnp.sum(jnp.where(member, keep_column[None, :], 0), axis=1)).astype(jnp.float32)
    return jnp.where(in_image, kept / (1.0 - drop_rate), 1.0)

def normalize(hidden, gain, shift):
    center = hidden - lax.optimization_barrier(jnp.mean(hidden, axis=-1, keepdims=True))
    inverse = lax.rsqrt(lax.optimization_barrier(jnp.mean(center * center, axis=-1, keepdims=True)) + norm_eps)
    return center * inverse * gain + shift

def attention_layer(hidden, vector_rows, attn_mats, factor, same_image):
    row_count = hidden.shape[0]
    feature_count = hidden.shape[1]
    normed = low(normalize(hidden, vector_rows[0], vector_rows[1]))
    joined_bias = jnp.concatenate([vector_rows[2], jnp.zeros_like(vector_rows[2]), vector_rows[3]])
    joined = low_back(low(jnp.dot(normed, attn_mats[:, :3 * feature_count], precision=highest) + joined_bias))
    query_rows = joined[:, :feature_count].reshape(row_count, H, HD)
    key_rows = joined[:, feature_count:2 * feature_count].reshape(row_count, H, HD)
    value_rows = joined[:, 2 * feature_count:].reshape(row_count, H, HD)
    scores = low_back(jnp.einsum('qhd,khd->hqk', query_rows, key_rows, precision=highest) * HD ** (-0.5))
    scores = jnp.where(same_image[None], scores, masked_score)
    row_peak = lax.optimization_barrier(jnp.max(scores, axis=-1, keepdims=True))
    exp_scores = jnp.exp(scores - row_peak)
    softmax_out = exp_scores / lax.optimization_barrier(jnp.sum(exp_scores, axis=-1, keepdims=True))
    mixed = low_back(low(jnp.einsum('hqk,khd->qhd', low(softmax_out), value_rows, precision=highest)))
    mixed = mixed.reshape(row_count, feature_count)
    branch = low_back(jnp.dot(mixed, attn_mats[:, 3 * feature_count:], precision=highest) + vector_rows[4])
    return low_back(low(hidden + factor[:, None] * branch))

def feedforward_layer(hidden, vector_rows, ff_mats, factor):
    normed = low(normalize(hidden, vector_rows[5], vector_rows[6]))
    inner = low_back(jnp.dot(normed, ff_mats[0], precision=highest) + vector_rows[8:].reshape(-1))
    activated = low(0.5 * inner * (1.0 + lax.erf(inner * root_half)))
    branch = low_back(jnp.einsum('rf,df->rd', activated, ff_mats[1], precision=highest) + vector_rows[7])
    return low_back(low(hidden + factor[:, None] * branch))

def forward_unit(patch_rows, image_ids, keep_flags, vector_rows, attn_mats, ff_mats, table):
    segment, member, in_image, table_row = image_layout(image_ids, patch_rows.shape[0])
    hidden = patch_rows + jnp.where(in_image[:, None], table[table_row], 0.0)
    same_image = segment[:, None] == segment[None, :]
    for layer_index in range(LAYERS):
        attention_factor = branch_factor(keep_flags[:, 2 * layer_index], member, in_image)
        hidden = attention_layer(hidden, vector_rows[layer_index], attn_mats[layer_index], attention_factor, same_image)
        feed_factor = branch_factor(keep_flags[:, 2 * layer_index + 1], member, in_image)
        hidden = feedforward_layer(hidden, vector_rows[layer_index], ff_mats[layer_index], feed_factor)
    return hidden

def adam_update(weight, first_moment, second_moment, gradient, layer_rates, decay_on):
    layer_rate = layer_rates.reshape((-1,) + (1,) * (weight.ndim - 1))
    mean_next = beta_one * first_moment + (1.0 - beta_one) * gradient
    square_next = beta_two * second_moment + (1.0 - beta_two) * gradient * gradient
    step_next = layer_rate * (mean_next / bias_one / (jnp.sqrt(square_next / bias_two) + adam_eps) + decay_on * weight)
    return (mean_next, square_next, step_next)

def reference(patches, positions, image_sizes, keep_masks, output_grad, vector_params, attention_weights, feedforward_weights, vector_first, attention_first, feedforward_first, vector_second, attention_second, feedforward_second, layer_rates):
    unit_count = MICRO * N_DP
    patch_units = patches.astype(jnp.float32).reshape(unit_count, TOK_MB, D)
    cotangent_units = output_grad.astype(jnp.float32).reshape(unit_count, TOK_MB, D)
    id_units = image_sizes.reshape(unit_count, SLOTS)
    keep_units = keep_masks.reshape(unit_count, SLOTS, N_SECTION)
    table = positions.astype(jnp.float32)

    def unit_step(grad_totals, unit_items):
        patch_rows, image_ids, keep_flags, cotangent = unit_items

        def forward(inputs, vector_rows, attn_mats, ff_mats):
            return forward_unit(inputs, image_ids, keep_flags, low(vector_rows), low(attn_mats), low(ff_mats), table)
        block_rows, pull_back = jax.vjp(forward, patch_rows, vector_params, attention_weights, feedforward_weights)
        input_rows, grad_vector, grad_attention, grad_feedforward = pull_back(cotangent)
        next_totals = (grad_totals[0] + grad_vector, grad_totals[1] + grad_attention, grad_totals[2] + grad_feedforward)
        return (next_totals, (block_rows, input_rows))
    zero_totals = (jnp.zeros_like(vector_params), jnp.zeros_like(attention_weights), jnp.zeros_like(feedforward_weights))
    totals, unit_outputs = lax.scan(unit_step, zero_totals, (patch_units, id_units, keep_units, cotangent_units))
    block_out = unit_outputs[0].reshape(MICRO, N_DP * TOK_MB, D).astype(jnp.bfloat16)
    input_grad = unit_outputs[1].reshape(MICRO, N_DP * TOK_MB, D)
    vector_mean, vector_square, vector_step = adam_update(vector_params, vector_first, vector_second, totals[0], layer_rates, 0.0)
    attention_mean, attention_square, attention_step = adam_update(attention_weights, attention_first, attention_second, totals[1], layer_rates, decay_rate)
    feedforward_mean, feedforward_square, feedforward_step = adam_update(feedforward_weights, feedforward_first, feedforward_second, totals[2], layer_rates, decay_rate)
    return (block_out, input_grad, totals[0], totals[1], totals[2], vector_mean, attention_mean, feedforward_mean, vector_square, attention_square, feedforward_square, vector_step, attention_step, feedforward_step)
```

```python
import functools

import jax
import jax.numpy as jnp
from jax import lax
from jax.experimental import pallas as pl
from jax.experimental.pallas import tpu as pltpu
from jax.sharding import PartitionSpec as P

H = 12
HD = 64
GRID_S = 10
GRID_M = 14
GRID_L = 24

beta_one = 0.9
beta_two = 0.999
bias_one = 1.0 - 0.9**10
bias_two = 1.0 - 0.999**10
adam_eps = 1e-08
decay_rate = 0.05
drop_rate = 0.1
norm_eps = 1e-06
masked_score = -1e30
root_half = 0.7071067811865476
normal_peak = 0.3989422804014327
BF = jnp.bfloat16
F32 = jnp.float32


def image_layout(image_ids, row_count):
    small_len = GRID_S * GRID_S + 2
    middle_len = GRID_M * GRID_M + 2
    large_len = GRID_L * GRID_L + 2
    slots = image_ids.shape[0]
    lengths = jnp.where(
        image_ids == 0,
        small_len,
        jnp.where(image_ids == 1, middle_len, jnp.where(image_ids == 2, large_len, 0)),
    ).astype(jnp.int32)
    slot = jnp.arange(slots, dtype=jnp.int32)
    slot_ends = jnp.sum(jnp.where(slot[None, :] <= slot[:, None], lengths[None, :], 0), axis=1)
    slot_starts = slot_ends - lengths
    row_index = jnp.arange(row_count, dtype=jnp.int32)
    segment = jnp.sum((row_index[:, None] >= slot_ends[None, :]).astype(jnp.int32), axis=1)
    member = segment[:, None] == slot[None, :]
    first_row = jnp.sum(jnp.where(member, slot_starts[None, :], 0), axis=1)
    kind_row = jnp.sum(jnp.where(member, image_ids[None, :], 0), axis=1)
    table_start = jnp.where(
        kind_row == 0, 0, jnp.where(kind_row == 1, small_len, small_len + middle_len)
    ).astype(jnp.int32)
    in_image = segment < slots
    table_row = jnp.where(in_image, table_start + row_index - first_row, 0)
    return (segment, member, in_image, table_row)


def normalize(hidden, gain, shift):
    center = hidden - jnp.mean(hidden, axis=-1, keepdims=True)
    inverse = lax.rsqrt(jnp.mean(center * center, axis=-1, keepdims=True) + norm_eps)
    scaled = center * inverse
    return (scaled * gain + shift, scaled, inverse)


def normalize_back(normed_grad, scaled, inverse, gain):
    scaled_grad = normed_grad * gain
    centered = scaled_grad - jnp.mean(scaled_grad, axis=-1, keepdims=True)
    return inverse * (centered - scaled * jnp.mean(scaled_grad * scaled, axis=-1, keepdims=True))


def nn(a, b):
    return jnp.dot(a, b, preferred_element_type=F32)


def nt(a, b):
    return lax.dot_general(a, b, (((1,), (1,)), ((), ())), preferred_element_type=F32)


def tn(a, b):
    return lax.dot_general(a, b, (((0,), (0,)), ((), ())), preferred_element_type=F32)


def split3(value):
    high = value.astype(BF)
    rest = value - high.astype(F32)
    middle = rest.astype(BF)
    return high, middle, (rest - middle.astype(F32)).astype(BF)


def attention_kernel(q_ref, k_ref, v_ref, code_q_ref, code_k_ref, o_ref, lse_ref):
    low = lax.broadcasted_iota(jnp.int32, q_ref.shape, 1) < HD
    outs = []
    for half in range(2):
        own = low if half == 0 else jnp.logical_not(low)
        q = jnp.where(own, q_ref[...] * jnp.asarray(HD ** (-0.5), BF), code_q_ref[...])
        k = jnp.where(own, k_ref[...], code_k_ref[...])
        scores = nt(q, k)
        peak = jnp.max(scores, axis=-1, keepdims=True)
        e = jnp.exp(scores - peak)
        total = jnp.sum(e, axis=-1, keepdims=True)
        p = (e * (1.0 / total)).astype(BF)
        outs.append(nn(p, v_ref[...]))
        lse_ref[:, half : half + 1] = peak + jnp.log(total)
    o_ref[...] = jnp.where(low, outs[0], outs[1]).astype(BF)


def attention_back_kernel(
    q_ref, k_ref, v_ref, do_ref, lse_ref, code_q_ref, code_k_ref, dq_ref, dk_ref, dv_ref
):
    lane = lax.broadcasted_iota(jnp.int32, q_ref.shape, 1)
    low = lane < HD
    scale = HD ** (-0.5)
    dqs, dks, dvs = [], [], []
    for half in range(2):
        own = low if half == 0 else jnp.logical_not(low)
        spare = 32 + (HD if half == 0 else 0)
        q_scaled = q_ref[...] * jnp.asarray(scale, BF)
        q = jnp.where(own, q_scaled, code_q_ref[...])
        k = jnp.where(own, k_ref[...], code_k_ref[...])
        v = jnp.where(own, v_ref[...], jnp.zeros_like(v_ref[...]))
        for at, part in enumerate(split3(-lse_ref[:, half : half + 1])):
            here = lane == spare + at
            q = jnp.where(here, part, q)
            k = jnp.where(here, jnp.ones_like(k), k)
        p = jnp.exp(nt(k, q))
        dp = nt(v, do_ref[...])
        row = jnp.sum(p * dp, axis=0, keepdims=True)
        ds = (p * (dp - row)).astype(BF)
        dvs.append(nn(p.astype(BF), do_ref[...]))
        dks.append(nn(ds, q_scaled))
        dqs.append(tn(ds, k_ref[...]) * scale)
    dq_ref[...] = jnp.where(low, dqs[0], dqs[1]).astype(BF)
    dk_ref[...] = jnp.where(low, dks[0], dks[1]).astype(BF)
    dv_ref[...] = jnp.where(low, dvs[0], dvs[1]).astype(BF)


def attention(q, k, v, code_q, code_k):
    rows, width = q.shape
    pair = pl.BlockSpec((rows, 2 * HD), lambda i: (0, i))
    whole = pl.BlockSpec((rows, 2 * HD), lambda i: (0, 0))
    return pl.pallas_call(
        attention_kernel,
        grid=(width // (2 * HD),),
        in_specs=[pair, pair, pair, whole, whole],
        out_specs=[pair, pl.BlockSpec((None, rows, 2), lambda i: (i, 0, 0))],
        out_shape=[
            jax.ShapeDtypeStruct((rows, width), BF),
            jax.ShapeDtypeStruct((width // (2 * HD), rows, 2), F32),
        ],
        compiler_params=pltpu.CompilerParams(vmem_limit_bytes=48 * 2**20),
        name="attention",
    )(q, k, v, code_q, code_k)


def attention_back(q, k, v, do, lse, code_q, code_k):
    rows, width = q.shape
    pair = pl.BlockSpec((rows, 2 * HD), lambda i: (0, i))
    whole = pl.BlockSpec((rows, 2 * HD), lambda i: (0, 0))
    return pl.pallas_call(
        attention_back_kernel,
        grid=(width // (2 * HD),),
        in_specs=[pair] * 4
        + [pl.BlockSpec((None, rows, 2), lambda i: (i, 0, 0)), whole, whole],
        out_specs=[pair] * 3,
        out_shape=[jax.ShapeDtypeStruct((rows, width), BF)] * 3,
        compiler_params=pltpu.CompilerParams(vmem_limit_bytes=48 * 2**20),
        name="attention_back",
    )(q, k, v, do, lse, code_q, code_k)


def assemble_kernel(count, at_ref, *refs):
    sources, out_ref, sems = refs[:12], refs[12], refs[13]
    s, z, c = at_ref[0], at_ref[1], at_ref[2]
    share, width = sources[0].shape[2], sources[0].shape[3]
    half = width // 2
    for mat in range(count):

        def place(source, q, chip, core, left=0, size=width, mat=mat):
            row = pl.multiple_of((chip * 2 + core) * share, share)
            target = out_ref.at[mat, q, pl.ds(row, share), pl.ds(left, size)]
            pltpu.make_async_copy(source, target, sems.at[mat]).start()

        for turn in range(2):
            own, far, x_far, y_far, d_left, d_right = sources[turn::2]
            core = c if turn == 0 else 1 - c
            for q in range(4):
                place(own.at[mat, q], q, z, core)
            for k in range(3):
                chip = lax.rem(z + 3 - k, 4)
                place(far.at[k, mat], s, chip, core)
                place(x_far.at[k, mat], s ^ 1, chip, core)
                place(y_far.at[k, mat], s ^ 2, chip, core)
                place(d_left.at[k, mat], s ^ 3, chip, core, 0, half)
                place(d_right.at[k, mat], s ^ 3, chip, core, half, half)
    for mat in range(count):
        pltpu.make_async_copy(out_ref.at[mat], out_ref.at[mat], sems.at[mat]).wait()


def assemble(at, sources):
    count, _, share, width = sources[0].shape
    return pl.pallas_call(
        functools.partial(assemble_kernel, count),
        in_specs=[pl.BlockSpec(memory_space=pltpu.SMEM)] + [pl.BlockSpec(memory_space=pl.ANY)] * 12,
        out_specs=pl.BlockSpec(memory_space=pl.ANY),
        out_shape=jax.ShapeDtypeStruct((count, 4, 8 * share, width), BF),
        scratch_shapes=[pltpu.SemaphoreType.DMA((count,))],
        compiler_params=pltpu.CompilerParams(vmem_limit_bytes=2**20),
        name="assemble",
    )(at, *sources)


def adam_update(weight, first_moment, second_moment, gradient, layer_rates, decay_on):
    layer_rate = layer_rates.reshape((-1,) + (1,) * (weight.ndim - 1))
    mean_next = beta_one * first_moment + (1.0 - beta_one) * gradient
    square_next = beta_two * second_moment + (1.0 - beta_two) * gradient * gradient
    step_next = layer_rate * (
        mean_next / bias_one / (jnp.sqrt(square_next / bias_two) + adam_eps) + decay_on * weight
    )
    return (mean_next, square_next, step_next)


def shards(
    patches,
    positions,
    image_sizes,
    keep_masks,
    output_grad,
    vector_params,
    attention_weights,
    feedforward_weights,
    vector_first,
    attention_first,
    feedforward_first,
    vector_second,
    attention_second,
    feedforward_second,
    layer_rates,
):
    both = ("section", "dp")
    micro_count, row_count, width = patches.shape
    layers = vector_params.shape[0]
    share = attention_weights.shape[1]
    half = width // 2
    s = lax.axis_index("section")
    s_low, s_high = s % 2, s // 2
    unit = s_low ^ s_high
    across = [(i, i ^ 1) for i in range(4)]
    along = [(i, i ^ 2) for i in range(4)]

    def quarter(array):
        return lax.dynamic_slice_in_dim(array, s * width, width, axis=array.ndim - 1)

    shards_dp = lax.axis_size("dp")
    d = lax.axis_index("dp")
    packed = (
        (attention_weights[0],),
        (feedforward_weights[0, 0], feedforward_weights[0, 1]),
        (attention_weights[1],),
        (feedforward_weights[1, 0], feedforward_weights[1, 1]),
    )
    if shards_dp == 8:
        around = [[(i, (i + 2 * k) % 8) for i in range(8)] for k in (1, 2, 3)]
        swap = [(i, i ^ 1) for i in range(8)]
        at = jnp.stack([s, d // 2, d % 2]).astype(jnp.int32)
        flat = vector_params.astype(BF).reshape(-1, share * 8)
        flat = jnp.pad(flat, ((0, 16 - flat.shape[0]), (0, 0)))
        mats, vector_pieces = [], None
        for group, members in enumerate(packed):
            count = len(members)
            own = jnp.stack([quarter(w).astype(BF) for w in members])
            blocks = jnp.stack(
                [w.astype(BF).reshape(share, 4, width).transpose(1, 0, 2) for w in members]
            )
            sent = own.reshape(-1, width)
            if group == 0:
                sent = jnp.concatenate([sent, flat])
            far = [lax.ppermute(sent, "dp", route) for route in around]
            if group == 0:
                vector_pieces = jnp.stack([flat] + [f[count * share :] for f in far])
                far = [f[: count * share] for f in far]
            far = jnp.stack(far).reshape(3, count, share, width)
            x_far = lax.ppermute(far, "section", across)
            y_far = lax.ppermute(far, "section", along)
            d_left = lax.ppermute(y_far[..., :half], "section", across)
            d_right = lax.ppermute(x_far[..., half:], "section", along)
            sources = []
            for piece in (blocks, far, x_far, y_far, d_left, d_right):
                sources += [piece, lax.ppermute(piece, "dp", swap)]
            mats.append(assemble(at, sources))
        both_cores = jnp.stack([vector_pieces, lax.ppermute(vector_pieces, "dp", swap)])
        chips = (d // 2 - jnp.arange(4)) % 4
        order = jnp.where(jnp.arange(4)[:, None] == chips[None, :], 1.0, 0.0).astype(BF)
        both_cores = jnp.einsum("zk,kcrw->zcrw", order, both_cores.transpose(1, 0, 2, 3))
        ordered = jnp.where(d % 2 == 0, both_cores, both_cores[:, ::-1])
        ordered = ordered.reshape(8, -1)[:, : layers * 12 * share].reshape(8, layers, 12, share)
        vectors = ordered.transpose(1, 2, 0, 3).reshape(layers, 12, width).astype(F32)
        weights = [(mats[2 * l][0], mats[2 * l + 1][0], mats[2 * l + 1][1]) for l in range(layers)]
    else:

        def gathered(piece):
            piece = lax.all_gather(quarter(piece).astype(BF), both, axis=0, tiled=True)
            return piece.reshape(4, width, width)

        vectors = lax.all_gather(vector_params.astype(BF), "dp", axis=2, tiled=True).astype(F32)
        mats = [[gathered(w) for w in members] for members in packed]
        weights = [(mats[2 * l][0], mats[2 * l + 1][0], mats[2 * l + 1][1]) for l in range(layers)]

    image_ids = lax.dynamic_index_in_dim(image_sizes[:, 0], unit, 0, keepdims=False)
    keep = lax.dynamic_index_in_dim(keep_masks[:, 0], unit, 0, keepdims=False)
    segment, member, inside, table_row = image_layout(image_ids, row_count)
    kept = jnp.sum(jnp.where(member[:, :, None], keep[None], 0), axis=1).astype(F32)
    factors = jnp.where(inside[:, None], kept / (1.0 - drop_rate), 1.0)
    patch_rows = lax.dynamic_index_in_dim(patches, unit, 0, keepdims=False).astype(F32)
    position_rows = jnp.take(positions, table_row, axis=0).astype(F32)
    hidden = patch_rows + jnp.where(inside[:, None], position_rows, 0.0)
    lane = jnp.arange(2 * HD, dtype=jnp.int32) % HD
    coded = lane[None, :] == segment[:, None]
    code_q = coded.astype(BF)
    code_k = jnp.where(coded | (lane[None, :] > image_sizes.shape[2]), 0.0, masked_score).astype(BF)

    saved = []
    for layer in range(layers):
        wa, w1, w2 = weights[layer]
        vec = [vectors[layer, i : i + 1] for i in range(12)]
        fa = factors[:, 2 * layer : 2 * layer + 1]
        ff = factors[:, 2 * layer + 1 : 2 * layer + 2]
        a, scaled, inverse = normalize(hidden, vec[0], vec[1])
        a = a.astype(BF)
        q = (nn(a, wa[0]) + vec[2]).astype(BF)
        k = nn(a, wa[1]).astype(BF)
        v = (nn(a, wa[2]) + vec[3]).astype(BF)
        o, lse = attention(q, k, v, code_q, code_k)
        mid = (hidden + fa * (nn(o, wa[3]) + vec[4])).astype(BF).astype(F32)
        a2, scaled2, inverse2 = normalize(mid, vec[5], vec[6])
        a2 = a2.astype(BF)
        gbs, slopes = [], []
        branch = vec[7]
        for part in range(4):
            u = nn(a2, w1[part]) + vec[8 + part]
            cdf = 0.5 * (1.0 + lax.erf(u * root_half))
            gb = (u * cdf).astype(BF)
            slopes.append(cdf + u * jnp.exp(-0.5 * u * u) * normal_peak)
            gbs.append(gb)
            branch = branch + nt(gb, w2[part])
        saved.append((hidden, a, q, k, v, o, lse, mid, a2, gbs, slopes))
        hidden = (mid + ff * branch).astype(BF).astype(F32)

    def pick(index, options):
        value = options[0]
        for at in range(1, len(options)):
            value = jnp.where(index == at, options[at], value)
        return value

    def reduced(pairs, rows):
        count = len(pairs)
        summed = []
        extra = jnp.pad(jnp.concatenate(rows), ((0, 128 - len(rows)), (0, 0))).T.astype(BF)
        for xy, (side, route) in enumerate(((s_low, across), (s_high, along))):
            parts = [pair[xy].astype(BF) for pair in pairs]
            mine = [lax.dynamic_slice_in_dim(part, side * half, half, 1) for part in parts]
            other = [lax.dynamic_slice_in_dim(part, (1 - side) * half, half, 1) for part in parts]
            if xy == 0:
                mine.append(extra)
                other.append(extra)
            mine = jnp.concatenate(mine, axis=1)
            other = lax.ppermute(jnp.concatenate(other, axis=1), "section", route)
            summed.append((mine.astype(F32) + other.astype(F32)).astype(BF))
        stacked = jnp.concatenate(summed, axis=1)
        scattered = lax.psum_scatter(stacked, "dp", scatter_dimension=0, tiled=True)
        cut = count * half
        vector = scattered[:, cut : cut + len(rows)].astype(F32).T
        everyone = jnp.concatenate([scattered[:, :cut], scattered[:, cut + 128 :]], axis=1)
        everyone = lax.all_gather(everyone, "section", axis=0, tiled=False)
        everyone = everyone.reshape(4, share, 2, count, half)
        order = ((0, 0), (1, 0), (0, 1), (2, 1), (2, 0), (3, 0), (1, 1), (3, 1))
        return vector, [
            jnp.concatenate([everyone[dev, :, xy, mat] for dev, xy in order], axis=1).astype(F32)
            for mat in range(count)
        ]

    up = lax.dynamic_index_in_dim(output_grad, unit, 0, keepdims=False).astype(F32)
    vector_grads = [None] * layers
    attention_grads = [None] * layers
    feed_grads = [None] * layers
    for layer in reversed(range(layers)):
        wa, w1, w2 = weights[layer]
        vec = [vectors[layer, i : i + 1] for i in range(12)]
        fa = factors[:, 2 * layer : 2 * layer + 1]
        ff = factors[:, 2 * layer + 1 : 2 * layer + 2]
        start, a, q, k, v, o, lse, mid, a2, gbs, slopes = saved[layer]
        eb = (ff * up).astype(BF)
        bias2 = jnp.sum(eb.astype(F32), axis=0, keepdims=True)
        dus = []
        dn = 0.0
        for part in range(4):
            du = (nn(eb, w2[part]) * slopes[part]).astype(BF)
            dus.append(du)
            dn = dn + nt(du, w1[part])
        first_bias = [jnp.sum(du.astype(F32), axis=0, keepdims=True) for du in dus]
        du_x = jnp.where(s_high == 0, dus[0], dus[2])
        du_y = jnp.where(s_low == 0, dus[1], dus[3])
        gb_x = jnp.where(s_high == 0, gbs[0], gbs[2])
        gb_y = jnp.where(s_low == 0, gbs[1], gbs[3])
        _, scaled, inverse = normalize(mid, vec[5], vec[6])
        gain2 = jnp.sum(dn * scaled, axis=0, keepdims=True)
        shift2 = jnp.sum(dn, axis=0, keepdims=True)
        up = (up + normalize_back(dn, scaled, inverse, vec[5])).astype(BF).astype(F32)
        feed_rows, feed = reduced(
            [(tn(a2, du_x), tn(a2, du_y)), (tn(eb, gb_x), tn(eb, gb_y))],
            [gain2, shift2, bias2] + first_bias,
        )

        eb = (fa * up).astype(BF)
        out_bias = jnp.sum(eb.astype(F32), axis=0, keepdims=True)
        do = nt(eb, wa[3]).astype(BF)
        dq, dk, dv = attention_back(q, k, v, do, lse, code_q, code_k)
        dn = nt(dq, wa[0]) + nt(dk, wa[1]) + nt(dv, wa[2])
        query_bias = jnp.sum(dq.astype(F32), axis=0, keepdims=True)
        value_bias = jnp.sum(dv.astype(F32), axis=0, keepdims=True)
        _, scaled, inverse = normalize(start, vec[0], vec[1])
        gain1 = jnp.sum(dn * scaled, axis=0, keepdims=True)
        shift1 = jnp.sum(dn, axis=0, keepdims=True)
        up = up + normalize_back(dn, scaled, inverse, vec[0])
        if layer > 0:
            up = up.astype(BF).astype(F32)
        grad_x = tn(a, jnp.where(s_high == 0, dq, dv))
        grad_y = tn(jnp.where(s_low == 0, a, o), jnp.where(s_low == 0, dk, eb))
        attention_rows, done = reduced(
            [(grad_x, grad_y)], [gain1, shift1, query_bias, value_bias, out_bias]
        )
        attention_grads[layer] = done[0]
        feed_grads[layer] = jnp.stack(feed)
        vector_grads[layer] = jnp.concatenate([attention_rows, feed_rows])

    def outward(rows):
        blocks = [rows[:, i * (width // 4) : (i + 1) * (width // 4)] for i in range(4)]
        mine = pick(s, blocks)
        theirs = lax.ppermute(pick(s ^ 1, blocks), "section", across)
        return jnp.where(unit == 0, jnp.stack([mine, theirs]), jnp.stack([theirs, mine]))

    block_result = outward(hidden.astype(BF))
    input_result = outward(up.astype(BF)).astype(F32)

    vector_grad = jnp.stack(vector_grads)
    attention_grad = jnp.stack(attention_grads)
    feedforward_grad = jnp.stack(feed_grads)
    vector_mean, vector_square, vector_step = adam_update(
        vector_params, vector_first, vector_second, vector_grad, layer_rates, 0.0
    )
    attention_mean, attention_square, attention_step = adam_update(
        attention_weights,
        attention_first,
        attention_second,
        attention_grad,
        layer_rates,
        decay_rate,
    )
    feedforward_mean, feedforward_square, feedforward_step = adam_update(
        feedforward_weights,
        feedforward_first,
        feedforward_second,
        feedforward_grad,
        layer_rates,
        decay_rate,
    )
    return (
        block_result,
        input_result,
        vector_grad,
        attention_grad,
        feedforward_grad,
        vector_mean,
        attention_mean,
        feedforward_mean,
        vector_square,
        attention_square,
        feedforward_square,
        vector_step,
        attention_step,
        feedforward_step,
    )


def solution(mesh):
    in_specs = (
        P(None, "dp", None),
        P(),
        P(None, "dp", None),
        P(None, "dp", None, None),
        P(None, "dp", None),
        P(None, None, "dp"),
        P(None, "dp", None),
        P(None, None, "dp", None),
        P(None, None, "dp"),
        P(None, "dp", None),
        P(None, None, "dp", None),
        P(None, None, "dp"),
        P(None, "dp", None),
        P(None, None, "dp", None),
        P(),
    )
    out_specs = (
        P(None, "dp", "section"),
        P(None, "dp", "section"),
        P(None, None, "dp"),
        P(None, "dp", None),
        P(None, None, "dp", None),
        P(None, None, "dp"),
        P(None, "dp", None),
        P(None, None, "dp", None),
        P(None, None, "dp"),
        P(None, "dp", None),
        P(None, None, "dp", None),
        P(None, None, "dp"),
        P(None, "dp", None),
        P(None, None, "dp", None),
    )
    return jax.shard_map(shards, mesh=mesh, in_specs=in_specs, out_specs=out_specs, check_vma=False)
```

```python
import functools

import jax
import jax.numpy as jnp
from jax import lax
from jax.experimental import pallas as pl
from jax.experimental.pallas import tpu as pltpu
from jax.sharding import PartitionSpec as P

H = 12
HD = 64
GRID_S = 10
GRID_M = 14
GRID_L = 24

beta_one = 0.9
beta_two = 0.999
bias_one = 1.0 - 0.9**10
bias_two = 1.0 - 0.999**10
adam_eps = 1e-08
decay_rate = 0.05
drop_rate = 0.1
norm_eps = 1e-06
masked_score = -1e30
root_half = 0.7071067811865476
normal_peak = 0.3989422804014327
BF = jnp.bfloat16
F32 = jnp.float32


def image_layout(image_ids, row_count):
    small_len = GRID_S * GRID_S + 2
    middle_len = GRID_M * GRID_M + 2
    large_len = GRID_L * GRID_L + 2
    slots = image_ids.shape[0]
    lengths = jnp.where(
        image_ids == 0,
        small_len,
        jnp.where(image_ids == 1, middle_len, jnp.where(image_ids == 2, large_len, 0)),
    ).astype(jnp.int32)
    slot = jnp.arange(slots, dtype=jnp.int32)
    slot_ends = jnp.sum(jnp.where(slot[None, :] <= slot[:, None], lengths[None, :], 0), axis=1)
    slot_starts = slot_ends - lengths
    row_index = jnp.arange(row_count, dtype=jnp.int32)
    segment = jnp.sum((row_index[:, None] >= slot_ends[None, :]).astype(jnp.int32), axis=1)
    member = segment[:, None] == slot[None, :]
    first_row = jnp.sum(jnp.where(member, slot_starts[None, :], 0), axis=1)
    kind_row = jnp.sum(jnp.where(member, image_ids[None, :], 0), axis=1)
    table_start = jnp.where(
        kind_row == 0, 0, jnp.where(kind_row == 1, small_len, small_len + middle_len)
    ).astype(jnp.int32)
    in_image = segment < slots
    table_row = jnp.where(in_image, table_start + row_index - first_row, 0)
    return (segment, member, in_image, table_row)


def nn(a, b):
    return jnp.dot(a, b, preferred_element_type=F32)


def nt(a, b):
    return lax.dot_general(a, b, (((1,), (1,)), ((), ())), preferred_element_type=F32)


def tn(a, b):
    return lax.dot_general(a, b, (((0,), (0,)), ((), ())), preferred_element_type=F32)


def split3(value):
    high = value.astype(BF)
    rest = value - high.astype(F32)
    middle = rest.astype(BF)
    return high, middle, (rest - middle.astype(F32)).astype(BF)


def attention_kernel(q_ref, k_ref, v_ref, code_q_ref, code_k_ref, o_ref, lse_ref):
    low = lax.broadcasted_iota(jnp.int32, q_ref.shape, 1) < HD
    outs = []
    for half in range(2):
        own = low if half == 0 else jnp.logical_not(low)
        q = jnp.where(own, q_ref[...] * jnp.asarray(HD ** (-0.5), BF), code_q_ref[...])
        k = jnp.where(own, k_ref[...], code_k_ref[...])
        scores = nt(q, k)
        peak = jnp.max(scores, axis=-1, keepdims=True)
        e = jnp.exp(scores - peak)
        total = jnp.sum(e, axis=-1, keepdims=True)
        p = (e * (1.0 / total)).astype(BF)
        outs.append(nn(p, v_ref[...]))
        lse_ref[:, half : half + 1] = peak + jnp.log(total)
    o_ref[...] = jnp.where(low, outs[0], outs[1]).astype(BF)


def attention_back_kernel(
    q_ref, k_ref, v_ref, do_ref, lse_ref, code_q_ref, code_k_ref, out_ref
):
    lane = lax.broadcasted_iota(jnp.int32, q_ref.shape, 1)
    low = lane < HD
    scale = HD ** (-0.5)
    dqs, dks, dvs = [], [], []
    for half in range(2):
        own = low if half == 0 else jnp.logical_not(low)
        spare = 32 + (HD if half == 0 else 0)
        q_scaled = q_ref[...] * jnp.asarray(scale, BF)
        q = jnp.where(own, q_scaled, code_q_ref[...])
        k = jnp.where(own, k_ref[...], code_k_ref[...])
        v = jnp.where(own, v_ref[...], jnp.zeros_like(v_ref[...]))
        for at, part in enumerate(split3(-lse_ref[:, half : half + 1])):
            here = lane == spare + at
            q = jnp.where(here, part, q)
            k = jnp.where(here, jnp.ones_like(k), k)
        p = jnp.exp(nt(k, q))
        dp = nt(v, do_ref[...])
        row = jnp.sum(p * dp, axis=0, keepdims=True)
        ds = (p * (dp - row)).astype(BF)
        dvs.append(nn(p.astype(BF), do_ref[...]))
        dks.append(nn(ds, q_scaled))
        dqs.append(tn(ds, k_ref[...]) * scale)
    out_ref[0] = jnp.where(low, dqs[0], dqs[1]).astype(BF)
    out_ref[1] = jnp.where(low, dks[0], dks[1]).astype(BF)
    out_ref[2] = jnp.where(low, dvs[0], dvs[1]).astype(BF)


VMEM_LIMIT = 56 * 2**20


def cost(microseconds):
    return pl.CostEstimate(flops=int(microseconds * 1.1e9), bytes_accessed=2**20, transcendentals=0)


def centered(hidden):
    center = hidden - jnp.mean(hidden, axis=-1, keepdims=True)
    inverse = lax.rsqrt(jnp.mean(center * center, axis=-1, keepdims=True) + norm_eps)
    return center * inverse, inverse


def normalize_back(normed_grad, scaled, inverse, gain):
    scaled_grad = normed_grad * gain
    mid = scaled_grad - jnp.mean(scaled_grad, axis=-1, keepdims=True)
    return inverse * (mid - scaled * jnp.mean(scaled_grad * scaled, axis=-1, keepdims=True))


def column_sum(value):
    return jnp.sum(value, axis=0, keepdims=True)


def view(weight, index):
    specs = []
    for array in weight[1]:
        if weight[0] == "full":
            _, n, _, share, width = array.shape
            specs.append(
                pl.BlockSpec((None, n, None, share, width), lambda p: (index(p), 0, weight[2], 0, 0))
            )
        else:
            _, _, n, share, width = array.shape
            specs.append(
                pl.BlockSpec((None, None, n, share, width), lambda p: (weight[2], index(p), 0, 0, 0))
            )
    return specs


def load(refs, core, held):
    n, share, width = refs[0].shape
    if len(refs) == 1:
        return refs[0][...].reshape(n * share, width)
    for turn, ref in enumerate(refs):
        side = core if turn == 0 else 1 - core
        for chip in range(n):
            row = pl.multiple_of((2 * chip + side) * share, share)
            held[pl.ds(row, share), :] = ref[chip]
    return held[...]


SMEM = pl.BlockSpec(memory_space=pltpu.SMEM)


def project_kernel(count, at_ref, hidden_ref, vec_ref, *refs):
    normed_ref, joined_ref, held = refs[count:]
    weight = load(refs[:count], at_ref[2], held)
    part = pl.program_id(0)

    @pl.when(part == 0)
    def _():
        scaled, _ = centered(hidden_ref[...].astype(F32))
        normed_ref[...] = (scaled * vec_ref[0:1] + vec_ref[1:2]).astype(BF)

    bias = jnp.where(part == 0, vec_ref[2:3], jnp.where(part == 2, vec_ref[3:4], 0.0))
    joined_ref[...] = (nn(normed_ref[...], weight) + bias).astype(BF)


def project(at, hidden, vec, wa):
    rows, width = hidden.shape
    whole = pl.BlockSpec((rows, width), lambda p: (0, 0))
    return pl.pallas_call(
        functools.partial(project_kernel, len(wa[1])),
        grid=(3,),
        in_specs=[SMEM, whole, pl.BlockSpec(vec.shape, lambda p: (0, 0))] + view(wa, lambda p: p),
        out_specs=[whole, pl.BlockSpec((None, rows, width), lambda p: (p, 0, 0))],
        out_shape=[
            jax.ShapeDtypeStruct((rows, width), BF),
            jax.ShapeDtypeStruct((3, rows, width), BF),
        ],
        compiler_params=pltpu.CompilerParams(vmem_limit_bytes=VMEM_LIMIT),
        scratch_shapes=[pltpu.VMEM((width, width), BF)],
        cost_estimate=cost(7),
        name="project",
    )(at, hidden, vec, *wa[1])


def feed_kernel(count, at_ref, hidden_ref, o_ref, vec_ref, factor_ref, *refs):
    mid_ref, normed_ref, gb_ref, slope_ref, out_ref, total, held1, held2 = refs[3 * count :]
    part = pl.program_id(0)
    core = at_ref[2]

    @pl.when(part == 0)
    def _():
        branch = nn(o_ref[...], load(refs[:count], core, held1)) + vec_ref[4:5]
        mid = (hidden_ref[...].astype(F32) + factor_ref[:, 0:1] * branch).astype(BF)
        mid_ref[...] = mid
        scaled, _ = centered(mid.astype(F32))
        normed_ref[...] = (scaled * vec_ref[5:6] + vec_ref[6:7]).astype(BF)
        total[...] = jnp.zeros_like(total)

    w1 = load(refs[count : 2 * count], core, held1)
    w2 = load(refs[2 * count : 3 * count], core, held2)
    u = nn(normed_ref[...], w1) + vec_ref[pl.ds(8 + part, 1), :]
    cdf = 0.5 * (1.0 + lax.erf(u * root_half))
    gb = (u * cdf).astype(BF)
    gb_ref[...] = gb
    slope_ref[...] = cdf + u * jnp.exp(-0.5 * u * u) * normal_peak
    total[...] += nt(gb, w2)

    @pl.when(part == 3)
    def _():
        branch = total[...] + vec_ref[7:8]
        out_ref[...] = (mid_ref[...].astype(F32) + factor_ref[:, 1:2] * branch).astype(BF)


def feed(at, hidden, o, vec, factor, wa, w1, w2):
    rows, width = hidden.shape
    whole = pl.BlockSpec((rows, width), lambda p: (0, 0))
    part = pl.BlockSpec((None, rows, width), lambda p: (p, 0, 0))
    flat = jax.ShapeDtypeStruct((rows, width), BF)
    return pl.pallas_call(
        functools.partial(feed_kernel, len(wa[1])),
        grid=(4,),
        in_specs=[
            SMEM,
            whole,
            whole,
            pl.BlockSpec(vec.shape, lambda p: (0, 0)),
            pl.BlockSpec(factor.shape, lambda p: (0, 0)),
        ]
        + view(wa, lambda p: 3)
        + view(w1, lambda p: p)
        + view(w2, lambda p: p),
        out_specs=[whole, whole, part, part, whole],
        out_shape=[
            flat,
            flat,
            jax.ShapeDtypeStruct((4, rows, width), BF),
            jax.ShapeDtypeStruct((4, rows, width), F32),
            flat,
        ],
        scratch_shapes=[pltpu.VMEM((rows, width), F32)] + [pltpu.VMEM((width, width), BF)] * 2,
        compiler_params=pltpu.CompilerParams(vmem_limit_bytes=VMEM_LIMIT),
        cost_estimate=cost(17),
        name="feed",
    )(at, hidden, o, vec, factor, *wa[1], *w1[1], *w2[1])


def feed_back_kernel(count, at_ref, up_ref, mid_ref, vec_ref, factor_ref, slope_ref, *refs):
    eb_ref, du_ref, out_ref, eba_ref, do_ref, sums_ref, total, held1, held2 = refs[3 * count :]
    part = pl.program_id(0)
    core = at_ref[2]

    @pl.when(part == 0)
    def _():
        eb = (factor_ref[:, 1:2] * up_ref[...].astype(F32)).astype(BF)
        eb_ref[...] = eb
        sums_ref[2:3] = column_sum(eb.astype(F32))
        total[...] = jnp.zeros_like(total)

    w1 = load(refs[count : 2 * count], core, held1)
    w2 = load(refs[2 * count : 3 * count], core, held2)
    du = (nn(eb_ref[...], w2) * slope_ref[...]).astype(BF)
    du_ref[...] = du
    sums_ref[pl.ds(3 + part, 1), :] = column_sum(du.astype(F32))
    total[...] += nt(du, w1)

    @pl.when(part == 3)
    def _():
        scaled, inverse = centered(mid_ref[...].astype(F32))
        dn = total[...]
        sums_ref[0:1] = column_sum(dn * scaled)
        sums_ref[1:2] = column_sum(dn)
        up = up_ref[...].astype(F32) + normalize_back(dn, scaled, inverse, vec_ref[5:6])
        up = up.astype(BF)
        out_ref[...] = up
        eba = (factor_ref[:, 0:1] * up.astype(F32)).astype(BF)
        eba_ref[...] = eba
        sums_ref[7:8] = column_sum(eba.astype(F32))
        do_ref[...] = nt(eba, load(refs[:count], core, held1)).astype(BF)


def feed_back(at, up, mid, vec, factor, slope, wa, w1, w2):
    rows, width = up.shape
    whole = pl.BlockSpec((rows, width), lambda p: (0, 0))
    part = pl.BlockSpec((None, rows, width), lambda p: (p, 0, 0))
    flat = jax.ShapeDtypeStruct((rows, width), BF)
    return pl.pallas_call(
        functools.partial(feed_back_kernel, len(wa[1])),
        grid=(4,),
        in_specs=[
            SMEM,
            whole,
            whole,
            pl.BlockSpec(vec.shape, lambda p: (0, 0)),
            pl.BlockSpec(factor.shape, lambda p: (0, 0)),
            part,
        ]
        + view(wa, lambda p: 3)
        + view(w1, lambda p: p)
        + view(w2, lambda p: p),
        out_specs=[whole, part, whole, whole, whole, pl.BlockSpec((8, width), lambda p: (0, 0))],
        out_shape=[
            flat,
            jax.ShapeDtypeStruct((4, rows, width), BF),
            flat,
            flat,
            flat,
            jax.ShapeDtypeStruct((8, width), F32),
        ],
        scratch_shapes=[pltpu.VMEM((rows, width), F32)] + [pltpu.VMEM((width, width), BF)] * 2,
        compiler_params=pltpu.CompilerParams(vmem_limit_bytes=VMEM_LIMIT),
        cost_estimate=cost(17),
        name="feed_back",
    )(at, up, mid, vec, factor, slope, *wa[1], *w1[1], *w2[1])


def project_back_kernel(count, at_ref, up_ref, hidden_ref, vec_ref, joined_ref, *refs):
    out_ref, sums_ref, total, held = refs[count:]
    part = pl.program_id(0)
    grad = nt(joined_ref[...], load(refs[:count], at_ref[2], held))
    sums_ref[pl.ds(2 + part, 1), :] = column_sum(joined_ref[...].astype(F32))

    @pl.when(part == 0)
    def _():
        total[...] = grad

    @pl.when(part > 0)
    def _():
        total[...] += grad

    @pl.when(part == 2)
    def _():
        scaled, inverse = centered(hidden_ref[...].astype(F32))
        dn = total[...]
        sums_ref[0:1] = column_sum(dn * scaled)
        sums_ref[1:2] = column_sum(dn)
        up = up_ref[...].astype(F32) + normalize_back(dn, scaled, inverse, vec_ref[0:1])
        out_ref[...] = up.astype(BF)


def project_back(at, up, hidden, vec, joined, wa):
    rows, width = up.shape
    whole = pl.BlockSpec((rows, width), lambda p: (0, 0))
    return pl.pallas_call(
        functools.partial(project_back_kernel, len(wa[1])),
        grid=(3,),
        in_specs=[
            SMEM,
            whole,
            whole,
            pl.BlockSpec(vec.shape, lambda p: (0, 0)),
            pl.BlockSpec((None, rows, width), lambda p: (p, 0, 0)),
        ]
        + view(wa, lambda p: p),
        out_specs=[whole, pl.BlockSpec((8, width), lambda p: (0, 0))],
        out_shape=[
            jax.ShapeDtypeStruct((rows, width), BF),
            jax.ShapeDtypeStruct((8, width), F32),
        ],
        scratch_shapes=[pltpu.VMEM((rows, width), F32), pltpu.VMEM((width, width), BF)],
        compiler_params=pltpu.CompilerParams(vmem_limit_bytes=VMEM_LIMIT),
        cost_estimate=cost(8),
        name="project_back",
    )(at, up, hidden, vec, joined, *wa[1])


def attention(joined, code_q, code_k):
    _, rows, width = joined.shape
    parts = [pl.BlockSpec((None, rows, 2 * HD), functools.partial(lambda n, i: (n, 0, i), n)) for n in range(3)]
    pair = pl.BlockSpec((rows, 2 * HD), lambda i: (0, i))
    whole = pl.BlockSpec((rows, 2 * HD), lambda i: (0, 0))
    return pl.pallas_call(
        attention_kernel,
        grid=(width // (2 * HD),),
        in_specs=parts + [whole, whole],
        out_specs=[pair, pl.BlockSpec((None, rows, 2), lambda i: (i, 0, 0))],
        out_shape=[
            jax.ShapeDtypeStruct((rows, width), BF),
            jax.ShapeDtypeStruct((width // (2 * HD), rows, 2), F32),
        ],
        compiler_params=pltpu.CompilerParams(vmem_limit_bytes=VMEM_LIMIT),
        cost_estimate=cost(15),
        name="attention",
    )(joined, joined, joined, code_q, code_k)


def attention_back(joined, do, lse, code_q, code_k):
    _, rows, width = joined.shape
    parts = [pl.BlockSpec((None, rows, 2 * HD), functools.partial(lambda n, i: (n, 0, i), n)) for n in range(3)]
    pair = pl.BlockSpec((rows, 2 * HD), lambda i: (0, i))
    whole = pl.BlockSpec((rows, 2 * HD), lambda i: (0, 0))
    return pl.pallas_call(
        attention_back_kernel,
        grid=(width // (2 * HD),),
        in_specs=parts + [pair, pl.BlockSpec((None, rows, 2), lambda i: (i, 0, 0)), whole, whole],
        out_specs=pl.BlockSpec((3, rows, 2 * HD), lambda i: (0, 0, i)),
        out_shape=jax.ShapeDtypeStruct((3, rows, width), BF),
        compiler_params=pltpu.CompilerParams(vmem_limit_bytes=VMEM_LIMIT),
        cost_estimate=cost(19),
        name="attention_back",
    )(joined, joined, joined, do, lse, code_q, code_k)


def which(xy, turn, at):
    s = at[0]
    quarter = jnp.where(xy == 0, s & 2, 1 + 2 * (s & 1))
    side = jnp.where(xy == 0, s & 1, s >> 1)
    return quarter, side ^ turn


def spread(product, own, keep_ref, send_ref, held):
    held[...] = product
    share = held.shape[0] // 8
    for chip in range(4):
        mine = pl.multiple_of((2 * chip + own) * share, share)
        other = pl.multiple_of((2 * chip + 1 - own) * share, share)
        keep_ref[chip, :share] = held[pl.ds(mine, share), :].astype(BF)
        send_ref[chip, :share] = held[pl.ds(other, share), :].astype(BF)


def feed_weight_kernel(at_ref, a_ref, eb_ref, du_ref, gb_ref, keep_ref, send_ref, turned, held):
    mat, xy, turn = pl.program_id(0), pl.program_id(1), pl.program_id(2)
    fresh = jnp.logical_and(xy == 0, turn == 0)

    @pl.when(jnp.logical_and(fresh, mat == 0))
    def _():
        turned[...] = a_ref[...].T

    @pl.when(jnp.logical_and(fresh, mat == 1))
    def _():
        turned[...] = eb_ref[...].T

    right = jnp.where(mat == 0, du_ref[...], gb_ref[...])
    spread(nn(turned[...], right), at_ref[2], keep_ref, send_ref, held)


def attention_weight_kernel(rows_too, at_ref, a_ref, o_ref, joined_ref, eb_ref, *rest):
    keep_ref, send_ref, turned, held = rest[-4:]
    share = held.shape[0] // 8
    if rows_too:
        for chip in range(4):
            keep_ref[chip, share:] = rest[0][2 * chip + at_ref[2]]
            send_ref[chip, share:] = rest[0][2 * chip + 1 - at_ref[2]]
    xy, turn = pl.program_id(0), pl.program_id(1)
    last = which(xy, turn, at_ref)[0] == 3

    @pl.when(jnp.logical_and(turn == 0, last))
    def _():
        turned[...] = o_ref[...].T

    @pl.when(jnp.logical_and(turn == 0, jnp.logical_not(last)))
    def _():
        turned[...] = a_ref[...].T

    right = jnp.where(last, eb_ref[...], joined_ref[...])
    spread(nn(turned[...], right), at_ref[2], keep_ref, send_ref, held)


def weight_outs(count, rows, width, more=0):
    share, half = width // 8 + more, width // 2
    shape = jax.ShapeDtypeStruct((2, 2, 4, count, share, half), BF)
    block = (None, None, 4, None, share, half)
    scratch = [pltpu.VMEM((width, rows), BF), pltpu.VMEM((width, half), F32)]
    return [shape, shape], block, scratch


def feed_weights(at, a, eb, du, gb, count, slot):
    rows, width = a.shape
    shapes, block, scratch = weight_outs(count, rows, width)
    whole = pl.BlockSpec((rows, width), lambda m, i, j, at: (0, 0))

    def du_at(m, i, j, at):
        quarter, half = which(jnp.where(m == 0, i, 1), jnp.where(m == 0, j, 1), at)
        return quarter, 0, half

    def gb_at(m, i, j, at):
        quarter, half = which(jnp.where(m == 1, i, 0), jnp.where(m == 1, j, 0), at)
        return quarter, 0, half

    out = pl.BlockSpec(block, lambda m, i, j, at: (i, j, 0, slot + m, 0, 0))
    return pl.pallas_call(
        feed_weight_kernel,
        grid_spec=pltpu.PrefetchScalarGridSpec(
            num_scalar_prefetch=1,
            grid=(2, 2, 2),
            in_specs=[
                whole,
                whole,
                pl.BlockSpec((None, rows, width // 2), du_at),
                pl.BlockSpec((None, rows, width // 2), gb_at),
            ],
            out_specs=[out, out],
            scratch_shapes=scratch,
        ),
        out_shape=shapes,
        compiler_params=pltpu.CompilerParams(vmem_limit_bytes=VMEM_LIMIT),
        cost_estimate=cost(11),
        name="feed_weights",
    )(at, a, eb, du, gb)


def attention_weights_grad(at, a, o, joined, eb, into, vector_rows=None):
    rows, width = a.shape
    count = 1 if into is None else into[0].shape[3]
    more = 0 if vector_rows is None else vector_rows.shape[1]
    shapes, block, scratch = weight_outs(count, rows, width, more)
    whole = pl.BlockSpec((rows, width), lambda i, j, at: (0, 0))

    def joined_at(i, j, at):
        quarter, half = which(i, j, at)
        return jnp.minimum(quarter, 2), 0, half

    out = pl.BlockSpec(block, lambda i, j, at: (i, j, 0, 0, 0, 0))
    if vector_rows is None:
        extra, aliases = tuple(into), {5: 0, 6: 1}
        extra_specs = [pl.BlockSpec(memory_space=pl.ANY)] * 2
    else:
        extra, aliases = (vector_rows,), {}
        extra_specs = [pl.BlockSpec(vector_rows.shape, lambda i, j, at: (0, 0, 0))]
    return pl.pallas_call(
        functools.partial(attention_weight_kernel, vector_rows is not None),
        grid_spec=pltpu.PrefetchScalarGridSpec(
            num_scalar_prefetch=1,
            grid=(2, 2),
            in_specs=[
                whole,
                whole,
                pl.BlockSpec((None, rows, width // 2), joined_at),
                pl.BlockSpec((rows, width // 2), lambda i, j, at: (0, which(i, j, at)[1])),
            ]
            + extra_specs,
            out_specs=[out, out],
            scratch_shapes=scratch,
        ),
        out_shape=shapes,
        input_output_aliases=aliases,
        compiler_params=pltpu.CompilerParams(vmem_limit_bytes=VMEM_LIMIT),
        cost_estimate=cost(8),
        name="attention_weights",
    )(at, a, o, joined, eb, *extra)


def adam_step(weight, first, second, gradient, rate, decay_on):
    mean_next = beta_one * first + (1.0 - beta_one) * gradient
    square_next = beta_two * second + (1.0 - beta_two) * gradient * gradient
    step_next = rate * (
        mean_next / bias_one / (jnp.sqrt(square_next / bias_two) + adam_eps) + decay_on * weight
    )
    return (mean_next, square_next, step_next)


def adam_update(weight, first_moment, second_moment, gradient, layer_rates, decay_on):
    rate = layer_rates.reshape((-1,) + (1,) * (weight.ndim - 1))
    return adam_step(weight, first_moment, second_moment, gradient, rate, decay_on)


def adam_kernel(layer, at_ref, rate_ref, grad_ref, weight_ref, first_ref, second_ref, *rest):
    outs = rest[-4:]
    s = at_ref[0]
    half = grad_ref.shape[-1]
    order = ((0, 0), (1, 0), (0, 1), (2, 1), (2, 0), (3, 0), (1, 1), (3, 1))
    for n, (device, xy) in enumerate(order):
        at = pl.ds(n * half, half)
        gradient = grad_ref[s ^ device, xy].astype(F32)
        new = adam_step(
            weight_ref[:, at], first_ref[:, at], second_ref[:, at], gradient, rate_ref[layer], decay_rate
        )
        for ref, value in zip(outs, (gradient,) + new):
            ref[:, at] = value


def adam(at, rates, gradient, weight, first, second, layer, slot, into):
    count = 1 if weight.ndim == 3 else weight.shape[1]
    share, columns = weight.shape[-2:]
    half = gradient.shape[-1]
    if weight.ndim == 3:
        spec = pl.BlockSpec((None, share, columns), lambda m, at, rates: (layer, 0, 0))
    else:
        spec = pl.BlockSpec((None, None, share, columns), lambda m, at, rates: (layer, m, 0, 0))
    extra = () if into is None else tuple(into)
    return pl.pallas_call(
        functools.partial(adam_kernel, layer),
        grid_spec=pltpu.PrefetchScalarGridSpec(
            num_scalar_prefetch=2,
            grid=(count,),
            in_specs=[
                pl.BlockSpec((4, 2, None, share, half), lambda m, at, rates: (0, 0, slot + m, 0, 0)),
                spec,
                spec,
                spec,
            ]
            + [pl.BlockSpec(memory_space=pl.ANY)] * len(extra),
            out_specs=[spec] * 4,
        ),
        out_shape=[jax.ShapeDtypeStruct(weight.shape, F32)] * 4,
        input_output_aliases={6 + n: n for n in range(len(extra))},
        compiler_params=pltpu.CompilerParams(vmem_limit_bytes=VMEM_LIMIT),
        cost_estimate=cost(6),
        name="adam",
    )(at, rates, gradient, weight, first, second, *extra)


def assemble_kernel(at_ref, own, far, x_far, y_far, d_left, d_right, out_ref):
    z, step = at_ref[1], pl.program_id(1)
    half = d_left.shape[-1]
    out_ref[z] = own[...]
    for n, source in enumerate((far, x_far, y_far)):

        @pl.when(step == n)
        def _(source=source):
            for k in range(3):
                out_ref[lax.rem(z + 3 - k, 4)] = source[k]

    @pl.when(step == 3)
    def _():
        for k in range(3):
            out_ref[lax.rem(z + 3 - k, 4), :, :half] = d_left[k]
            out_ref[lax.rem(z + 3 - k, 4), :, half:] = d_right[k]


def assemble(at, sources):
    count, _, share, width = sources[0].shape
    piece = pl.BlockSpec((3, None, share, width), lambda m, j, at: (0, m, 0, 0))
    cut = pl.BlockSpec((3, None, share, width // 2), lambda m, j, at: (0, m, 0, 0))
    own = pl.BlockSpec((None, None, share, width), lambda m, j, at: (m, at[0] ^ j, 0, 0))
    return pl.pallas_call(
        assemble_kernel,
        grid_spec=pltpu.PrefetchScalarGridSpec(
            num_scalar_prefetch=1,
            grid=(count, 4),
            in_specs=[own, piece, piece, piece, cut, cut],
            out_specs=pl.BlockSpec(
                (None, None, 4, share, width), lambda m, j, at: (m, at[0] ^ j, 0, 0, 0)
            ),
        ),
        out_shape=jax.ShapeDtypeStruct((count, 4, 4, share, width), BF),
        compiler_params=pltpu.CompilerParams(vmem_limit_bytes=24 * 2**20),
        cost_estimate=cost(3 * count),
        name="assemble",
    )(at, *sources)


def pack_kernel(at_ref, wa_ref, wf_ref, flat_ref, first_ref, feed_ref, second_ref):
    share = wa_ref.shape[1]
    first_ref[:share] = wa_ref[0].astype(BF)
    first_ref[share:] = flat_ref[...]
    for n in range(2):
        feed_ref[n * share : (n + 1) * share] = wf_ref[0, n].astype(BF)
        second_ref[1 + n] = wf_ref[1, n].astype(BF)
    second_ref[0] = wa_ref[1].astype(BF)


def pack(at, wa, wf, flat):
    layers, share, columns = wa.shape
    width = columns // 4
    shapes = [(share + flat.shape[0], width), (2 * share, width), (3, share, width)]
    return pl.pallas_call(
        pack_kernel,
        grid_spec=pltpu.PrefetchScalarGridSpec(
            num_scalar_prefetch=1,
            grid=(1,),
            in_specs=[
                pl.BlockSpec((layers, share, width), lambda i, at: (0, 0, at[0])),
                pl.BlockSpec((layers, 2, share, width), lambda i, at: (0, 0, 0, at[0])),
                pl.BlockSpec(flat.shape, lambda i, at: (0, 0)),
            ],
            out_specs=[
                pl.BlockSpec(shapes[0], lambda i, at: (0, 0)),
                pl.BlockSpec(shapes[1], lambda i, at: (0, 0)),
                pl.BlockSpec(shapes[2], lambda i, at: (0, 0, 0)),
            ],
        ),
        out_shape=[jax.ShapeDtypeStruct(shape, BF) for shape in shapes],
        cost_estimate=cost(2),
        name="pack",
    )(at, wa, wf, flat)


def cast_kernel(weight_ref, out_ref):
    out_ref[...] = weight_ref[...].astype(BF)


def cast_blocks(weight, layer):
    share, columns = weight.shape[-2:]
    count = 1 if weight.ndim == 3 else weight.shape[1]
    if weight.ndim == 3:
        spec = pl.BlockSpec((None, share, columns // 4), lambda m, q: (layer, 0, q))
    else:
        spec = pl.BlockSpec((None, None, share, columns // 4), lambda m, q: (layer, m, 0, q))
    return pl.pallas_call(
        cast_kernel,
        grid=(count, 4),
        in_specs=[spec],
        out_specs=pl.BlockSpec((None, None, share, columns // 4), lambda m, q: (m, q, 0, 0)),
        out_shape=jax.ShapeDtypeStruct((count, 4, share, columns // 4), BF),
        cost_estimate=cost(2 * count),
        name="cast",
    )(weight)


def after(value, *others):
    return lax.optimization_barrier((value,) + others)[0]


def shards(
    patches,
    positions,
    image_sizes,
    keep_masks,
    output_grad,
    vector_params,
    attention_weights,
    feedforward_weights,
    vector_first,
    attention_first,
    feedforward_first,
    vector_second,
    attention_second,
    feedforward_second,
    layer_rates,
):
    both = ("section", "dp")
    micro_count, row_count, width = patches.shape
    layers = vector_params.shape[0]
    share = attention_weights.shape[1]
    half = width // 2
    s = lax.axis_index("section")
    d = lax.axis_index("dp")
    s_low, s_high = s % 2, s // 2
    unit = s_low ^ s_high
    across = [(i, i ^ 1) for i in range(4)]
    along = [(i, i ^ 2) for i in range(4)]
    athwart = [(i, i ^ 3) for i in range(4)]
    shards_dp = lax.axis_size("dp")
    tuned = shards_dp == 8
    around = [[(i, (i + 2 * k) % 8) for i in range(8)] for k in (1, 2, 3)]
    swap = [(i, i ^ 1) for i in range(8)]
    at = jnp.stack([s, d // 2, d % 2]).astype(jnp.int32)
    z = d // 2

    def quarter(array):
        return lax.dynamic_slice_in_dim(array, s * width, width, axis=array.ndim - 1)

    if tuned:
        flat = vector_params.astype(BF).reshape(-1, share * 8)
        flat = jnp.pad(flat, ((0, 16 - flat.shape[0]), (0, 0)))
        first_sent, feed_sent, second_sent = pack(at, attention_weights, feedforward_weights, flat)

        def around_z(sent):
            return [lax.ppermute(sent, "dp", route) for route in around]

        def around_xy(far):
            x_far = lax.ppermute(far, "section", across)
            y_far = lax.ppermute(far, "section", along)
            return x_far, y_far

        def around_d(x_far, y_far):
            d_left = lax.ppermute(y_far[..., :half], "section", across)
            d_right = lax.ppermute(x_far[..., half:], "section", along)
            return d_left, d_right

        far = around_z(first_sent)
        vector_pieces = jnp.stack([flat] + [f[share:] for f in far])
        far = jnp.stack([f[:share] for f in far]).reshape(3, 1, share, width)
        feed_sent, second_sent = lax.optimization_barrier((feed_sent, second_sent, far))[:2]
        second = lax.all_gather(second_sent, both, axis=0, tiled=False)
        second = second.reshape(4, 8, 3, share, width)
        blocks = cast_blocks(attention_weights, 0)
        x_far, y_far = around_xy(far)
        feed_far = jnp.stack(around_z(feed_sent)).reshape(3, 2, share, width)
        feed_blocks = cast_blocks(feedforward_weights, 0)
        x_far, y_far, feed_far = lax.optimization_barrier((x_far, y_far, feed_far))
        d_left, d_right = around_d(x_far, y_far)
        first_half = assemble(at, (blocks, far, x_far, y_far, d_left, d_right))
        first_halves = (first_half, lax.ppermute(first_half, "dp", swap))
        both_cores = jnp.stack([vector_pieces, lax.ppermute(vector_pieces, "dp", swap)])
        chips = (d // 2 - jnp.arange(4)) % 4
        order = jnp.where(jnp.arange(4)[:, None] == chips[None, :], 1.0, 0.0).astype(BF)
        both_cores = jnp.einsum("zk,kcrw->zcrw", order, both_cores.transpose(1, 0, 2, 3))
        ordered = jnp.where(d % 2 == 0, both_cores, both_cores[:, ::-1])
        ordered = ordered.reshape(8, -1)[:, : layers * 12 * share].reshape(8, layers, 12, share)
        vectors = ordered.transpose(1, 2, 0, 3).reshape(layers, 12, width).astype(F32)
        first_weights = ("halves", first_halves, 0)
    else:

        def gathered(piece):
            piece = lax.all_gather(quarter(piece).astype(BF), both, axis=0, tiled=True)
            return ("full", (piece.reshape(4, 1, 1, width, width),), 0)

        vectors = lax.all_gather(vector_params.astype(BF), "dp", axis=2, tiled=True).astype(F32)
        weights = [
            (
                gathered(attention_weights[l]),
                gathered(feedforward_weights[l, 0]),
                gathered(feedforward_weights[l, 1]),
            )
            for l in range(layers)
        ]

    image_ids = lax.dynamic_index_in_dim(image_sizes[:, 0], unit, 0, keepdims=False)
    keep = lax.dynamic_index_in_dim(keep_masks[:, 0], unit, 0, keepdims=False)
    segment, member, inside, table_row = image_layout(image_ids, row_count)
    kept = jnp.sum(jnp.where(member[:, :, None], keep[None], 0), axis=1).astype(F32)
    factors = jnp.where(inside[:, None], kept / (1.0 - drop_rate), 1.0)
    patch_rows = lax.dynamic_index_in_dim(patches, unit, 0, keepdims=False).astype(F32)
    position_rows = jnp.take(positions, table_row, axis=0).astype(F32)
    hidden = patch_rows + jnp.where(inside[:, None], position_rows, 0.0)
    lane = jnp.arange(2 * HD, dtype=jnp.int32) % HD
    coded = lane[None, :] == segment[:, None]
    code_q = coded.astype(BF)
    code_k = jnp.where(coded | (lane[None, :] > image_sizes.shape[2]), 0.0, masked_score).astype(BF)

    saved = []
    for layer in range(layers):
        vec = vectors[layer]
        factor = factors[:, 2 * layer : 2 * layer + 2]
        if tuned and layer == 0:
            hidden = after(hidden, feed_far)
            a, joined = project(at, hidden, vec, first_weights)
            x_far, y_far = around_xy(feed_far)
            x_far, y_far, joined = lax.optimization_barrier((x_far, y_far, joined))
            o, lse = attention(joined, code_q, code_k)
            d_left, d_right = around_d(x_far, y_far)
            feed_half = assemble(at, (feed_blocks, feed_far, x_far, y_far, d_left, d_right))
            feed_halves = (feed_half, lax.ppermute(feed_half, "dp", swap))
            weights = [
                (first_weights, ("halves", feed_halves, 0), ("halves", feed_halves, 1)),
                tuple(("full", (second,), n) for n in range(3)),
            ]
            wa, w1, w2 = weights[0]
        else:
            wa, w1, w2 = weights[layer]
            a, joined = project(at, hidden, vec, wa)
            o, lse = attention(joined, code_q, code_k)
        mid, a2, gb, slope, following = feed(at, hidden, o, vec, factor, wa, w1, w2)
        saved.append((hidden, a, joined, o, lse, mid, a2, gb, slope))
        hidden = following

    def pick(index, options):
        value = options[0]
        for n in range(1, len(options)):
            value = jnp.where(index == n, options[n], value)
        return value

    def outward(rows):
        blocks = [rows[:, i * (width // 4) : (i + 1) * (width // 4)] for i in range(4)]
        mine = pick(s, blocks)
        theirs = lax.ppermute(pick(s ^ 1, blocks), "section", across)
        return jnp.where(unit == 0, jnp.stack([mine, theirs]), jnp.stack([theirs, mine]))

    block_result = outward(hidden)

    def over_units(here):
        return (
            lax.ppermute(here[0, 1], "section", across),
            lax.ppermute(here[1, 1], "section", along),
        )

    def added(kept_part, got):
        return (kept_part.astype(F32) + got.astype(F32)).astype(BF)

    def units_added(here, x_got, y_got):
        return (here[:, 0].astype(F32) + jnp.stack([x_got, y_got]).astype(F32)).astype(BF)

    def over_chips(summed):
        return [
            lax.ppermute(
                lax.dynamic_index_in_dim(summed, (z + k) % 4, 1, keepdims=False), "dp", route
            )
            for k, route in zip((1, 2, 3), around)
        ]

    def chips_added(summed, got):
        total = lax.dynamic_index_in_dim(summed, z, 1, keepdims=False).astype(F32)
        for part in got:
            total = total + part.astype(F32)
        return total.astype(BF)

    def over_sections(total):
        return [lax.ppermute(total, "section", route) for route in (across, along, athwart)]

    def joint(*values):
        return lax.optimization_barrier(values)

    def reduced_plainly(pairs):
        count = len(pairs)
        summed = []
        for xy, (side, route) in enumerate(((s_low, across), (s_high, along))):
            parts = [pair[xy].astype(BF) for pair in pairs]
            mine = [lax.dynamic_slice_in_dim(part, side * half, half, 1) for part in parts]
            other = [lax.dynamic_slice_in_dim(part, (1 - side) * half, half, 1) for part in parts]
            other = lax.ppermute(jnp.concatenate(other, axis=1), "section", route)
            summed.append((jnp.concatenate(mine, axis=1).astype(F32) + other.astype(F32)).astype(BF))
        stacked = jnp.concatenate(summed, axis=1)
        scattered = lax.psum_scatter(stacked, "dp", scatter_dimension=0, tiled=True)
        everyone = lax.all_gather(scattered, "section", axis=0, tiled=False)
        everyone = everyone.reshape(4, share, 2, count, half)
        order = ((0, 0), (1, 0), (0, 1), (2, 1), (2, 0), (3, 0), (1, 1), (3, 1))
        return [
            jnp.concatenate([everyone[dev, :, xy, mat] for dev, xy in order], axis=1).astype(F32)
            for mat in range(count)
        ]

    up = lax.dynamic_index_in_dim(output_grad, unit, 0, keepdims=False)
    vector_rows = [None] * layers

    def put_rows(layer, attention_sums, feed_sums):
        vector_rows[layer] = jnp.concatenate(
            [attention_sums[0:3], attention_sums[4:5], feed_sums[7:8], feed_sums[0:7]]
        )

    def vectors_updated(vector_grad):
        return (vector_grad,) + adam_update(
            vector_params, vector_first, vector_second, vector_grad, layer_rates, 0.0
        )

    if tuned:
        wa, w1, w2 = weights[1]
        start, a, joined, o, lse, mid, a2, gb, slope = saved[1]
        eb, du, up, eba, do, feed_sums = feed_back(
            at, up, mid, vectors[1], factors[:, 2:4], slope, wa, w1, w2
        )
        parts = feed_weights(at, a2, eb, du, gb, 3, 1)
        do = after(do, *parts)
        dqkv = attention_back(joined, do, lse, code_q, code_k)
        kept1, sent1 = attention_weights_grad(at, a, o, dqkv, eba, parts)
        up = after(up, kept1, sent1)
        got = lax.ppermute(sent1, "dp", swap)
        up, attention_sums = project_back(at, up, start, vectors[1], dqkv, wa)
        put_rows(1, attention_sums, feed_sums)
        got, up = joint(got, up)
        here1 = added(kept1, got)
        wa, w1, w2 = weights[0]
        start, a, joined, o, lse, mid, a2, gb, slope = saved[0]
        up = after(up, here1)
        x_got, y_got = over_units(here1)
        eb, du, up, eba, do, feed_sums = feed_back(
            at, up, mid, vectors[0], factors[:, 0:2], slope, wa, w1, w2
        )
        x_got, y_got, up, do, du = joint(x_got, y_got, up, do, du)
        summed1 = units_added(here1, x_got, y_got)
        du = after(du, summed1)
        z_got = over_chips(summed1)
        kept2, sent2 = feed_weights(at, a2, eb, du, gb, 2, 0)
        do = after(do, kept2, sent2)
        got2 = lax.ppermute(sent2, "dp", swap)
        dqkv = attention_back(joined, do, lse, code_q, code_k)
        *z_got, got2, dqkv = joint(*z_got, got2, dqkv)
        total1 = chips_added(summed1, z_got)
        here2 = added(kept2, got2)
        dqkv = after(dqkv, total1, here2)
        g_got = over_sections(total1)
        x_got, y_got = over_units(here2)
        up, attention_sums = project_back(at, up, start, vectors[0], dqkv, wa)
        put_rows(0, attention_sums, feed_sums)
        rows_all = jnp.concatenate(vector_rows).astype(BF)
        lines = layers * 12 * share // half
        rows_all = rows_all.reshape(lines, half // share, 8, share).transpose(2, 0, 1, 3)
        rows_all = jnp.pad(rows_all.reshape(8, lines, half), ((0, 0), (0, 16 - lines), (0, 0)))
        dqkv = after(dqkv, up)
        kept3, sent3 = attention_weights_grad(at, a, o, dqkv, eba, None, rows_all)
        *g_got, x_got, y_got, kept3, sent3 = joint(*g_got, x_got, y_got, kept3, sent3)
        got3 = lax.ppermute(sent3, "dp", swap)
        summed2 = units_added(here2, x_got, y_got)
        here3 = added(kept3, got3)
        z_got = over_chips(summed2)
        x_got, y_got = over_units(here3)
        input_result = outward(up).astype(F32)
        gradient1 = jnp.stack([total1] + g_got)
        gradient1 = after(gradient1, here3)
        attention_out = adam(
            at, layer_rates, gradient1, attention_weights, attention_first,
            attention_second, 1, 0, None,
        )
        feed_out = adam(
            at, layer_rates, gradient1, feedforward_weights, feedforward_first,
            feedforward_second, 1, 1, None,
        )
        x_got, y_got, *z_got, attention_out0, feed_out0 = joint(
            x_got, y_got, *z_got, attention_out[0], feed_out[0]
        )
        attention_out = [attention_out0] + list(attention_out[1:])
        feed_out = [feed_out0] + list(feed_out[1:])
        summed3 = units_added(here3, x_got, y_got)
        z_got3 = over_chips(summed3)
        total2 = chips_added(summed2, z_got)
        g_got2 = over_sections(total2)
        total3 = chips_added(summed3, z_got3)
        g_got3 = over_sections(total3[:, :, :share])
        vector_grad = total3[0, 0, share : share + lines].astype(F32)
        vector_grad = vector_grad.reshape(layers, 12, share)
        vector_out = vectors_updated(vector_grad)
        gradient2 = jnp.stack([total2] + g_got2)
        gradient2 = after(gradient2, total3)
        feed_out = adam(
            at, layer_rates, gradient2, feedforward_weights, feedforward_first,
            feedforward_second, 0, 0, feed_out,
        )
        gradient3 = jnp.stack([total3[:, :, :share]] + g_got3)
        gradient3 = after(gradient3, feed_out[0])
        attention_out = adam(
            at, layer_rates, gradient3, attention_weights, attention_first,
            attention_second, 0, 0, attention_out,
        )
    else:
        plain_attention, plain_feed = [None] * layers, [None] * layers

        def x_of(array):
            return jnp.where(s_high == 0, array[0], array[2])

        def y_of(array):
            return jnp.where(s_low == 0, array[1], array[3])

        for layer in reversed(range(layers)):
            wa, w1, w2 = weights[layer]
            start, a, joined, o, lse, mid, a2, gb, slope = saved[layer]
            factor = factors[:, 2 * layer : 2 * layer + 2]
            eb, du, up, eba, do, feed_sums = feed_back(
                at, up, mid, vectors[layer], factor, slope, wa, w1, w2
            )
            dqkv = attention_back(joined, do, lse, code_q, code_k)
            up, attention_sums = project_back(at, up, start, vectors[layer], dqkv, wa)
            put_rows(layer, attention_sums, feed_sums)
            all_four = jnp.concatenate([dqkv, eba[None]])
            plain_feed[layer] = jnp.stack(
                reduced_plainly(
                    [(tn(a2, x_of(du)), tn(a2, y_of(du))), (tn(eb, x_of(gb)), tn(eb, y_of(gb)))]
                )
            )
            y_left = jnp.where(s_low == 0, a, o)
            plain_attention[layer] = reduced_plainly(
                [(tn(a, x_of(all_four)), tn(y_left, y_of(all_four)))]
            )[0]
        rows_all = jnp.concatenate(vector_rows)
        rows_all = rows_all + lax.ppermute(rows_all, "section", across)
        rows_all = jnp.pad(rows_all, ((0, 128 - rows_all.shape[0]), (0, 0))).T
        vector_grad = lax.psum_scatter(rows_all, "dp", scatter_dimension=0, tiled=True)
        vector_out = vectors_updated(vector_grad[:, : layers * 12].T.reshape(layers, 12, share))
        input_result = outward(up).astype(F32)
        gradient = jnp.stack(plain_attention)
        attention_out = (gradient,) + adam_update(
            attention_weights, attention_first, attention_second, gradient, layer_rates, decay_rate
        )
        gradient = jnp.stack(plain_feed)
        feed_out = (gradient,) + adam_update(
            feedforward_weights,
            feedforward_first,
            feedforward_second,
            gradient,
            layer_rates,
            decay_rate,
        )
    outs = [block_result, input_result]
    for group in zip(vector_out, attention_out, feed_out):
        outs.extend(group)
    return tuple(outs)


def solution(mesh):
    in_specs = (
        P(None, "dp", None),
        P(),
        P(None, "dp", None),
        P(None, "dp", None, None),
        P(None, "dp", None),
        P(None, None, "dp"),
        P(None, "dp", None),
        P(None, None, "dp", None),
        P(None, None, "dp"),
        P(None, "dp", None),
        P(None, None, "dp", None),
        P(None, None, "dp"),
        P(None, "dp", None),
        P(None, None, "dp", None),
        P(),
    )
    out_specs = (
        P(None, "dp", "section"),
        P(None, "dp", "section"),
        P(None, None, "dp"),
        P(None, "dp", None),
        P(None, None, "dp", None),
        P(None, None, "dp"),
        P(None, "dp", None),
        P(None, None, "dp", None),
        P(None, None, "dp"),
        P(None, "dp", None),
        P(None, None, "dp", None),
        P(None, None, "dp"),
        P(None, "dp", None),
        P(None, None, "dp", None),
    )
    return jax.shard_map(shards, mesh=mesh, in_specs=in_specs, out_specs=out_specs, check_vma=False)
```

```python
import functools

import jax
import jax.numpy as jnp
from jax import lax
from jax.experimental import pallas as pl
from jax.experimental.pallas import tpu as pltpu
from jax.sharding import PartitionSpec as P

H = 12
HD = 64
GRID_S = 10
GRID_M = 14
GRID_L = 24

beta_one = 0.9
beta_two = 0.999
bias_one = 1.0 - 0.9**10
bias_two = 1.0 - 0.999**10
adam_eps = 1e-08
decay_rate = 0.05
drop_rate = 0.1
norm_eps = 1e-06
masked_score = -1e30
root_half = 0.7071067811865476
normal_peak = 0.3989422804014327
BF = jnp.bfloat16
F32 = jnp.float32


def image_layout(image_ids, row_count):
    small_len = GRID_S * GRID_S + 2
    middle_len = GRID_M * GRID_M + 2
    large_len = GRID_L * GRID_L + 2
    slots = image_ids.shape[0]
    lengths = jnp.where(
        image_ids == 0,
        small_len,
        jnp.where(image_ids == 1, middle_len, jnp.where(image_ids == 2, large_len, 0)),
    ).astype(jnp.int32)
    slot = jnp.arange(slots, dtype=jnp.int32)
    slot_ends = jnp.sum(jnp.where(slot[None, :] <= slot[:, None], lengths[None, :], 0), axis=1)
    slot_starts = slot_ends - lengths
    row_index = jnp.arange(row_count, dtype=jnp.int32)
    segment = jnp.sum((row_index[:, None] >= slot_ends[None, :]).astype(jnp.int32), axis=1)
    member = segment[:, None] == slot[None, :]
    first_row = jnp.sum(jnp.where(member, slot_starts[None, :], 0), axis=1)
    kind_row = jnp.sum(jnp.where(member, image_ids[None, :], 0), axis=1)
    table_start = jnp.where(
        kind_row == 0, 0, jnp.where(kind_row == 1, small_len, small_len + middle_len)
    ).astype(jnp.int32)
    in_image = segment < slots
    table_row = jnp.where(in_image, table_start + row_index - first_row, 0)
    return (segment, member, in_image, table_row)


def nn(a, b):
    return jnp.dot(a, b, preferred_element_type=F32)


def nt(a, b):
    return lax.dot_general(a, b, (((1,), (1,)), ((), ())), preferred_element_type=F32)


def tn(a, b):
    return lax.dot_general(a, b, (((0,), (0,)), ((), ())), preferred_element_type=F32)


def split3(value):
    high = value.astype(BF)
    rest = value - high.astype(F32)
    middle = rest.astype(BF)
    return high, middle, (rest - middle.astype(F32)).astype(BF)


def attention_kernel(q_ref, k_ref, v_ref, code_q_ref, code_k_ref, o_ref, lse_ref):
    low = lax.broadcasted_iota(jnp.int32, q_ref.shape, 1) < HD
    outs = []
    for half in range(2):
        own = low if half == 0 else jnp.logical_not(low)
        q = jnp.where(own, q_ref[...] * jnp.asarray(HD ** (-0.5), BF), code_q_ref[...])
        k = jnp.where(own, k_ref[...], code_k_ref[...])
        scores = nt(q, k)
        peak = jnp.max(scores, axis=-1, keepdims=True)
        e = jnp.exp(scores - peak)
        total = jnp.sum(e, axis=-1, keepdims=True)
        outs.append(nn(e.astype(BF), v_ref[...]) * (1.0 / total))
        lse_ref[:, half : half + 1] = peak + jnp.log(total)
    o_ref[...] = jnp.where(low, outs[0], outs[1]).astype(BF)


def attention_back_kernel(
    q_ref, k_ref, v_ref, do_ref, lse_ref, code_q_ref, code_k_ref, out_ref
):
    lane = lax.broadcasted_iota(jnp.int32, q_ref.shape, 1)
    low = lane < HD
    scale = HD ** (-0.5)
    dqs, dks, dvs = [], [], []
    for half in range(2):
        own = low if half == 0 else jnp.logical_not(low)
        spare = 32 + (HD if half == 0 else 0)
        q_scaled = q_ref[...] * jnp.asarray(scale, BF)
        q = jnp.where(own, q_scaled, code_q_ref[...])
        k = jnp.where(own, k_ref[...], code_k_ref[...])
        v = jnp.where(own, v_ref[...], jnp.zeros_like(v_ref[...]))
        for at, part in enumerate(split3(-lse_ref[:, half : half + 1])):
            here = lane == spare + at
            q = jnp.where(here, part, q)
            k = jnp.where(here, jnp.ones_like(k), k)
        p = jnp.exp(nt(k, q))
        dp = nt(v, do_ref[...])
        row = jnp.sum(p * dp, axis=0, keepdims=True)
        ds = (p * (dp - row)).astype(BF)
        dvs.append(nn(p.astype(BF), do_ref[...]))
        dks.append(nn(ds, q_scaled))
        dqs.append(tn(ds, k_ref[...]) * scale)
    out_ref[0] = jnp.where(low, dqs[0], dqs[1]).astype(BF)
    out_ref[1] = jnp.where(low, dks[0], dks[1]).astype(BF)
    out_ref[2] = jnp.where(low, dvs[0], dvs[1]).astype(BF)


VMEM_LIMIT = 56 * 2**20


def cost(microseconds):
    return pl.CostEstimate(flops=int(microseconds * 1.1e9), bytes_accessed=2**20, transcendentals=0)


def centered(hidden):
    center = hidden - jnp.mean(hidden, axis=-1, keepdims=True)
    inverse = lax.rsqrt(jnp.mean(center * center, axis=-1, keepdims=True) + norm_eps)
    return center * inverse, inverse


def normalize_back(normed_grad, scaled, inverse, gain):
    scaled_grad = normed_grad * gain
    mid = scaled_grad - jnp.mean(scaled_grad, axis=-1, keepdims=True)
    return inverse * (mid - scaled * jnp.mean(scaled_grad * scaled, axis=-1, keepdims=True))


def column_sum(value):
    return jnp.sum(value, axis=0, keepdims=True)


def view(weight, index):
    specs = []
    for array in weight[1]:
        if weight[0] == "full":
            _, n, _, width = array.shape
            specs.append(
                pl.BlockSpec((None, n, width // n, width), lambda p: (index(p), 0, weight[2], 0))
            )
        else:
            _, _, n, share, width = array.shape
            specs.append(
                pl.BlockSpec((None, None, n, share, width), lambda p: (weight[2], index(p), 0, 0, 0))
            )
    return specs


def cut(refs, weights):
    out = []
    for count in weights:
        out.append(refs[:count])
        refs = refs[count:]
    return (*out, refs)


def load(refs, core, held):
    n, share, width = refs[0].shape
    if len(refs) == 1:
        return refs[0][...].reshape(n * share, width)
    for turn, ref in enumerate(refs):
        side = core if turn == 0 else 1 - core
        for chip in range(n):
            row = pl.multiple_of((2 * chip + side) * share, share)
            held[pl.ds(row, share), :] = ref[chip]
    return held[...]


SMEM = pl.BlockSpec(memory_space=pltpu.SMEM)


def project_kernel(count, at_ref, hidden_ref, vec_ref, *refs):
    normed_ref, joined_ref, held = refs[count:]
    weight = load(refs[:count], at_ref[2], held)
    part = pl.program_id(0)

    @pl.when(part == 0)
    def _():
        scaled, _ = centered(hidden_ref[...].astype(F32))
        normed_ref[...] = (scaled * vec_ref[0:1] + vec_ref[1:2]).astype(BF)

    bias = jnp.where(part == 0, vec_ref[2:3], jnp.where(part == 2, vec_ref[3:4], 0.0))
    joined_ref[...] = (nn(normed_ref[...], weight) + bias).astype(BF)


def project(at, hidden, vec, wa):
    rows, width = hidden.shape
    whole = pl.BlockSpec((rows, width), lambda p: (0, 0))
    return pl.pallas_call(
        functools.partial(project_kernel, len(wa[1])),
        grid=(3,),
        in_specs=[SMEM, whole, pl.BlockSpec(vec.shape, lambda p: (0, 0))] + view(wa, lambda p: p),
        out_specs=[whole, pl.BlockSpec((None, rows, width), lambda p: (p, 0, 0))],
        out_shape=[
            jax.ShapeDtypeStruct((rows, width), BF),
            jax.ShapeDtypeStruct((3, rows, width), BF),
        ],
        compiler_params=pltpu.CompilerParams(vmem_limit_bytes=VMEM_LIMIT),
        scratch_shapes=[pltpu.VMEM((width, width), BF)],
        cost_estimate=cost(7),
        name="project",
    )(at, hidden, vec, *wa[1])


def feed_kernel(counts, at_ref, hidden_ref, o_ref, vec_ref, factor_ref, *refs):
    wo_refs, w1_refs, w2_refs, refs = cut(refs, counts)
    mid_ref, normed_ref, gb_ref, slope_ref, out_ref, total, held1, held2 = refs
    part = pl.program_id(0)
    core = at_ref[2]

    @pl.when(part == 0)
    def _():
        branch = nn(o_ref[...], load(wo_refs, core, held1)) + vec_ref[4:5]
        mid = (hidden_ref[...].astype(F32) + factor_ref[:, 0:1] * branch).astype(BF)
        mid_ref[...] = mid
        scaled, _ = centered(mid.astype(F32))
        normed_ref[...] = (scaled * vec_ref[5:6] + vec_ref[6:7]).astype(BF)
        total[...] = jnp.zeros_like(total)

    w1 = load(w1_refs, core, held1)
    w2 = load(w2_refs, core, held2)
    u = nn(normed_ref[...], w1) + vec_ref[pl.ds(8 + part, 1), :]
    cdf = 0.5 * (1.0 + lax.erf(u * root_half))
    gb = (u * cdf).astype(BF)
    gb_ref[...] = gb
    slope_ref[...] = cdf + u * jnp.exp(-0.5 * u * u) * normal_peak
    total[...] += nt(gb, w2)

    @pl.when(part == 3)
    def _():
        branch = total[...] + vec_ref[7:8]
        out_ref[...] = (mid_ref[...].astype(F32) + factor_ref[:, 1:2] * branch).astype(BF)


def feed(at, hidden, o, vec, factor, wa, w1, w2):
    rows, width = hidden.shape
    whole = pl.BlockSpec((rows, width), lambda p: (0, 0))
    part = pl.BlockSpec((None, rows, width), lambda p: (p, 0, 0))
    flat = jax.ShapeDtypeStruct((rows, width), BF)
    return pl.pallas_call(
        functools.partial(feed_kernel, [len(w[1]) for w in (wa, w1, w2)]),
        grid=(4,),
        in_specs=[
            SMEM,
            whole,
            whole,
            pl.BlockSpec(vec.shape, lambda p: (0, 0)),
            pl.BlockSpec(factor.shape, lambda p: (0, 0)),
        ]
        + view(wa, lambda p: 3)
        + view(w1, lambda p: p)
        + view(w2, lambda p: p),
        out_specs=[whole, whole, part, part, whole],
        out_shape=[
            flat,
            flat,
            jax.ShapeDtypeStruct((4, rows, width), BF),
            jax.ShapeDtypeStruct((4, rows, width), F32),
            flat,
        ],
        scratch_shapes=[pltpu.VMEM((rows, width), F32)] + [pltpu.VMEM((width, width), BF)] * 2,
        compiler_params=pltpu.CompilerParams(vmem_limit_bytes=VMEM_LIMIT),
        cost_estimate=cost(17),
        name="feed",
    )(at, hidden, o, vec, factor, *wa[1], *w1[1], *w2[1])


def feed_back_kernel(counts, at_ref, up_ref, mid_ref, vec_ref, factor_ref, slope_ref, *refs):
    wo_refs, w1_refs, w2_refs, refs = cut(refs, counts)
    eb_ref, du_ref, out_ref, eba_ref, do_ref, sums_ref, total, held1, held2 = refs
    part = pl.program_id(0)
    core = at_ref[2]

    @pl.when(part == 0)
    def _():
        eb = (factor_ref[:, 1:2] * up_ref[...].astype(F32)).astype(BF)
        eb_ref[...] = eb
        sums_ref[2:3] = column_sum(eb.astype(F32))
        total[...] = jnp.zeros_like(total)

    w1 = load(w1_refs, core, held1)
    w2 = load(w2_refs, core, held2)
    du = (nn(eb_ref[...], w2) * slope_ref[...]).astype(BF)
    du_ref[...] = du
    sums_ref[pl.ds(3 + part, 1), :] = column_sum(du.astype(F32))
    total[...] += nt(du, w1)

    @pl.when(part == 3)
    def _():
        scaled, inverse = centered(mid_ref[...].astype(F32))
        dn = total[...]
        sums_ref[0:1] = column_sum(dn * scaled)
        sums_ref[1:2] = column_sum(dn)
        up = up_ref[...].astype(F32) + normalize_back(dn, scaled, inverse, vec_ref[5:6])
        up = up.astype(BF)
        out_ref[...] = up
        eba = (factor_ref[:, 0:1] * up.astype(F32)).astype(BF)
        eba_ref[...] = eba
        sums_ref[7:8] = column_sum(eba.astype(F32))
        do_ref[...] = nt(eba, load(wo_refs, core, held1)).astype(BF)


def feed_back(at, up, mid, vec, factor, slope, wa, w1, w2):
    rows, width = up.shape
    whole = pl.BlockSpec((rows, width), lambda p: (0, 0))
    part = pl.BlockSpec((None, rows, width), lambda p: (p, 0, 0))
    flat = jax.ShapeDtypeStruct((rows, width), BF)
    return pl.pallas_call(
        functools.partial(feed_back_kernel, [len(w[1]) for w in (wa, w1, w2)]),
        grid=(4,),
        in_specs=[
            SMEM,
            whole,
            whole,
            pl.BlockSpec(vec.shape, lambda p: (0, 0)),
            pl.BlockSpec(factor.shape, lambda p: (0, 0)),
            part,
        ]
        + view(wa, lambda p: 3)
        + view(w1, lambda p: p)
        + view(w2, lambda p: p),
        out_specs=[whole, part, whole, whole, whole, pl.BlockSpec((8, width), lambda p: (0, 0))],
        out_shape=[
            flat,
            jax.ShapeDtypeStruct((4, rows, width), BF),
            flat,
            flat,
            flat,
            jax.ShapeDtypeStruct((8, width), F32),
        ],
        scratch_shapes=[pltpu.VMEM((rows, width), F32)] + [pltpu.VMEM((width, width), BF)] * 2,
        compiler_params=pltpu.CompilerParams(vmem_limit_bytes=VMEM_LIMIT),
        cost_estimate=cost(17),
        name="feed_back",
    )(at, up, mid, vec, factor, slope, *wa[1], *w1[1], *w2[1])


def project_back_kernel(count, at_ref, up_ref, hidden_ref, vec_ref, joined_ref, *refs):
    out_ref, sums_ref, total, held = refs[count:]
    part = pl.program_id(0)
    grad = nt(joined_ref[...], load(refs[:count], at_ref[2], held))
    sums_ref[pl.ds(2 + part, 1), :] = column_sum(joined_ref[...].astype(F32))

    @pl.when(part == 0)
    def _():
        total[...] = grad

    @pl.when(part > 0)
    def _():
        total[...] += grad

    @pl.when(part == 2)
    def _():
        scaled, inverse = centered(hidden_ref[...].astype(F32))
        dn = total[...]
        sums_ref[0:1] = column_sum(dn * scaled)
        sums_ref[1:2] = column_sum(dn)
        up = up_ref[...].astype(F32) + normalize_back(dn, scaled, inverse, vec_ref[0:1])
        out_ref[...] = up.astype(BF)


def project_back(at, up, hidden, vec, joined, wa):
    rows, width = up.shape
    whole = pl.BlockSpec((rows, width), lambda p: (0, 0))
    return pl.pallas_call(
        functools.partial(project_back_kernel, len(wa[1])),
        grid=(3,),
        in_specs=[
            SMEM,
            whole,
            whole,
            pl.BlockSpec(vec.shape, lambda p: (0, 0)),
            pl.BlockSpec((None, rows, width), lambda p: (p, 0, 0)),
        ]
        + view(wa, lambda p: p),
        out_specs=[whole, pl.BlockSpec((8, width), lambda p: (0, 0))],
        out_shape=[
            jax.ShapeDtypeStruct((rows, width), BF),
            jax.ShapeDtypeStruct((8, width), F32),
        ],
        scratch_shapes=[pltpu.VMEM((rows, width), F32), pltpu.VMEM((width, width), BF)],
        compiler_params=pltpu.CompilerParams(vmem_limit_bytes=VMEM_LIMIT),
        cost_estimate=cost(8),
        name="project_back",
    )(at, up, hidden, vec, joined, *wa[1])


def attention(joined, code_q, code_k):
    _, rows, width = joined.shape
    parts = [pl.BlockSpec((None, rows, 2 * HD), functools.partial(lambda n, i: (n, 0, i), n)) for n in range(3)]
    pair = pl.BlockSpec((rows, 2 * HD), lambda i: (0, i))
    whole = pl.BlockSpec((rows, 2 * HD), lambda i: (0, 0))
    return pl.pallas_call(
        attention_kernel,
        grid=(width // (2 * HD),),
        in_specs=parts + [whole, whole],
        out_specs=[pair, pl.BlockSpec((None, rows, 2), lambda i: (i, 0, 0))],
        out_shape=[
            jax.ShapeDtypeStruct((rows, width), BF),
            jax.ShapeDtypeStruct((width // (2 * HD), rows, 2), F32),
        ],
        compiler_params=pltpu.CompilerParams(vmem_limit_bytes=VMEM_LIMIT),
        cost_estimate=cost(15),
        name="attention",
    )(joined, joined, joined, code_q, code_k)


def attention_back(joined, do, lse, code_q, code_k):
    _, rows, width = joined.shape
    parts = [pl.BlockSpec((None, rows, 2 * HD), functools.partial(lambda n, i: (n, 0, i), n)) for n in range(3)]
    pair = pl.BlockSpec((rows, 2 * HD), lambda i: (0, i))
    whole = pl.BlockSpec((rows, 2 * HD), lambda i: (0, 0))
    return pl.pallas_call(
        attention_back_kernel,
        grid=(width // (2 * HD),),
        in_specs=parts + [pair, pl.BlockSpec((None, rows, 2), lambda i: (i, 0, 0)), whole, whole],
        out_specs=pl.BlockSpec((3, rows, 2 * HD), lambda i: (0, 0, i)),
        out_shape=jax.ShapeDtypeStruct((3, rows, width), BF),
        compiler_params=pltpu.CompilerParams(vmem_limit_bytes=VMEM_LIMIT),
        cost_estimate=cost(19),
        name="attention_back",
    )(joined, joined, joined, do, lse, code_q, code_k)


def which(xy, turn, at):
    s = at[0]
    quarter = jnp.where(xy == 0, s & 2, 1 + 2 * (s & 1))
    side = jnp.where(xy == 0, s & 1, s >> 1)
    return quarter, side ^ turn


def spread(product, own, keep_ref, send_ref, held):
    held[...] = product
    share = held.shape[0] // 8
    for chip in range(4):
        mine = pl.multiple_of((2 * chip + own) * share, share)
        other = pl.multiple_of((2 * chip + 1 - own) * share, share)
        keep_ref[chip, :share] = held[pl.ds(mine, share), :].astype(BF)
        send_ref[chip, :share] = held[pl.ds(other, share), :].astype(BF)


def spread_all(product, xy, turn, mine_ref, x_ref, y_ref):
    share = product.shape[0] // 8
    rows = [product[n * share : (n + 1) * share].astype(BF) for n in range(8)]
    for ref, here in (
        (mine_ref, turn == 0),
        (x_ref, jnp.logical_and(turn == 1, xy == 0)),
        (y_ref, jnp.logical_and(turn == 1, xy == 1)),
    ):

        @pl.when(here)
        def _(ref=ref):
            for n in range(8):
                ref[n] = rows[n]


def attention_weight_kernel(rows_too, at_ref, a_ref, o_ref, joined_ref, eb_ref, *rest):
    turned, held = rest[-2:]
    share = held.shape[0] // 8
    if rows_too:
        keep_ref, send_ref = rest[-4:-2]
        for chip in range(4):
            keep_ref[chip, share:] = rest[0][2 * chip + at_ref[2]]
            send_ref[chip, share:] = rest[0][2 * chip + 1 - at_ref[2]]
    xy, turn = pl.program_id(0), pl.program_id(1)
    last = which(xy, turn, at_ref)[0] == 3

    @pl.when(jnp.logical_and(turn == 0, last))
    def _():
        turned[...] = o_ref[...].T

    @pl.when(jnp.logical_and(turn == 0, jnp.logical_not(last)))
    def _():
        turned[...] = a_ref[...].T

    right = jnp.where(last, eb_ref[...], joined_ref[...])
    product = nn(turned[...], right)
    if rows_too:
        spread(product, at_ref[2], keep_ref, send_ref, held)
    else:
        spread_all(product, xy, turn, *rest[-5:-2])


def weight_outs(count, rows, width, more=0):
    share, half = width // 8 + more, width // 2
    shape = jax.ShapeDtypeStruct((2, 2, 4, count, share, half), BF)
    block = (None, None, 4, None, share, half)
    scratch = [pltpu.VMEM((width, rows), BF), pltpu.VMEM((width, half), F32)]
    return [shape, shape], block, scratch


def load_into(refs, core, target):
    if len(refs) == 1:
        n, share, width = refs[0].shape
        target[...] = refs[0][...].reshape(n * share, width)
        return target[...]
    return load(refs, core, target)


def wide_half(ref, quarter, half, columns):
    return ref[quarter, :, pl.ds(pl.multiple_of(half * columns, 128), columns)]


def feed_both_kernel(counts, at_ref, hidden_ref, o_ref, up_ref, vec_ref, factor_ref, *refs):
    wo_refs, w1_refs, w2_refs, refs = cut(refs, counts)
    out_ref, back_ref, eba_ref, do_ref, sums_ref, mine_ref, x_ref, y_ref = refs[:8]
    total, w1, w2, held, normed, mid_held, eb, gb, slope, du, turned = refs[8:]
    step = pl.program_id(0)
    core = at_ref[2]

    @pl.when(step == 0)
    def _():
        branch = nn(o_ref[...], load(wo_refs, core, held)) + vec_ref[4:5]
        mid = (hidden_ref[...].astype(F32) + factor_ref[:, 0:1] * branch).astype(BF)
        mid_held[...] = mid
        scaled, _ = centered(mid.astype(F32))
        normed[...] = (scaled * vec_ref[5:6] + vec_ref[6:7]).astype(BF)
        total[...] = jnp.zeros_like(total)

    @pl.when(step < 4)
    def _():
        u = nn(normed[...], load_into(w1_refs, core, w1.at[step])) + vec_ref[pl.ds(8 + step, 1), :]
        cdf = 0.5 * (1.0 + lax.erf(u * root_half))
        active = (u * cdf).astype(BF)
        gb[step] = active
        slope[step] = cdf + u * jnp.exp(-0.5 * u * u) * normal_peak
        total[...] += nt(active, load_into(w2_refs, core, w2.at[step]))

    @pl.when(step == 3)
    def _():
        branch = total[...] + vec_ref[7:8]
        out_ref[...] = (mid_held[...].astype(F32) + factor_ref[:, 1:2] * branch).astype(BF)
        own = (factor_ref[:, 1:2] * up_ref[...].astype(F32)).astype(BF)
        eb[...] = own
        sums_ref[2:3] = column_sum(own.astype(F32))
        total[...] = jnp.zeros_like(total)
        turned[0] = normed[...].T
        turned[1] = own.T

    @pl.when(jnp.logical_and(step >= 4, step < 8))
    def _():
        part = step - 4
        own = (nn(eb[...], w2[part]) * slope[part]).astype(BF)
        du[part] = own
        sums_ref[pl.ds(3 + part, 1), :] = column_sum(own.astype(F32))
        total[...] += nt(own, w1[part])

    @pl.when(step == 7)
    def _():
        scaled, inverse = centered(mid_held[...].astype(F32))
        dn = total[...]
        sums_ref[0:1] = column_sum(dn * scaled)
        sums_ref[1:2] = column_sum(dn)
        up = up_ref[...].astype(F32) + normalize_back(dn, scaled, inverse, vec_ref[5:6])
        up = up.astype(BF)
        back_ref[...] = up
        eba = (factor_ref[:, 0:1] * up.astype(F32)).astype(BF)
        eba_ref[...] = eba
        sums_ref[7:8] = column_sum(eba.astype(F32))
        do_ref[...] = nt(eba, load(wo_refs, core, held)).astype(BF)

    share, half = mine_ref.shape[1:]
    for mat, source in ((0, du), (1, gb)):

        @pl.when(jnp.logical_and(step >= 8 + 2 * mat, step < 10 + 2 * mat))
        def _(mat=mat, source=source):
            xy = (step - 8) % 2
            for turn in range(2):
                quarter, column = which(xy, turn, at_ref)
                product = nn(turned[mat], wide_half(source, quarter, column, half)).astype(BF)
                rows = [product[n * share : (n + 1) * share] for n in range(8)]
                for ref, here in ((mine_ref, turn == 0), (x_ref, xy == 0), (y_ref, xy == 1)):
                    if turn == 0 and ref is mine_ref:
                        for n in range(8):
                            ref[n] = rows[n]
                    elif turn == 1 and ref is not mine_ref:

                        @pl.when(here)
                        def _(ref=ref):
                            for n in range(8):
                                ref[n] = rows[n]


def feed_both(at, hidden, o, up, vec, factor, wa, w1, w2):
    rows, width = hidden.shape
    share, half = width // 8, width // 2
    whole = pl.BlockSpec((rows, width), lambda t: (0, 0))
    once = pl.BlockSpec((rows, width), lambda t: (0, 0), pipeline_mode=pl.Buffered(1))
    flat = jax.ShapeDtypeStruct((rows, width), BF)

    def mat_of(t):
        return jnp.maximum(t - 8, 0) // 2

    return pl.pallas_call(
        functools.partial(feed_both_kernel, [len(w[1]) for w in (wa, w1, w2)]),
        grid=(12,),
        in_specs=[
            SMEM,
            once,
            once,
            once,
            pl.BlockSpec(vec.shape, lambda t: (0, 0)),
            pl.BlockSpec(factor.shape, lambda t: (0, 0)),
        ]
        + view(wa, lambda t: 3)
        + view(w1, lambda t: jnp.minimum(t, 3))
        + view(w2, lambda t: jnp.minimum(t, 3)),
        out_specs=[whole] * 4
        + [
            pl.BlockSpec((8, width), lambda t: (0, 0)),
            pl.BlockSpec(
                (8, None, None, share, half), lambda t: (0, jnp.maximum(t - 8, 0) % 2, mat_of(t), 0, 0)
            ),
            pl.BlockSpec((8, None, share, half), lambda t: (0, mat_of(t), 0, 0)),
            pl.BlockSpec((8, None, share, half), lambda t: (0, mat_of(t), 0, 0)),
        ],
        out_shape=[flat] * 4
        + [
            jax.ShapeDtypeStruct((8, width), F32),
            jax.ShapeDtypeStruct((8, 2, 2, share, half), BF),
            jax.ShapeDtypeStruct((8, 2, share, half), BF),
            jax.ShapeDtypeStruct((8, 2, share, half), BF),
        ],
        scratch_shapes=[
            pltpu.VMEM((rows, width), F32),
            pltpu.VMEM((4, width, width), BF),
            pltpu.VMEM((4, width, width), BF),
            pltpu.VMEM((width, width), BF),
            pltpu.VMEM((rows, width), BF),
            pltpu.VMEM((rows, width), BF),
            pltpu.VMEM((rows, width), BF),
            pltpu.VMEM((4, rows, width), BF),
            pltpu.VMEM((4, rows, width), F32),
            pltpu.VMEM((4, rows, width), BF),
            pltpu.VMEM((2, width, rows), BF),
        ],
        compiler_params=pltpu.CompilerParams(vmem_limit_bytes=60 * 2**20),
        cost_estimate=cost(34),
        name="feed_both",
    )(at, hidden, o, up, vec, factor, *wa[1], *w1[1], *w2[1])


def feed_back_whole_kernel(
    counts, at_ref, up_ref, mid_ref, a_ref, vec_ref, factor_ref, slope_ref, gb_ref, *refs
):
    wo_refs, w1_refs, w2_refs, refs = cut(refs, counts)
    back_ref, eba_ref, do_ref, sums_ref, keep_ref, send_ref = refs[:6]
    total, held1, held2, eb, du, turned, held = refs[6:]
    step = pl.program_id(0)
    core = at_ref[2]

    @pl.when(step == 0)
    def _():
        own = (factor_ref[:, 1:2] * up_ref[...].astype(F32)).astype(BF)
        eb[...] = own
        sums_ref[2:3] = column_sum(own.astype(F32))
        total[...] = jnp.zeros_like(total)
        turned[0] = a_ref[...].T
        turned[1] = own.T

    @pl.when(step < 4)
    def _():
        own = (nn(eb[...], load(w2_refs, core, held2)) * slope_ref[...]).astype(BF)
        du[step] = own
        sums_ref[pl.ds(3 + step, 1), :] = column_sum(own.astype(F32))
        total[...] += nt(own, load(w1_refs, core, held1))

    @pl.when(step == 3)
    def _():
        scaled, inverse = centered(mid_ref[...].astype(F32))
        dn = total[...]
        sums_ref[0:1] = column_sum(dn * scaled)
        sums_ref[1:2] = column_sum(dn)
        up = up_ref[...].astype(F32) + normalize_back(dn, scaled, inverse, vec_ref[5:6])
        up = up.astype(BF)
        back_ref[...] = up
        eba = (factor_ref[:, 0:1] * up.astype(F32)).astype(BF)
        eba_ref[...] = eba
        sums_ref[7:8] = column_sum(eba.astype(F32))
        do_ref[...] = nt(eba, load(wo_refs, core, held1)).astype(BF)

    half = keep_ref.shape[-1]
    for mat in range(2):

        @pl.when(jnp.logical_and(step >= 4 + 2 * mat, step < 6 + 2 * mat))
        def _(mat=mat):
            for turn in range(2):
                quarter, column = which((step - 4) % 2, turn, at_ref)
                if mat == 0:
                    right = wide_half(du, quarter, column, half)
                else:
                    right = gb_ref[:, pl.ds(pl.multiple_of(column * half, 128), half)]
                spread(nn(turned[mat], right), core, keep_ref.at[turn], send_ref.at[turn], held)


def feed_back_whole(at, up, mid, a, vec, factor, slope, gb, wa, w1, w2):
    rows, width = up.shape
    share, half = width // 8, width // 2
    whole = pl.BlockSpec((rows, width), lambda t, at: (0, 0))
    once = pl.BlockSpec((rows, width), lambda t, at: (0, 0), pipeline_mode=pl.Buffered(1))
    flat = jax.ShapeDtypeStruct((rows, width), BF)

    def scalars_too(specs):
        return [
            pl.BlockSpec(spec.block_shape, functools.partial(lambda f, t, at: f(t), spec.index_map))
            for spec in specs
        ]

    def gb_at(t, at):
        return which(jnp.where(t == 7, 1, 0), 0, at)[0], 0, 0

    chunk = pl.BlockSpec(
        (None, 2, 4, None, share, half),
        lambda t, at: (jnp.maximum(t - 4, 0) % 2, 0, 0, jnp.maximum(t - 4, 0) // 2, 0, 0),
    )
    return pl.pallas_call(
        functools.partial(feed_back_whole_kernel, [len(w[1]) for w in (wa, w1, w2)]),
        grid_spec=pltpu.PrefetchScalarGridSpec(
            num_scalar_prefetch=1,
            grid=(8,),
            in_specs=[
                once,
                once,
                once,
                pl.BlockSpec(vec.shape, lambda t, at: (0, 0)),
                pl.BlockSpec(factor.shape, lambda t, at: (0, 0)),
                pl.BlockSpec((None, rows, width), lambda t, at: (jnp.minimum(t, 3), 0, 0)),
                pl.BlockSpec((None, rows, width), gb_at),
            ]
            + scalars_too(
                view(wa, lambda t: 3)
                + view(w1, lambda t: jnp.minimum(t, 3))
                + view(w2, lambda t: jnp.minimum(t, 3))
            ),
            out_specs=[whole] * 3 + [pl.BlockSpec((8, width), lambda t, at: (0, 0)), chunk, chunk],
            scratch_shapes=[
                pltpu.VMEM((rows, width), F32),
                pltpu.VMEM((width, width), BF),
                pltpu.VMEM((width, width), BF),
                pltpu.VMEM((rows, width), BF),
                pltpu.VMEM((4, rows, width), BF),
                pltpu.VMEM((2, width, rows), BF),
                pltpu.VMEM((width, half), F32),
            ],
        ),
        out_shape=[flat] * 3
        + [jax.ShapeDtypeStruct((8, width), F32)]
        + [jax.ShapeDtypeStruct((2, 2, 4, 2, share, half), BF)] * 2,
        compiler_params=pltpu.CompilerParams(vmem_limit_bytes=60 * 2**20),
        cost_estimate=cost(22),
        name="feed_back_whole",
    )(at, up, mid, a, vec, factor, slope, gb, *wa[1], *w1[1], *w2[1])


def owner_outs(count, rows, width, mat):
    share, half = width // 8, width // 2
    shapes = [jax.ShapeDtypeStruct((8, 2, count, share, half), BF)]
    shapes += [jax.ShapeDtypeStruct((8, count, share, half), BF)] * 2
    outs = [
        pl.BlockSpec((8, None, None, share, half), lambda *i: (0, i[-3], mat(*i), 0, 0)),
        pl.BlockSpec((8, None, share, half), lambda *i: (0, mat(*i), 0, 0)),
        pl.BlockSpec((8, None, share, half), lambda *i: (0, mat(*i), 0, 0)),
    ]
    return shapes, outs


def attention_weights_grad(at, a, o, joined, eb, vector_rows=None):
    rows, width = a.shape
    count = 1
    more = 0 if vector_rows is None else vector_rows.shape[1]
    shapes, block, scratch = weight_outs(count, rows, width, more)
    whole = pl.BlockSpec((rows, width), lambda i, j, at: (0, 0))

    def joined_at(i, j, at):
        quarter, half = which(i, j, at)
        return jnp.minimum(quarter, 2), 0, half

    if vector_rows is None:
        shapes, outs = owner_outs(count, rows, width, lambda i, j, at: 0)
        extra, extra_specs = (), []
    else:
        outs = [pl.BlockSpec(block, lambda i, j, at: (i, j, 0, 0, 0, 0))] * 2
        extra = (vector_rows,)
        extra_specs = [pl.BlockSpec(vector_rows.shape, lambda i, j, at: (0, 0, 0))]
    return pl.pallas_call(
        functools.partial(attention_weight_kernel, vector_rows is not None),
        grid_spec=pltpu.PrefetchScalarGridSpec(
            num_scalar_prefetch=1,
            grid=(2, 2),
            in_specs=[
                whole,
                whole,
                pl.BlockSpec((None, rows, width // 2), joined_at),
                pl.BlockSpec((rows, width // 2), lambda i, j, at: (0, which(i, j, at)[1])),
            ]
            + extra_specs,
            out_specs=outs,
            scratch_shapes=scratch,
        ),
        out_shape=shapes,
        compiler_params=pltpu.CompilerParams(vmem_limit_bytes=VMEM_LIMIT),
        cost_estimate=cost(8),
        name="attention_weights",
    )(at, a, o, joined, eb, *extra)


def units_kernel(*refs):
    out_ref, slot = refs[-1], 0
    for mine_ref, x_ref, y_ref in (refs[:3], refs[3:6]):
        count = x_ref.shape[0]
        for xy, got in enumerate((x_ref, y_ref)):
            total = mine_ref[xy].astype(F32) + got[...].astype(F32)
            out_ref[xy, slot : slot + count] = total.astype(BF)
        slot += count


def units_sum(*groups):
    specs, total = [], 0
    for mine, x_got, y_got in groups:
        owners, _, count, share, half = mine.shape
        one = pl.BlockSpec((None, count, share, half), lambda n: (n, 0, 0, 0))
        specs += [pl.BlockSpec((None, 2, count, share, half), lambda n: (n, 0, 0, 0, 0)), one, one]
        total += count
    return pl.pallas_call(
        units_kernel,
        grid=(owners,),
        in_specs=specs,
        out_specs=pl.BlockSpec((None, 2, total, share, half), lambda n: (n, 0, 0, 0, 0)),
        out_shape=jax.ShapeDtypeStruct((owners, 2, total, share, half), BF),
        cost_estimate=cost(6),
        name="units_sum",
    )(*[array for group in groups for array in group])


def adam_step(weight, first, second, gradient, rate, decay_on):
    mean_next = beta_one * first + (1.0 - beta_one) * gradient
    square_next = beta_two * second + (1.0 - beta_two) * gradient * gradient
    step_next = rate * (
        mean_next / bias_one / (jnp.sqrt(square_next / bias_two) + adam_eps) + decay_on * weight
    )
    return (mean_next, square_next, step_next)


def adam_update(weight, first_moment, second_moment, gradient, layer_rates, decay_on):
    rate = layer_rates.reshape((-1,) + (1,) * (weight.ndim - 1))
    return adam_step(weight, first_moment, second_moment, gradient, rate, decay_on)


def adam_kernel(layer, placed, at_ref, rate_ref, grad_ref, weight_ref, first_ref, second_ref, *rest):
    outs = rest[-4:]
    s = at_ref[0]
    half = grad_ref.shape[-1]
    order = ((0, 0), (1, 0), (0, 1), (2, 1), (2, 0), (3, 0), (1, 1), (3, 1))
    for n, (device, xy) in enumerate(order):
        at = pl.ds(n * half, half)
        gradient = grad_ref[device if placed else s ^ device, xy].astype(F32)
        new = adam_step(
            weight_ref[:, at], first_ref[:, at], second_ref[:, at], gradient, rate_ref[layer], decay_rate
        )
        for ref, value in zip(outs, (gradient,) + new):
            ref[:, at] = value


def adam(at, rates, gradient, weight, first, second, layer, slot, into):
    count = 1 if weight.ndim == 3 else weight.shape[1]
    share, columns = weight.shape[-2:]
    half = gradient.shape[-1]
    if weight.ndim == 3:
        spec = pl.BlockSpec((None, share, columns), lambda m, at, rates: (layer, 0, 0))
    else:
        spec = pl.BlockSpec((None, None, share, columns), lambda m, at, rates: (layer, m, 0, 0))
    extra = () if into is None else tuple(into)
    return pl.pallas_call(
        functools.partial(adam_kernel, layer, layer == 1),
        grid_spec=pltpu.PrefetchScalarGridSpec(
            num_scalar_prefetch=2,
            grid=(count,),
            in_specs=[
                pl.BlockSpec((4, 2, None, share, half), lambda m, at, rates: (0, 0, slot + m, 0, 0)),
                spec,
                spec,
                spec,
            ]
            + [pl.BlockSpec(memory_space=pl.ANY)] * len(extra),
            out_specs=[spec] * 4,
        ),
        out_shape=[jax.ShapeDtypeStruct(weight.shape, F32)] * 4,
        input_output_aliases={6 + n: n for n in range(len(extra))},
        compiler_params=pltpu.CompilerParams(vmem_limit_bytes=VMEM_LIMIT),
        cost_estimate=cost(6),
        name="adam",
    )(at, rates, gradient, weight, first, second, *extra)


def assemble_kernel(at_ref, own, far, x_far, y_far, d_left, d_right, out_ref):
    z, step = at_ref[1], pl.program_id(1)
    half = d_left.shape[-1]
    out_ref[z] = own[...]
    for n, source in enumerate((far, x_far, y_far)):

        @pl.when(step == n)
        def _(source=source):
            for k in range(3):
                out_ref[lax.rem(z + 3 - k, 4)] = source[k]

    @pl.when(step == 3)
    def _():
        for k in range(3):
            out_ref[lax.rem(z + 3 - k, 4), :, :half] = d_left[k]
            out_ref[lax.rem(z + 3 - k, 4), :, half:] = d_right[k]


def assemble(at, sources, first):
    count, _, share, width = sources[0].shape
    piece = pl.BlockSpec((3, None, share, width), lambda m, j, at: (0, first + m, 0, 0))
    cut = pl.BlockSpec((3, None, share, width // 2), lambda m, j, at: (0, first + m, 0, 0))
    own = pl.BlockSpec((None, None, share, width), lambda m, j, at: (m, at[0] ^ j, 0, 0))
    return pl.pallas_call(
        assemble_kernel,
        grid_spec=pltpu.PrefetchScalarGridSpec(
            num_scalar_prefetch=1,
            grid=(count, 4),
            in_specs=[own, piece, piece, piece, cut, cut],
            out_specs=pl.BlockSpec(
                (None, None, 4, share, width), lambda m, j, at: (m, at[0] ^ j, 0, 0, 0)
            ),
        ),
        out_shape=jax.ShapeDtypeStruct((count, 4, 4, share, width), BF),
        compiler_params=pltpu.CompilerParams(vmem_limit_bytes=VMEM_LIMIT),
        cost_estimate=cost(3 * count),
        name="assemble",
    )(at, *sources)


def pack_kernel(at_ref, wa_ref, wf_ref, flat_ref, a_ref, b_ref, c_ref):
    share = wa_ref.shape[1]
    a_ref[:share] = wa_ref[0].astype(BF)
    a_ref[share:] = flat_ref[...]
    for n in range(2):
        b_ref[n * share : (n + 1) * share] = wf_ref[0, n].astype(BF)
        c_ref[n * share : (n + 1) * share] = wf_ref[1, n].astype(BF)
    b_ref[2 * share :] = wa_ref[1].astype(BF)


def pack(at, wa, wf, flat):
    layers, share, columns = wa.shape
    width = columns // 4
    shapes = [(share + flat.shape[0], width), (3 * share, width), (2 * share, width)]
    return pl.pallas_call(
        pack_kernel,
        grid_spec=pltpu.PrefetchScalarGridSpec(
            num_scalar_prefetch=1,
            grid=(1,),
            in_specs=[
                pl.BlockSpec((layers, share, width), lambda i, at: (0, 0, at[0])),
                pl.BlockSpec((layers, 2, share, width), lambda i, at: (0, 0, 0, at[0])),
                pl.BlockSpec(flat.shape, lambda i, at: (0, 0)),
            ],
            out_specs=[pl.BlockSpec(shape, lambda i, at: (0, 0)) for shape in shapes],
        ),
        out_shape=[jax.ShapeDtypeStruct(shape, BF) for shape in shapes],
        cost_estimate=cost(2),
        name="pack",
    )(at, wa, wf, flat)


def cast_kernel(weight_ref, out_ref):
    out_ref[...] = weight_ref[...].astype(BF)


def cast_blocks(weight, layer):
    share, columns = weight.shape[-2:]
    count = 1 if weight.ndim == 3 else weight.shape[1]
    if weight.ndim == 3:
        spec = pl.BlockSpec((None, share, columns // 4), lambda m, q: (layer, 0, q))
    else:
        spec = pl.BlockSpec((None, None, share, columns // 4), lambda m, q: (layer, m, 0, q))
    return pl.pallas_call(
        cast_kernel,
        grid=(count, 4),
        in_specs=[spec],
        out_specs=pl.BlockSpec((None, None, share, columns // 4), lambda m, q: (m, q, 0, 0)),
        out_shape=jax.ShapeDtypeStruct((count, 4, share, columns // 4), BF),
        cost_estimate=cost(3 * count),
        name="cast",
    )(weight)


def after(value, *others):
    return lax.optimization_barrier((value,) + others)[0]


def shards(
    patches,
    positions,
    image_sizes,
    keep_masks,
    output_grad,
    vector_params,
    attention_weights,
    feedforward_weights,
    vector_first,
    attention_first,
    feedforward_first,
    vector_second,
    attention_second,
    feedforward_second,
    layer_rates,
):
    both = ("section", "dp")
    micro_count, row_count, width = patches.shape
    layers = vector_params.shape[0]
    share = attention_weights.shape[1]
    half = width // 2
    s = lax.axis_index("section")
    d = lax.axis_index("dp")
    s_low, s_high = s % 2, s // 2
    unit = s_low ^ s_high
    across = [(i, i ^ 1) for i in range(4)]
    along = [(i, i ^ 2) for i in range(4)]
    athwart = [(i, i ^ 3) for i in range(4)]
    shards_dp = lax.axis_size("dp")
    tuned = shards_dp == 8
    around = [[(i, (i + 2 * k) % 8) for i in range(8)] for k in (1, 2, 3)]
    swap = [(i, i ^ 1) for i in range(8)]
    at = jnp.stack([s, d // 2, d % 2]).astype(jnp.int32)
    z = d // 2

    def quarter(array):
        return lax.dynamic_slice_in_dim(array, s * width, width, axis=array.ndim - 1)

    if tuned:
        flat = vector_params.astype(BF).reshape(-1, share * 8)
        flat = jnp.pad(flat, ((0, 16 - flat.shape[0]), (0, 0)))
        a_sent, b_sent, c_sent = pack(at, attention_weights, feedforward_weights, flat)

        def around_z(sent):
            return [lax.ppermute(sent, "dp", route) for route in around]

        def around_xy(far):
            x_far = lax.ppermute(far, "section", across)
            y_far = lax.ppermute(far, "section", along)
            return x_far, y_far

        def around_d(x_far, y_far):
            d_left = lax.ppermute(y_far[..., :half], "section", across)
            d_right = lax.ppermute(x_far[..., half:], "section", along)
            return d_left, d_right

        def swapped(half_rows):
            return (half_rows, lax.ppermute(half_rows, "dp", swap))

        far = around_z(a_sent)
        vector_pieces = jnp.stack([flat] + [f[share:] for f in far])
        a_far = jnp.stack([f[:share] for f in far]).reshape(3, 1, share, width)
        a_far, b_sent = lax.optimization_barrier((a_far, b_sent))
        a_x, a_y = around_xy(a_far)
        wa_in, wf_in, _ = lax.optimization_barrier((attention_weights, feedforward_weights, a_far))
        a_blocks, t_blocks = cast_blocks(attention_weights, 0), cast_blocks(wa_in, 1)
        b_blocks, c_blocks = cast_blocks(feedforward_weights, 0), cast_blocks(wf_in, 1)
        b_far = jnp.stack(around_z(b_sent)).reshape(3, 3, share, width)
        a_x, a_y, b_far, c_sent, a_blocks, b_blocks, c_blocks, t_blocks = lax.optimization_barrier(
            (a_x, a_y, b_far, c_sent, a_blocks, b_blocks, c_blocks, t_blocks)
        )
        a_left, a_right = around_d(a_x, a_y)
        b_x, b_y = around_xy(b_far)
        a_halves = swapped(assemble(at, (a_blocks, a_far, a_x, a_y, a_left, a_right), 0))
        a_halves, c_sent = lax.optimization_barrier((a_halves, c_sent))
        c_far = around_z(c_sent)
        both_cores = jnp.stack([vector_pieces, lax.ppermute(vector_pieces, "dp", swap)])
        chips = (d // 2 - jnp.arange(4)) % 4
        order = jnp.where(jnp.arange(4)[:, None] == chips[None, :], 1.0, 0.0).astype(BF)
        both_cores = jnp.einsum("zk,kcrw->zcrw", order, both_cores.transpose(1, 0, 2, 3))
        ordered = jnp.where(d % 2 == 0, both_cores, both_cores[:, ::-1])
        ordered = ordered.reshape(8, -1)[:, : layers * 12 * share].reshape(8, layers, 12, share)
        vectors = ordered.transpose(1, 2, 0, 3).reshape(layers, 12, width).astype(F32)
        weights = [[("halves", a_halves, 0)], []]
    else:

        def gathered(piece):
            piece = lax.all_gather(quarter(piece).astype(BF), both, axis=0, tiled=True)
            return ("full", (piece.reshape(4, 1, width, width),), 0)

        vectors = lax.all_gather(vector_params.astype(BF), "dp", axis=2, tiled=True).astype(F32)
        weights = [
            (
                gathered(attention_weights[l]),
                gathered(feedforward_weights[l, 0]),
                gathered(feedforward_weights[l, 1]),
            )
            for l in range(layers)
        ]

    image_ids = lax.dynamic_index_in_dim(image_sizes[:, 0], unit, 0, keepdims=False)
    keep = lax.dynamic_index_in_dim(keep_masks[:, 0], unit, 0, keepdims=False)
    segment, member, inside, table_row = image_layout(image_ids, row_count)
    kept = jnp.sum(jnp.where(member[:, :, None], keep[None], 0), axis=1).astype(F32)
    factors = jnp.where(inside[:, None], kept / (1.0 - drop_rate), 1.0)
    patch_rows = lax.dynamic_index_in_dim(patches, unit, 0, keepdims=False).astype(F32)
    position_rows = jnp.take(positions, table_row, axis=0).astype(F32)
    hidden = patch_rows + jnp.where(inside[:, None], position_rows, 0.0)
    lane = jnp.arange(2 * HD, dtype=jnp.int32) % HD
    coded = lane[None, :] == segment[:, None]
    code_q = coded.astype(BF)
    code_k = jnp.where(coded | (lane[None, :] > image_sizes.shape[2]), 0.0, masked_score).astype(BF)

    saved = []
    output_rows = lax.dynamic_index_in_dim(output_grad, unit, 0, keepdims=False)
    for layer in range(layers):
        vec = vectors[layer]
        factor = factors[:, 2 * layer : 2 * layer + 2]
        a, joined = project(at, hidden, vec, weights[layer][0])
        if tuned and layer == 1:
            c_left, c_right, joined = lax.optimization_barrier((c_left, c_right, joined))
            c_halves = swapped(assemble(at, (c_blocks, c_far, c_x, c_y, c_left, c_right), 0))
            joined = after(joined, c_halves[0])
            weights[1] += [("halves", c_halves, 0), ("halves", c_halves, 1)]
        o, lse = attention(joined, code_q, code_k)
        if tuned and layer == 0:
            b_x, b_y, c_far, o = lax.optimization_barrier((b_x, b_y, c_far, o))
            b_left, b_right = around_d(b_x, b_y)
            c_far = jnp.stack(c_far).reshape(3, 2, share, width)
            c_x, c_y = around_xy(c_far)
            b_halves = swapped(assemble(at, (b_blocks, b_far, b_x, b_y, b_left, b_right), 0))
            t_blocks = after(t_blocks, b_halves[0])
            t_halves = swapped(assemble(at, (t_blocks, b_far, b_x, b_y, b_left, b_right), 2))
            o = after(o, t_halves[0])
            weights[0] += [("halves", b_halves, 0), ("halves", b_halves, 1)]
            weights[1] += [("halves", t_halves, 0)]
        wa, w1, w2 = weights[layer]
        if tuned and layer == 1:
            hidden, up1, eba1, do1, sums1, kept_feed, x_sent, y_sent = feed_both(
                at, hidden, o, output_rows, vec, factor, wa, w1, w2
            )
            saved.append((saved_hidden, a, joined, o, lse))
            break
        mid, a2, gb, slope, following = feed(at, hidden, o, vec, factor, wa, w1, w2)
        saved.append((hidden, a, joined, o, lse, mid, a2, gb, slope))
        hidden = following
        if tuned and layer == 0:
            c_x, c_y, hidden = lax.optimization_barrier((c_x, c_y, hidden))
            c_left, c_right = around_d(c_x, c_y)
            saved_hidden = hidden

    def pick(index, options):
        value = options[0]
        for n in range(1, len(options)):
            value = jnp.where(index == n, options[n], value)
        return value

    def outward(rows):
        blocks = [rows[:, i * (width // 4) : (i + 1) * (width // 4)] for i in range(4)]
        return pick(s, blocks), lax.ppermute(pick(s ^ 1, blocks), "section", across)

    def ordered_units(mine, theirs):
        return jnp.where(unit == 0, jnp.stack([mine, theirs]), jnp.stack([theirs, mine]))

    def over_units(here):
        return (
            lax.ppermute(here[0, 1], "section", across),
            lax.ppermute(here[1, 1], "section", along),
        )

    def added(kept_part, got):
        return (kept_part.astype(F32) + got.astype(F32)).astype(BF)

    def units_added(here, x_got, y_got):
        return (here[:, 0].astype(F32) + jnp.stack([x_got, y_got]).astype(F32)).astype(BF)

    def over_chips(summed):
        return [
            lax.ppermute(
                lax.dynamic_index_in_dim(summed, (z + k) % 4, 1, keepdims=False), "dp", route
            )
            for k, route in zip((1, 2, 3), around)
        ]

    def chips_added(summed, got):
        total = lax.dynamic_index_in_dim(summed, z, 1, keepdims=False).astype(F32)
        for part in got:
            total = total + part.astype(F32)
        return total.astype(BF)

    def over_sections(total):
        return [lax.ppermute(total, "section", route) for route in (across, along, athwart)]

    def joint(*values):
        return lax.optimization_barrier(values)

    def reduced_plainly(pairs):
        count = len(pairs)
        summed = []
        for xy, (side, route) in enumerate(((s_low, across), (s_high, along))):
            parts = [pair[xy].astype(BF) for pair in pairs]
            mine = [lax.dynamic_slice_in_dim(part, side * half, half, 1) for part in parts]
            other = [lax.dynamic_slice_in_dim(part, (1 - side) * half, half, 1) for part in parts]
            other = lax.ppermute(jnp.concatenate(other, axis=1), "section", route)
            summed.append((jnp.concatenate(mine, axis=1).astype(F32) + other.astype(F32)).astype(BF))
        stacked = jnp.concatenate(summed, axis=1)
        scattered = lax.psum_scatter(stacked, "dp", scatter_dimension=0, tiled=True)
        everyone = lax.all_gather(scattered, "section", axis=0, tiled=False)
        everyone = everyone.reshape(4, share, 2, count, half)
        order = ((0, 0), (1, 0), (0, 1), (2, 1), (2, 0), (3, 0), (1, 1), (3, 1))
        return [
            jnp.concatenate([everyone[dev, :, xy, mat] for dev, xy in order], axis=1).astype(F32)
            for mat in range(count)
        ]

    up = output_rows
    vector_rows = [None] * layers

    def put_rows(layer, attention_sums, feed_sums):
        vector_rows[layer] = jnp.concatenate(
            [attention_sums[0:3], attention_sums[4:5], feed_sums[7:8], feed_sums[0:7]]
        )

    def vectors_updated(vector_grad):
        return (vector_grad,) + adam_update(
            vector_params, vector_first, vector_second, vector_grad, layer_rates, 0.0
        )

    if tuned:
        wa, w1, w2 = weights[1]
        start, a, joined, o, lse = saved[1]
        up, eba, do, feed_sums = up1, eba1, do1, sums1
        do, kept_feed, x_sent, y_sent = joint(do, kept_feed, x_sent, y_sent)
        x_feed = lax.ppermute(x_sent, "section", across)
        y_feed = lax.ppermute(y_sent, "section", along)
        dqkv = attention_back(joined, do, lse, code_q, code_k)
        kept1, x_sent, y_sent = attention_weights_grad(at, a, o, dqkv, eba)
        x_feed, y_feed, kept1, x_sent, y_sent = joint(x_feed, y_feed, kept1, x_sent, y_sent)
        up = after(up, kept1)
        x_got = lax.ppermute(x_sent, "section", across)
        y_got = lax.ppermute(y_sent, "section", along)
        up, attention_sums = project_back(at, up, start, vectors[1], dqkv, wa)
        put_rows(1, attention_sums, feed_sums)
        x_got, y_got, up, hidden = joint(x_got, y_got, up, hidden)
        block_mine, block_theirs = outward(hidden)
        summed1 = units_sum((kept1, x_got, y_got), (kept_feed, x_feed, y_feed))
        total1 = lax.psum_scatter(summed1, "dp", scatter_dimension=0, tiled=True)
        up = after(up, summed1)
        wa, w1, w2 = weights[0]
        start, a, joined, o, lse, mid, a2, gb, slope = saved[0]
        up, eba, do, feed_sums, kept2, sent2 = feed_back_whole(
            at, up, mid, a2, vectors[0], factors[:, 0:2], slope, gb, wa, w1, w2
        )
        got2 = lax.ppermute(sent2, "dp", swap)
        here2 = added(kept2, got2)
        do = after(do, here2)
        x_got, y_got = over_units(here2)
        dqkv = attention_back(joined, do, lse, code_q, code_k)
        x_got, y_got, dqkv, total1 = joint(x_got, y_got, dqkv, total1)
        gradient1 = lax.all_gather(total1[0], "section", axis=0, tiled=False)
        summed2 = units_added(here2, x_got, y_got)
        dqkv = after(dqkv, summed2)
        z_got = over_chips(summed2)
        up, attention_sums = project_back(at, up, start, vectors[0], dqkv, wa)
        put_rows(0, attention_sums, feed_sums)
        rows_all = jnp.concatenate(vector_rows).astype(BF)
        lines = layers * 12 * share // half
        rows_all = rows_all.reshape(lines, half // share, 8, share).transpose(2, 0, 1, 3)
        rows_all = jnp.pad(rows_all.reshape(8, lines, half), ((0, 0), (0, 16 - lines), (0, 0)))
        dqkv, up = joint(dqkv, up)
        kept3, sent3 = attention_weights_grad(at, a, o, dqkv, eba, rows_all)
        got3 = lax.ppermute(sent3, "dp", swap)
        here3 = added(kept3, got3)
        x_got, y_got = over_units(here3)
        x_got, y_got, *z_got = joint(x_got, y_got, *z_got)
        summed3 = units_added(here3, x_got, y_got)
        z_got3 = over_chips(summed3)
        total2 = after(chips_added(summed2, z_got), summed3)
        g_got2 = over_sections(total2)
        gradient1 = after(gradient1, total2)
        attention_out = adam(
            at, layer_rates, gradient1, attention_weights, attention_first,
            attention_second, 1, 0, None,
        )
        feed_out = adam(
            at, layer_rates, gradient1, feedforward_weights, feedforward_first,
            feedforward_second, 1, 1, None,
        )
        *z_got3, attention_out0, feed_out0 = joint(*z_got3, attention_out[0], feed_out[0])
        attention_out = [attention_out0] + list(attention_out[1:])
        feed_out = [feed_out0] + list(feed_out[1:])
        total3 = chips_added(summed3, z_got3)
        g_got3 = over_sections(total3[:, :, :share])
        input_mine, input_theirs = outward(after(up, total3))
        vector_grad = total3[0, 0, share : share + lines].astype(F32)
        vector_grad = vector_grad.reshape(layers, 12, share)
        vector_out = vectors_updated(vector_grad)
        gradient2 = jnp.stack([total2] + g_got2)
        gradient2 = after(gradient2, total3)
        feed_out = adam(
            at, layer_rates, gradient2, feedforward_weights, feedforward_first,
            feedforward_second, 0, 0, feed_out,
        )
        *g_got3, feed_out0 = joint(*g_got3, feed_out[0])
        feed_out = [feed_out0] + list(feed_out[1:])
        gradient3 = jnp.stack([total3[:, :, :share]] + g_got3)
        attention_out = adam(
            at, layer_rates, gradient3, attention_weights, attention_first,
            attention_second, 0, 0, attention_out,
        )
    else:
        plain_attention, plain_feed = [None] * layers, [None] * layers
        block_mine, block_theirs = outward(hidden)

        def x_of(array):
            return jnp.where(s_high == 0, array[0], array[2])

        def y_of(array):
            return jnp.where(s_low == 0, array[1], array[3])

        for layer in reversed(range(layers)):
            wa, w1, w2 = weights[layer]
            start, a, joined, o, lse, mid, a2, gb, slope = saved[layer]
            factor = factors[:, 2 * layer : 2 * layer + 2]
            eb, du, up, eba, do, feed_sums = feed_back(
                at, up, mid, vectors[layer], factor, slope, wa, w1, w2
            )
            dqkv = attention_back(joined, do, lse, code_q, code_k)
            up, attention_sums = project_back(at, up, start, vectors[layer], dqkv, wa)
            put_rows(layer, attention_sums, feed_sums)
            all_four = jnp.concatenate([dqkv, eba[None]])
            plain_feed[layer] = jnp.stack(
                reduced_plainly(
                    [(tn(a2, x_of(du)), tn(a2, y_of(du))), (tn(eb, x_of(gb)), tn(eb, y_of(gb)))]
                )
            )
            y_left = jnp.where(s_low == 0, a, o)
            plain_attention[layer] = reduced_plainly(
                [(tn(a, x_of(all_four)), tn(y_left, y_of(all_four)))]
            )[0]
        rows_all = jnp.concatenate(vector_rows)
        rows_all = rows_all + lax.ppermute(rows_all, "section", across)
        rows_all = jnp.pad(rows_all, ((0, 128 - rows_all.shape[0]), (0, 0))).T
        vector_grad = lax.psum_scatter(rows_all, "dp", scatter_dimension=0, tiled=True)
        vector_out = vectors_updated(vector_grad[:, : layers * 12].T.reshape(layers, 12, share))
        input_mine, input_theirs = outward(up)
        gradient = jnp.stack(plain_attention)
        attention_out = (gradient,) + adam_update(
            attention_weights, attention_first, attention_second, gradient, layer_rates, decay_rate
        )
        gradient = jnp.stack(plain_feed)
        feed_out = (gradient,) + adam_update(
            feedforward_weights,
            feedforward_first,
            feedforward_second,
            gradient,
            layer_rates,
            decay_rate,
        )
    outs = [
        ordered_units(block_mine, block_theirs),
        ordered_units(input_mine, input_theirs).astype(F32),
    ]
    for group in zip(vector_out, attention_out, feed_out):
        outs.extend(group)
    return tuple(outs)


def solution(mesh):
    in_specs = (
        P(None, "dp", None),
        P(),
        P(None, "dp", None),
        P(None, "dp", None, None),
        P(None, "dp", None),
        P(None, None, "dp"),
        P(None, "dp", None),
        P(None, None, "dp", None),
        P(None, None, "dp"),
        P(None, "dp", None),
        P(None, None, "dp", None),
        P(None, None, "dp"),
        P(None, "dp", None),
        P(None, None, "dp", None),
        P(),
    )
    out_specs = (
        P(None, "dp", "section"),
        P(None, "dp", "section"),
        P(None, None, "dp"),
        P(None, "dp", None),
        P(None, None, "dp", None),
        P(None, None, "dp"),
        P(None, "dp", None),
        P(None, None, "dp", None),
        P(None, None, "dp"),
        P(None, "dp", None),
        P(None, None, "dp", None),
        P(None, None, "dp"),
        P(None, "dp", None),
        P(None, None, "dp", None),
    )
    return jax.shard_map(shards, mesh=mesh, in_specs=in_specs, out_specs=out_specs, check_vma=False)
```

```python
import functools

import jax
import jax.numpy as jnp
from jax import lax
from jax.experimental import pallas as pl
from jax.experimental.pallas import tpu as pltpu
from jax.sharding import PartitionSpec as P

H = 12
HD = 64
GRID_S = 10
GRID_M = 14
GRID_L = 24

beta_one = 0.9
beta_two = 0.999
bias_one = 1.0 - 0.9**10
bias_two = 1.0 - 0.999**10
adam_eps = 1e-08
decay_rate = 0.05
drop_rate = 0.1
norm_eps = 1e-06
masked_score = -1e30
root_half = 0.7071067811865476
normal_peak = 0.3989422804014327
BF = jnp.bfloat16
F32 = jnp.float32


def image_layout(image_ids, row_count):
    small_len = GRID_S * GRID_S + 2
    middle_len = GRID_M * GRID_M + 2
    large_len = GRID_L * GRID_L + 2
    slots = image_ids.shape[0]
    lengths = jnp.where(
        image_ids == 0,
        small_len,
        jnp.where(image_ids == 1, middle_len, jnp.where(image_ids == 2, large_len, 0)),
    ).astype(jnp.int32)
    slot = jnp.arange(slots, dtype=jnp.int32)
    slot_ends = jnp.sum(jnp.where(slot[None, :] <= slot[:, None], lengths[None, :], 0), axis=1)
    slot_starts = slot_ends - lengths
    row_index = jnp.arange(row_count, dtype=jnp.int32)
    segment = jnp.sum((row_index[:, None] >= slot_ends[None, :]).astype(jnp.int32), axis=1)
    member = segment[:, None] == slot[None, :]
    first_row = jnp.sum(jnp.where(member, slot_starts[None, :], 0), axis=1)
    kind_row = jnp.sum(jnp.where(member, image_ids[None, :], 0), axis=1)
    table_start = jnp.where(
        kind_row == 0, 0, jnp.where(kind_row == 1, small_len, small_len + middle_len)
    ).astype(jnp.int32)
    in_image = segment < slots
    table_row = jnp.where(in_image, table_start + row_index - first_row, 0)
    return (segment, member, in_image, table_row)


def nn(a, b):
    return jnp.dot(a, b, preferred_element_type=F32)


def nt(a, b):
    return lax.dot_general(a, b, (((1,), (1,)), ((), ())), preferred_element_type=F32)


def tn(a, b):
    return lax.dot_general(a, b, (((0,), (0,)), ((), ())), preferred_element_type=F32)


def split3(value):
    high = value.astype(BF)
    rest = value - high.astype(F32)
    middle = rest.astype(BF)
    return high, middle, (rest - middle.astype(F32)).astype(BF)


def attention_kernel(q_ref, k_ref, v_ref, code_q_ref, code_k_ref, o_ref, lse_ref):
    low = lax.broadcasted_iota(jnp.int32, q_ref.shape, 1) < HD
    outs = []
    for half in range(2):
        own = low if half == 0 else jnp.logical_not(low)
        q = jnp.where(own, q_ref[...] * jnp.asarray(HD ** (-0.5), BF), code_q_ref[...])
        k = jnp.where(own, k_ref[...], code_k_ref[...])
        scores = nt(q, k)
        peak = jnp.max(scores, axis=-1, keepdims=True)
        e = jnp.exp(scores - peak)
        total = jnp.sum(e, axis=-1, keepdims=True)
        outs.append(nn(e.astype(BF), v_ref[...]) * (1.0 / total))
        lse_ref[:, half : half + 1] = peak + jnp.log(total)
    o_ref[...] = jnp.where(low, outs[0], outs[1]).astype(BF)


def attention_back_kernel(
    q_ref, k_ref, v_ref, do_ref, lse_ref, code_q_ref, code_k_ref, out_ref
):
    lane = lax.broadcasted_iota(jnp.int32, q_ref.shape, 1)
    low = lane < HD
    scale = HD ** (-0.5)
    dqs, dks, dvs = [], [], []
    for half in range(2):
        own = low if half == 0 else jnp.logical_not(low)
        spare = 32 + (HD if half == 0 else 0)
        q_scaled = q_ref[...] * jnp.asarray(scale, BF)
        q = jnp.where(own, q_scaled, code_q_ref[...])
        k = jnp.where(own, k_ref[...], code_k_ref[...])
        v = jnp.where(own, v_ref[...], jnp.zeros_like(v_ref[...]))
        for at, part in enumerate(split3(-lse_ref[:, half : half + 1])):
            here = lane == spare + at
            q = jnp.where(here, part, q)
            k = jnp.where(here, jnp.ones_like(k), k)
        p = jnp.exp(nt(k, q))
        dp = nt(v, do_ref[...])
        row = jnp.sum(p * dp, axis=0, keepdims=True)
        ds = (p * (dp - row)).astype(BF)
        dvs.append(nn(p.astype(BF), do_ref[...]))
        dks.append(nn(ds, q_scaled))
        dqs.append(tn(ds, k_ref[...]) * scale)
    out_ref[0] = jnp.where(low, dqs[0], dqs[1]).astype(BF)
    out_ref[1] = jnp.where(low, dks[0], dks[1]).astype(BF)
    out_ref[2] = jnp.where(low, dvs[0], dvs[1]).astype(BF)


VMEM_LIMIT = 56 * 2**20
TURNS = (1, 3, 2)


def cost(microseconds):
    return pl.CostEstimate(flops=int(microseconds * 1.1e9), bytes_accessed=2**20, transcendentals=0)


def centered(hidden):
    center = hidden - jnp.mean(hidden, axis=-1, keepdims=True)
    inverse = lax.rsqrt(jnp.mean(center * center, axis=-1, keepdims=True) + norm_eps)
    return center * inverse, inverse


def normalize_back(normed_grad, scaled, inverse, gain):
    scaled_grad = normed_grad * gain
    mid = scaled_grad - jnp.mean(scaled_grad, axis=-1, keepdims=True)
    return inverse * (mid - scaled * jnp.mean(scaled_grad * scaled, axis=-1, keepdims=True))


def column_sum(value):
    return jnp.sum(value, axis=0, keepdims=True)


def view(weight, index):
    specs = []
    for array in weight[1]:
        if weight[0] == "full":
            _, n, _, width = array.shape
            specs.append(
                pl.BlockSpec((None, n, width // n, width), lambda p: (index(p), 0, weight[2], 0))
            )
        else:
            _, _, n, share, width = array.shape
            specs.append(
                pl.BlockSpec((None, None, n, share, width), lambda p: (weight[2], index(p), 0, 0, 0))
            )
    return specs


def cut(refs, weights):
    out = []
    for count in weights:
        out.append(refs[:count])
        refs = refs[count:]
    return (*out, refs)


def load(refs, core, held):
    n, share, width = refs[0].shape
    if len(refs) == 1:
        return refs[0][...].reshape(n * share, width)
    for turn, ref in enumerate(refs):
        side = core if turn == 0 else 1 - core
        for chip in range(n):
            row = pl.multiple_of((2 * chip + side) * share, share)
            held[pl.ds(row, share), :] = ref[chip]
    return held[...]


SMEM = pl.BlockSpec(memory_space=pltpu.SMEM)


def project_kernel(count, at_ref, hidden_ref, vec_ref, *refs):
    normed_ref, joined_ref, held = refs[count:]
    weight = load(refs[:count], at_ref[2], held)
    part = pl.program_id(0)

    @pl.when(part == 0)
    def _():
        scaled, _ = centered(hidden_ref[...].astype(F32))
        normed_ref[...] = (scaled * vec_ref[0:1] + vec_ref[1:2]).astype(BF)

    bias = jnp.where(part == 0, vec_ref[2:3], jnp.where(part == 2, vec_ref[3:4], 0.0))
    joined_ref[...] = (nn(normed_ref[...], weight) + bias).astype(BF)


def project(at, hidden, vec, wa):
    rows, width = hidden.shape
    whole = pl.BlockSpec((rows, width), lambda p: (0, 0))
    return pl.pallas_call(
        functools.partial(project_kernel, len(wa[1])),
        grid=(3,),
        in_specs=[SMEM, whole, pl.BlockSpec(vec.shape, lambda p: (0, 0))] + view(wa, lambda p: p),
        out_specs=[whole, pl.BlockSpec((None, rows, width), lambda p: (p, 0, 0))],
        out_shape=[
            jax.ShapeDtypeStruct((rows, width), BF),
            jax.ShapeDtypeStruct((3, rows, width), BF),
        ],
        compiler_params=pltpu.CompilerParams(vmem_limit_bytes=VMEM_LIMIT),
        scratch_shapes=[pltpu.VMEM((width, width), BF)],
        cost_estimate=cost(7),
        name="project",
    )(at, hidden, vec, *wa[1])


def feed_kernel(counts, at_ref, hidden_ref, o_ref, vec_ref, factor_ref, *refs):
    wo_refs, w1_refs, w2_refs, refs = cut(refs, counts)
    mid_ref, normed_ref, gb_ref, slope_ref, out_ref, total, held1, held2 = refs
    part = pl.program_id(0)
    core = at_ref[2]

    @pl.when(part == 0)
    def _():
        branch = nn(o_ref[...], load(wo_refs, core, held1)) + vec_ref[4:5]
        mid = (hidden_ref[...].astype(F32) + factor_ref[:, 0:1] * branch).astype(BF)
        mid_ref[...] = mid
        scaled, _ = centered(mid.astype(F32))
        normed_ref[...] = (scaled * vec_ref[5:6] + vec_ref[6:7]).astype(BF)
        total[...] = jnp.zeros_like(total)

    w1 = load(w1_refs, core, held1)
    w2 = load(w2_refs, core, held2)
    u = nn(normed_ref[...], w1) + vec_ref[pl.ds(8 + part, 1), :]
    cdf = 0.5 * (1.0 + lax.erf(u * root_half))
    gb = (u * cdf).astype(BF)
    gb_ref[...] = gb
    slope_ref[...] = cdf + u * jnp.exp(-0.5 * u * u) * normal_peak
    total[...] += nt(gb, w2)

    @pl.when(part == 3)
    def _():
        branch = total[...] + vec_ref[7:8]
        out_ref[...] = (mid_ref[...].astype(F32) + factor_ref[:, 1:2] * branch).astype(BF)


def feed(at, hidden, o, vec, factor, wa, w1, w2):
    rows, width = hidden.shape
    whole = pl.BlockSpec((rows, width), lambda p: (0, 0))
    part = pl.BlockSpec((None, rows, width), lambda p: (p, 0, 0))
    flat = jax.ShapeDtypeStruct((rows, width), BF)
    return pl.pallas_call(
        functools.partial(feed_kernel, [len(w[1]) for w in (wa, w1, w2)]),
        grid=(4,),
        in_specs=[
            SMEM,
            whole,
            whole,
            pl.BlockSpec(vec.shape, lambda p: (0, 0)),
            pl.BlockSpec(factor.shape, lambda p: (0, 0)),
        ]
        + view(wa, lambda p: 3)
        + view(w1, lambda p: p)
        + view(w2, lambda p: p),
        out_specs=[whole, whole, part, part, whole],
        out_shape=[
            flat,
            flat,
            jax.ShapeDtypeStruct((4, rows, width), BF),
            jax.ShapeDtypeStruct((4, rows, width), F32),
            flat,
        ],
        scratch_shapes=[pltpu.VMEM((rows, width), F32)] + [pltpu.VMEM((width, width), BF)] * 2,
        compiler_params=pltpu.CompilerParams(vmem_limit_bytes=VMEM_LIMIT),
        cost_estimate=cost(17),
        name="feed",
    )(at, hidden, o, vec, factor, *wa[1], *w1[1], *w2[1])


def feed_back_kernel(counts, at_ref, up_ref, mid_ref, vec_ref, factor_ref, slope_ref, *refs):
    wo_refs, w1_refs, w2_refs, refs = cut(refs, counts)
    eb_ref, du_ref, out_ref, eba_ref, do_ref, sums_ref, total, held1, held2 = refs
    part = pl.program_id(0)
    core = at_ref[2]

    @pl.when(part == 0)
    def _():
        eb = (factor_ref[:, 1:2] * up_ref[...].astype(F32)).astype(BF)
        eb_ref[...] = eb
        sums_ref[2:3] = column_sum(eb.astype(F32))
        total[...] = jnp.zeros_like(total)

    w1 = load(w1_refs, core, held1)
    w2 = load(w2_refs, core, held2)
    du = (nn(eb_ref[...], w2) * slope_ref[...]).astype(BF)
    du_ref[...] = du
    sums_ref[pl.ds(3 + part, 1), :] = column_sum(du.astype(F32))
    total[...] += nt(du, w1)

    @pl.when(part == 3)
    def _():
        scaled, inverse = centered(mid_ref[...].astype(F32))
        dn = total[...]
        sums_ref[0:1] = column_sum(dn * scaled)
        sums_ref[1:2] = column_sum(dn)
        up = up_ref[...].astype(F32) + normalize_back(dn, scaled, inverse, vec_ref[5:6])
        up = up.astype(BF)
        out_ref[...] = up
        eba = (factor_ref[:, 0:1] * up.astype(F32)).astype(BF)
        eba_ref[...] = eba
        sums_ref[7:8] = column_sum(eba.astype(F32))
        do_ref[...] = nt(eba, load(wo_refs, core, held1)).astype(BF)


def feed_back(at, up, mid, vec, factor, slope, wa, w1, w2):
    rows, width = up.shape
    whole = pl.BlockSpec((rows, width), lambda p: (0, 0))
    part = pl.BlockSpec((None, rows, width), lambda p: (p, 0, 0))
    flat = jax.ShapeDtypeStruct((rows, width), BF)
    return pl.pallas_call(
        functools.partial(feed_back_kernel, [len(w[1]) for w in (wa, w1, w2)]),
        grid=(4,),
        in_specs=[
            SMEM,
            whole,
            whole,
            pl.BlockSpec(vec.shape, lambda p: (0, 0)),
            pl.BlockSpec(factor.shape, lambda p: (0, 0)),
            part,
        ]
        + view(wa, lambda p: 3)
        + view(w1, lambda p: p)
        + view(w2, lambda p: p),
        out_specs=[whole, part, whole, whole, whole, pl.BlockSpec((8, width), lambda p: (0, 0))],
        out_shape=[
            flat,
            jax.ShapeDtypeStruct((4, rows, width), BF),
            flat,
            flat,
            flat,
            jax.ShapeDtypeStruct((8, width), F32),
        ],
        scratch_shapes=[pltpu.VMEM((rows, width), F32)] + [pltpu.VMEM((width, width), BF)] * 2,
        compiler_params=pltpu.CompilerParams(vmem_limit_bytes=VMEM_LIMIT),
        cost_estimate=cost(17),
        name="feed_back",
    )(at, up, mid, vec, factor, slope, *wa[1], *w1[1], *w2[1])


def project_back_kernel(count, at_ref, up_ref, hidden_ref, vec_ref, joined_ref, *refs):
    out_ref, sums_ref, total, held = refs[count:]
    part = pl.program_id(0)
    grad = nt(joined_ref[...], load(refs[:count], at_ref[2], held))
    sums_ref[pl.ds(2 + part, 1), :] = column_sum(joined_ref[...].astype(F32))

    @pl.when(part == 0)
    def _():
        total[...] = grad

    @pl.when(part > 0)
    def _():
        total[...] += grad

    @pl.when(part == 2)
    def _():
        scaled, inverse = centered(hidden_ref[...].astype(F32))
        dn = total[...]
        sums_ref[0:1] = column_sum(dn * scaled)
        sums_ref[1:2] = column_sum(dn)
        up = up_ref[...].astype(F32) + normalize_back(dn, scaled, inverse, vec_ref[0:1])
        out_ref[...] = up.astype(BF)


def project_back(at, up, hidden, vec, joined, wa):
    rows, width = up.shape
    whole = pl.BlockSpec((rows, width), lambda p: (0, 0))
    return pl.pallas_call(
        functools.partial(project_back_kernel, len(wa[1])),
        grid=(3,),
        in_specs=[
            SMEM,
            whole,
            whole,
            pl.BlockSpec(vec.shape, lambda p: (0, 0)),
            pl.BlockSpec((None, rows, width), lambda p: (p, 0, 0)),
        ]
        + view(wa, lambda p: p),
        out_specs=[whole, pl.BlockSpec((8, width), lambda p: (0, 0))],
        out_shape=[
            jax.ShapeDtypeStruct((rows, width), BF),
            jax.ShapeDtypeStruct((8, width), F32),
        ],
        scratch_shapes=[pltpu.VMEM((rows, width), F32), pltpu.VMEM((width, width), BF)],
        compiler_params=pltpu.CompilerParams(vmem_limit_bytes=VMEM_LIMIT),
        cost_estimate=cost(8),
        name="project_back",
    )(at, up, hidden, vec, joined, *wa[1])


def attention(joined, code_q, code_k):
    _, rows, width = joined.shape
    parts = [pl.BlockSpec((None, rows, 2 * HD), functools.partial(lambda n, i: (n, 0, i), n)) for n in range(3)]
    pair = pl.BlockSpec((rows, 2 * HD), lambda i: (0, i))
    whole = pl.BlockSpec((rows, 2 * HD), lambda i: (0, 0))
    return pl.pallas_call(
        attention_kernel,
        grid=(width // (2 * HD),),
        in_specs=parts + [whole, whole],
        out_specs=[pair, pl.BlockSpec((None, rows, 2), lambda i: (i, 0, 0))],
        out_shape=[
            jax.ShapeDtypeStruct((rows, width), BF),
            jax.ShapeDtypeStruct((width // (2 * HD), rows, 2), F32),
        ],
        compiler_params=pltpu.CompilerParams(vmem_limit_bytes=VMEM_LIMIT),
        cost_estimate=cost(15),
        name="attention",
    )(joined, joined, joined, code_q, code_k)


def attention_back(joined, do, lse, code_q, code_k):
    _, rows, width = joined.shape
    parts = [pl.BlockSpec((None, rows, 2 * HD), functools.partial(lambda n, i: (n, 0, i), n)) for n in range(3)]
    pair = pl.BlockSpec((rows, 2 * HD), lambda i: (0, i))
    whole = pl.BlockSpec((rows, 2 * HD), lambda i: (0, 0))
    return pl.pallas_call(
        attention_back_kernel,
        grid=(width // (2 * HD),),
        in_specs=parts + [pair, pl.BlockSpec((None, rows, 2), lambda i: (i, 0, 0)), whole, whole],
        out_specs=pl.BlockSpec((3, rows, 2 * HD), lambda i: (0, 0, i)),
        out_shape=jax.ShapeDtypeStruct((3, rows, width), BF),
        compiler_params=pltpu.CompilerParams(vmem_limit_bytes=VMEM_LIMIT),
        cost_estimate=cost(19),
        name="attention_back",
    )(joined, joined, joined, do, lse, code_q, code_k)


def which(xy, turn, at):
    s = at[0]
    quarter = jnp.where(xy == 0, s & 2, 1 + 2 * (s & 1))
    side = jnp.where(xy == 0, s & 1, s >> 1)
    return quarter, side ^ turn


def spread(product, own, keep_ref, send_ref, held):
    held[...] = product
    share = held.shape[0] // 8
    for chip in range(4):
        mine = pl.multiple_of((2 * chip + own) * share, share)
        other = pl.multiple_of((2 * chip + 1 - own) * share, share)
        keep_ref[chip, :share] = held[pl.ds(mine, share), :].astype(BF)
        send_ref[chip, :share] = held[pl.ds(other, share), :].astype(BF)


def spread_all(product, xy, turn, mine_ref, x_ref, y_ref):
    share = product.shape[0] // 8
    rows = [product[n * share : (n + 1) * share].astype(BF) for n in range(8)]
    for ref, here in (
        (mine_ref, turn == 0),
        (x_ref, jnp.logical_and(turn == 1, xy == 0)),
        (y_ref, jnp.logical_and(turn == 1, xy == 1)),
    ):

        @pl.when(here)
        def _(ref=ref):
            for n in range(8):
                ref[n] = rows[n]


def attention_weight_kernel(rows_too, at_ref, a_ref, o_ref, joined_ref, eb_ref, *rest):
    turned, held = rest[-2:]
    share = held.shape[0] // 8
    if rows_too:
        keep_ref, send_ref = rest[-4:-2]
        for chip in range(4):
            keep_ref[chip, share:] = rest[0][2 * chip + at_ref[2]]
            send_ref[chip, share:] = rest[0][2 * chip + 1 - at_ref[2]]
    xy, turn = pl.program_id(0), pl.program_id(1)
    last = which(xy, turn, at_ref)[0] == 3

    @pl.when(jnp.logical_and(turn == 0, last))
    def _():
        turned[...] = o_ref[...].T

    @pl.when(jnp.logical_and(turn == 0, jnp.logical_not(last)))
    def _():
        turned[...] = a_ref[...].T

    right = jnp.where(last, eb_ref[...], joined_ref[...])
    product = nn(turned[...], right)
    if rows_too:
        spread(product, at_ref[2], keep_ref, send_ref, held)
    else:
        spread_all(product, xy, turn, *rest[-5:-2])


def weight_outs(count, rows, width, more=0):
    share, half = width // 8 + more, width // 2
    shape = jax.ShapeDtypeStruct((2, 2, 4, count, share, half), BF)
    block = (None, None, 4, None, share, half)
    scratch = [pltpu.VMEM((width, rows), BF), pltpu.VMEM((width, half), F32)]
    return [shape, shape], block, scratch


def load_into(refs, core, target):
    if len(refs) == 1:
        n, share, width = refs[0].shape
        target[...] = refs[0][...].reshape(n * share, width)
        return target[...]
    return load(refs, core, target)


def wide_half(ref, quarter, half, columns):
    return ref[quarter, :, pl.ds(pl.multiple_of(half * columns, 128), columns)]


def feed_both_kernel(counts, at_ref, hidden_ref, o_ref, up_ref, vec_ref, factor_ref, *refs):
    wo_refs, w1_refs, w2_refs, refs = cut(refs, counts)
    out_ref, back_ref, eba_ref, do_ref, sums_ref, mine_ref, x_ref, y_ref = refs[:8]
    total, w1, w2, held, normed, mid_held, eb, gb, slope, du, turned = refs[8:]
    step = pl.program_id(0)
    core = at_ref[2]

    @pl.when(step == 0)
    def _():
        branch = nn(o_ref[...], load(wo_refs, core, held)) + vec_ref[4:5]
        mid = (hidden_ref[...].astype(F32) + factor_ref[:, 0:1] * branch).astype(BF)
        mid_held[...] = mid
        scaled, _ = centered(mid.astype(F32))
        normed[...] = (scaled * vec_ref[5:6] + vec_ref[6:7]).astype(BF)
        total[...] = jnp.zeros_like(total)

    @pl.when(step < 4)
    def _():
        u = nn(normed[...], load_into(w1_refs, core, w1.at[step])) + vec_ref[pl.ds(8 + step, 1), :]
        cdf = 0.5 * (1.0 + lax.erf(u * root_half))
        active = (u * cdf).astype(BF)
        gb[step] = active
        slope[step] = cdf + u * jnp.exp(-0.5 * u * u) * normal_peak
        total[...] += nt(active, load_into(w2_refs, core, w2.at[step]))

    @pl.when(step == 3)
    def _():
        branch = total[...] + vec_ref[7:8]
        out_ref[...] = (mid_held[...].astype(F32) + factor_ref[:, 1:2] * branch).astype(BF)
        own = (factor_ref[:, 1:2] * up_ref[...].astype(F32)).astype(BF)
        eb[...] = own
        sums_ref[2:3] = column_sum(own.astype(F32))
        total[...] = jnp.zeros_like(total)
        turned[0] = normed[...].T
        turned[1] = own.T

    @pl.when(jnp.logical_and(step >= 4, step < 8))
    def _():
        part = step - 4
        own = (nn(eb[...], w2[part]) * slope[part]).astype(BF)
        du[part] = own
        sums_ref[pl.ds(3 + part, 1), :] = column_sum(own.astype(F32))
        total[...] += nt(own, w1[part])

    @pl.when(step == 7)
    def _():
        scaled, inverse = centered(mid_held[...].astype(F32))
        dn = total[...]
        sums_ref[0:1] = column_sum(dn * scaled)
        sums_ref[1:2] = column_sum(dn)
        up = up_ref[...].astype(F32) + normalize_back(dn, scaled, inverse, vec_ref[5:6])
        up = up.astype(BF)
        back_ref[...] = up
        eba = (factor_ref[:, 0:1] * up.astype(F32)).astype(BF)
        eba_ref[...] = eba
        sums_ref[7:8] = column_sum(eba.astype(F32))
        do_ref[...] = nt(eba, load(wo_refs, core, held)).astype(BF)

    share, half = mine_ref.shape[1:]
    for mat, source in ((0, du), (1, gb)):

        @pl.when(jnp.logical_and(step >= 8 + 2 * mat, step < 10 + 2 * mat))
        def _(mat=mat, source=source):
            xy = (step - 8) % 2
            for turn in range(2):
                quarter, column = which(xy, turn, at_ref)
                product = nn(turned[mat], wide_half(source, quarter, column, half)).astype(BF)
                rows = [product[n * share : (n + 1) * share] for n in range(8)]
                for ref, here in ((mine_ref, turn == 0), (x_ref, xy == 0), (y_ref, xy == 1)):
                    if turn == 0 and ref is mine_ref:
                        for n in range(8):
                            ref[n] = rows[n]
                    elif turn == 1 and ref is not mine_ref:

                        @pl.when(here)
                        def _(ref=ref):
                            for n in range(8):
                                ref[n] = rows[n]


def feed_both(at, hidden, o, up, vec, factor, wa, w1, w2):
    rows, width = hidden.shape
    share, half = width // 8, width // 2
    whole = pl.BlockSpec((rows, width), lambda t: (0, 0))
    once = pl.BlockSpec((rows, width), lambda t: (0, 0), pipeline_mode=pl.Buffered(1))
    flat = jax.ShapeDtypeStruct((rows, width), BF)

    def mat_of(t):
        return jnp.maximum(t - 8, 0) // 2

    return pl.pallas_call(
        functools.partial(feed_both_kernel, [len(w[1]) for w in (wa, w1, w2)]),
        grid=(12,),
        in_specs=[
            SMEM,
            once,
            once,
            once,
            pl.BlockSpec(vec.shape, lambda t: (0, 0)),
            pl.BlockSpec(factor.shape, lambda t: (0, 0)),
        ]
        + view(wa, lambda t: 3)
        + view(w1, lambda t: jnp.minimum(t, 3))
        + view(w2, lambda t: jnp.minimum(t, 3)),
        out_specs=[whole] * 4
        + [
            pl.BlockSpec((8, width), lambda t: (0, 0)),
            pl.BlockSpec(
                (8, None, None, share, half), lambda t: (0, jnp.maximum(t - 8, 0) % 2, mat_of(t), 0, 0)
            ),
            pl.BlockSpec((8, None, share, half), lambda t: (0, mat_of(t), 0, 0)),
            pl.BlockSpec((8, None, share, half), lambda t: (0, mat_of(t), 0, 0)),
        ],
        out_shape=[flat] * 4
        + [
            jax.ShapeDtypeStruct((8, width), F32),
            jax.ShapeDtypeStruct((8, 2, 2, share, half), BF),
            jax.ShapeDtypeStruct((8, 2, share, half), BF),
            jax.ShapeDtypeStruct((8, 2, share, half), BF),
        ],
        scratch_shapes=[
            pltpu.VMEM((rows, width), F32),
            pltpu.VMEM((4, width, width), BF),
            pltpu.VMEM((4, width, width), BF),
            pltpu.VMEM((width, width), BF),
            pltpu.VMEM((rows, width), BF),
            pltpu.VMEM((rows, width), BF),
            pltpu.VMEM((rows, width), BF),
            pltpu.VMEM((4, rows, width), BF),
            pltpu.VMEM((4, rows, width), F32),
            pltpu.VMEM((4, rows, width), BF),
            pltpu.VMEM((2, width, rows), BF),
        ],
        compiler_params=pltpu.CompilerParams(vmem_limit_bytes=60 * 2**20),
        cost_estimate=cost(34),
        name="feed_both",
    )(at, hidden, o, up, vec, factor, *wa[1], *w1[1], *w2[1])


def feed_back_whole_kernel(
    counts, at_ref, up_ref, mid_ref, a_ref, vec_ref, factor_ref, slope_ref, gb_ref, *refs
):
    wo_refs, w1_refs, w2_refs, refs = cut(refs, counts)
    back_ref, eba_ref, do_ref, sums_ref, keep_ref, send_ref = refs[:6]
    total, held1, held2, eb, du, turned, held = refs[6:]
    step = pl.program_id(0)
    core = at_ref[2]

    @pl.when(step == 0)
    def _():
        own = (factor_ref[:, 1:2] * up_ref[...].astype(F32)).astype(BF)
        eb[...] = own
        sums_ref[2:3] = column_sum(own.astype(F32))
        total[...] = jnp.zeros_like(total)
        turned[0] = a_ref[...].T
        turned[1] = own.T

    @pl.when(step < 4)
    def _():
        own = (nn(eb[...], load(w2_refs, core, held2)) * slope_ref[...]).astype(BF)
        du[step] = own
        sums_ref[pl.ds(3 + step, 1), :] = column_sum(own.astype(F32))
        total[...] += nt(own, load(w1_refs, core, held1))

    @pl.when(step == 3)
    def _():
        scaled, inverse = centered(mid_ref[...].astype(F32))
        dn = total[...]
        sums_ref[0:1] = column_sum(dn * scaled)
        sums_ref[1:2] = column_sum(dn)
        up = up_ref[...].astype(F32) + normalize_back(dn, scaled, inverse, vec_ref[5:6])
        up = up.astype(BF)
        back_ref[...] = up
        eba = (factor_ref[:, 0:1] * up.astype(F32)).astype(BF)
        eba_ref[...] = eba
        sums_ref[7:8] = column_sum(eba.astype(F32))
        do_ref[...] = nt(eba, load(wo_refs, core, held1)).astype(BF)

    half = keep_ref.shape[-1]
    for mat in range(2):

        @pl.when(jnp.logical_and(step >= 4 + 2 * mat, step < 6 + 2 * mat))
        def _(mat=mat):
            for turn in range(2):
                quarter, column = which((step - 4) % 2, turn, at_ref)
                if mat == 0:
                    right = wide_half(du, quarter, column, half)
                else:
                    right = gb_ref[:, pl.ds(pl.multiple_of(column * half, 128), half)]
                spread(nn(turned[mat], right), core, keep_ref.at[turn], send_ref.at[turn], held)


def feed_back_whole(at, up, mid, a, vec, factor, slope, gb, wa, w1, w2):
    rows, width = up.shape
    share, half = width // 8, width // 2
    whole = pl.BlockSpec((rows, width), lambda t, at: (0, 0))
    once = pl.BlockSpec((rows, width), lambda t, at: (0, 0), pipeline_mode=pl.Buffered(1))
    flat = jax.ShapeDtypeStruct((rows, width), BF)

    def scalars_too(specs):
        return [
            pl.BlockSpec(spec.block_shape, functools.partial(lambda f, t, at: f(t), spec.index_map))
            for spec in specs
        ]

    def gb_at(t, at):
        return which(jnp.where(t == 7, 1, 0), 0, at)[0], 0, 0

    chunk = pl.BlockSpec(
        (None, 2, 4, None, share, half),
        lambda t, at: (jnp.maximum(t - 4, 0) % 2, 0, 0, jnp.maximum(t - 4, 0) // 2, 0, 0),
    )
    return pl.pallas_call(
        functools.partial(feed_back_whole_kernel, [len(w[1]) for w in (wa, w1, w2)]),
        grid_spec=pltpu.PrefetchScalarGridSpec(
            num_scalar_prefetch=1,
            grid=(8,),
            in_specs=[
                once,
                once,
                once,
                pl.BlockSpec(vec.shape, lambda t, at: (0, 0)),
                pl.BlockSpec(factor.shape, lambda t, at: (0, 0)),
                pl.BlockSpec((None, rows, width), lambda t, at: (jnp.minimum(t, 3), 0, 0)),
                pl.BlockSpec((None, rows, width), gb_at),
            ]
            + scalars_too(
                view(wa, lambda t: 3)
                + view(w1, lambda t: jnp.minimum(t, 3))
                + view(w2, lambda t: jnp.minimum(t, 3))
            ),
            out_specs=[whole] * 3 + [pl.BlockSpec((8, width), lambda t, at: (0, 0)), chunk, chunk],
            scratch_shapes=[
                pltpu.VMEM((rows, width), F32),
                pltpu.VMEM((width, width), BF),
                pltpu.VMEM((width, width), BF),
                pltpu.VMEM((rows, width), BF),
                pltpu.VMEM((4, rows, width), BF),
                pltpu.VMEM((2, width, rows), BF),
                pltpu.VMEM((width, half), F32),
            ],
        ),
        out_shape=[flat] * 3
        + [jax.ShapeDtypeStruct((8, width), F32)]
        + [jax.ShapeDtypeStruct((2, 2, 4, 2, share, half), BF)] * 2,
        compiler_params=pltpu.CompilerParams(vmem_limit_bytes=60 * 2**20),
        cost_estimate=cost(22),
        name="feed_back_whole",
    )(at, up, mid, a, vec, factor, slope, gb, *wa[1], *w1[1], *w2[1])


def owner_outs(count, rows, width, mat):
    share, half = width // 8, width // 2
    shapes = [jax.ShapeDtypeStruct((8, 2, count, share, half), BF)]
    shapes += [jax.ShapeDtypeStruct((8, count, share, half), BF)] * 2
    outs = [
        pl.BlockSpec((8, None, None, share, half), lambda *i: (0, i[-3], mat(*i), 0, 0)),
        pl.BlockSpec((8, None, share, half), lambda *i: (0, mat(*i), 0, 0)),
        pl.BlockSpec((8, None, share, half), lambda *i: (0, mat(*i), 0, 0)),
    ]
    return shapes, outs


def attention_weights_grad(at, a, o, joined, eb, vector_rows=None):
    rows, width = a.shape
    count = 1
    more = 0 if vector_rows is None else vector_rows.shape[1]
    shapes, block, scratch = weight_outs(count, rows, width, more)
    whole = pl.BlockSpec((rows, width), lambda i, j, at: (0, 0))

    def joined_at(i, j, at):
        quarter, half = which(i, j, at)
        return jnp.minimum(quarter, 2), 0, half

    if vector_rows is None:
        shapes, outs = owner_outs(count, rows, width, lambda i, j, at: 0)
        extra, extra_specs = (), []
    else:
        outs = [pl.BlockSpec(block, lambda i, j, at: (i, j, 0, 0, 0, 0))] * 2
        extra = (vector_rows,)
        extra_specs = [pl.BlockSpec(vector_rows.shape, lambda i, j, at: (0, 0, 0))]
    return pl.pallas_call(
        functools.partial(attention_weight_kernel, vector_rows is not None),
        grid_spec=pltpu.PrefetchScalarGridSpec(
            num_scalar_prefetch=1,
            grid=(2, 2),
            in_specs=[
                whole,
                whole,
                pl.BlockSpec((None, rows, width // 2), joined_at),
                pl.BlockSpec((rows, width // 2), lambda i, j, at: (0, which(i, j, at)[1])),
            ]
            + extra_specs,
            out_specs=outs,
            scratch_shapes=scratch,
        ),
        out_shape=shapes,
        compiler_params=pltpu.CompilerParams(vmem_limit_bytes=VMEM_LIMIT),
        cost_estimate=cost(8),
        name="attention_weights",
    )(at, a, o, joined, eb, *extra)


def units_kernel(*refs):
    out_ref, slot = refs[-1], 0
    for mine_ref, x_ref, y_ref in (refs[:3], refs[3:6]):
        count = x_ref.shape[0]
        for xy, got in enumerate((x_ref, y_ref)):
            total = mine_ref[xy].astype(F32) + got[...].astype(F32)
            out_ref[xy, slot : slot + count] = total.astype(BF)
        slot += count


def units_sum(*groups):
    specs, total = [], 0
    for mine, x_got, y_got in groups:
        owners, _, count, share, half = mine.shape
        one = pl.BlockSpec((None, count, share, half), lambda n: (n, 0, 0, 0))
        specs += [pl.BlockSpec((None, 2, count, share, half), lambda n: (n, 0, 0, 0, 0)), one, one]
        total += count
    return pl.pallas_call(
        units_kernel,
        grid=(owners,),
        in_specs=specs,
        out_specs=pl.BlockSpec((None, 2, total, share, half), lambda n: (n, 0, 0, 0, 0)),
        out_shape=jax.ShapeDtypeStruct((owners, 2, total, share, half), BF),
        cost_estimate=cost(6),
        name="units_sum",
    )(*[array for group in groups for array in group])


def adam_step(weight, first, second, gradient, rate, decay_on):
    mean_next = beta_one * first + (1.0 - beta_one) * gradient
    square_next = beta_two * second + (1.0 - beta_two) * gradient * gradient
    step_next = rate * (
        mean_next / bias_one / (jnp.sqrt(square_next / bias_two) + adam_eps) + decay_on * weight
    )
    return (mean_next, square_next, step_next)


def adam_update(weight, first_moment, second_moment, gradient, layer_rates, decay_on):
    rate = layer_rates.reshape((-1,) + (1,) * (weight.ndim - 1))
    return adam_step(weight, first_moment, second_moment, gradient, rate, decay_on)


def adam_kernel(layer, placed, at_ref, rate_ref, grad_ref, weight_ref, first_ref, second_ref, *rest):
    outs = rest[-4:]
    s = at_ref[0]
    half = grad_ref.shape[-1]
    order = ((0, 0), (1, 0), (0, 1), (2, 1), (2, 0), (3, 0), (1, 1), (3, 1))
    for n, (device, xy) in enumerate(order):
        at = pl.ds(n * half, half)
        gradient = grad_ref[device if placed else s ^ device, xy].astype(F32)
        new = adam_step(
            weight_ref[:, at], first_ref[:, at], second_ref[:, at], gradient, rate_ref[layer], decay_rate
        )
        for ref, value in zip(outs, (gradient,) + new):
            ref[:, at] = value


def adam(at, rates, gradient, weight, first, second, layer, slot, into):
    count = 1 if weight.ndim == 3 else weight.shape[1]
    share, columns = weight.shape[-2:]
    half = gradient.shape[-1]
    if weight.ndim == 3:
        spec = pl.BlockSpec((None, share, columns), lambda m, at, rates: (layer, 0, 0))
    else:
        spec = pl.BlockSpec((None, None, share, columns), lambda m, at, rates: (layer, m, 0, 0))
    extra = () if into is None else tuple(into)
    return pl.pallas_call(
        functools.partial(adam_kernel, layer, layer == 1),
        grid_spec=pltpu.PrefetchScalarGridSpec(
            num_scalar_prefetch=2,
            grid=(count,),
            in_specs=[
                pl.BlockSpec((4, 2, None, share, half), lambda m, at, rates: (0, 0, slot + m, 0, 0)),
                spec,
                spec,
                spec,
            ]
            + [pl.BlockSpec(memory_space=pl.ANY)] * len(extra),
            out_specs=[spec] * 4,
        ),
        out_shape=[jax.ShapeDtypeStruct(weight.shape, F32)] * 4,
        input_output_aliases={6 + n: n for n in range(len(extra))},
        compiler_params=pltpu.CompilerParams(vmem_limit_bytes=VMEM_LIMIT),
        cost_estimate=cost(6),
        name="adam",
    )(at, rates, gradient, weight, first, second, *extra)


def assemble_kernel(at_ref, own, *refs):
    out_ref, turns = refs[-1], refs[:-1]
    z, step = at_ref[1], pl.program_id(1)
    out_ref[z] = own[...]
    for place, k in enumerate(TURNS):
        far, x_far, y_far, d_left, d_right = turns[5 * place : 5 * place + 5]
        chip = lax.rem(z + 4 - k, 4)
        half = d_left.shape[-1]
        for n, source in enumerate((far, x_far, y_far)):

            @pl.when(step == n)
            def _(source=source, chip=chip):
                out_ref[chip] = source[...]

        @pl.when(step == 3)
        def _(d_left=d_left, d_right=d_right, chip=chip, half=half):
            out_ref[chip, :, :half] = d_left[...]
            out_ref[chip, :, half:] = d_right[...]


def assemble(at, own, turns, first):
    count, _, share, width = own.shape
    piece = pl.BlockSpec((share, width), lambda m, j, at: (first + m, 0))
    part = pl.BlockSpec((share, width // 2), lambda m, j, at: (first + m, 0))
    return pl.pallas_call(
        assemble_kernel,
        grid_spec=pltpu.PrefetchScalarGridSpec(
            num_scalar_prefetch=1,
            grid=(count, 4),
            in_specs=[pl.BlockSpec((None, None, share, width), lambda m, j, at: (m, at[0] ^ j, 0, 0))]
            + [piece, piece, piece, part, part] * 3,
            out_specs=pl.BlockSpec(
                (None, None, 4, share, width), lambda m, j, at: (m, at[0] ^ j, 0, 0, 0)
            ),
        ),
        out_shape=jax.ShapeDtypeStruct((count, 4, 4, share, width), BF),
        compiler_params=pltpu.CompilerParams(vmem_limit_bytes=VMEM_LIMIT),
        cost_estimate=cost(3 * count),
        name="assemble",
    )(at, own, *[array for turn in turns for array in turn])


def pack_kernel(at_ref, wa_ref, wf_ref, flat_ref, first_ref, second_ref, third_ref):
    share = wa_ref.shape[1]
    first_ref[:share] = wa_ref[0].astype(BF)
    first_ref[share:] = flat_ref[...]
    for n in range(2):
        second_ref[n * share : (n + 1) * share] = wf_ref[0, n].astype(BF)
        third_ref[n * share : (n + 1) * share] = wf_ref[1, n].astype(BF)
    second_ref[2 * share :] = wa_ref[1].astype(BF)


def pack(at, wa, wf, flat):
    layers, share, columns = wa.shape
    width = columns // 4
    shapes = [(share + flat.shape[0], width), (3 * share, width), (2 * share, width)]
    return pl.pallas_call(
        pack_kernel,
        grid_spec=pltpu.PrefetchScalarGridSpec(
            num_scalar_prefetch=1,
            grid=(1,),
            in_specs=[
                pl.BlockSpec((layers, share, width), lambda i, at: (0, 0, at[0])),
                pl.BlockSpec((layers, 2, share, width), lambda i, at: (0, 0, 0, at[0])),
                pl.BlockSpec(flat.shape, lambda i, at: (0, 0)),
            ],
            out_specs=[pl.BlockSpec(shape, lambda i, at: (0, 0)) for shape in shapes],
        ),
        out_shape=[jax.ShapeDtypeStruct(shape, BF) for shape in shapes],
        cost_estimate=cost(2),
        name="pack",
    )(at, wa, wf, flat)


def cast_kernel(weight_ref, out_ref):
    out_ref[...] = weight_ref[...].astype(BF)


def cast_blocks(weight, layer):
    share, columns = weight.shape[-2:]
    count = 1 if weight.ndim == 3 else weight.shape[1]
    if weight.ndim == 3:
        spec = pl.BlockSpec((None, share, columns // 4), lambda m, q: (layer, 0, q))
    else:
        spec = pl.BlockSpec((None, None, share, columns // 4), lambda m, q: (layer, m, 0, q))
    return pl.pallas_call(
        cast_kernel,
        grid=(count, 4),
        in_specs=[spec],
        out_specs=pl.BlockSpec((None, None, share, columns // 4), lambda m, q: (m, q, 0, 0)),
        out_shape=jax.ShapeDtypeStruct((count, 4, share, columns // 4), BF),
        cost_estimate=cost(3 * count),
        name="cast",
    )(weight)


def after(value, *others):
    return lax.optimization_barrier((value,) + others)[0]


def shards(
    patches,
    positions,
    image_sizes,
    keep_masks,
    output_grad,
    vector_params,
    attention_weights,
    feedforward_weights,
    vector_first,
    attention_first,
    feedforward_first,
    vector_second,
    attention_second,
    feedforward_second,
    layer_rates,
):
    both = ("section", "dp")
    micro_count, row_count, width = patches.shape
    layers = vector_params.shape[0]
    share = attention_weights.shape[1]
    half = width // 2
    s = lax.axis_index("section")
    d = lax.axis_index("dp")
    s_low, s_high = s % 2, s // 2
    unit = s_low ^ s_high
    across = [(i, i ^ 1) for i in range(4)]
    along = [(i, i ^ 2) for i in range(4)]
    athwart = [(i, i ^ 3) for i in range(4)]
    shards_dp = lax.axis_size("dp")
    tuned = shards_dp == 8
    around = [[(i, (i + 2 * k) % 8) for i in range(8)] for k in (1, 2, 3)]
    turned = [around[k - 1] for k in TURNS]
    swap = [(i, i ^ 1) for i in range(8)]
    at = jnp.stack([s, d // 2, d % 2]).astype(jnp.int32)
    z = d // 2

    def quarter(array):
        return lax.dynamic_slice_in_dim(array, s * width, width, axis=array.ndim - 1)

    if tuned:
        flat = vector_params.astype(BF).reshape(-1, share * 8)
        flat = jnp.pad(flat, ((0, 16 - flat.shape[0]), (0, 0)))
        first_sent, second_sent, third_sent = pack(at, attention_weights, feedforward_weights, flat)
        first = lax.all_gather(first_sent, both, axis=0, tiled=False)
        first = first.reshape(4, 8, -1, width)

        def along_z(sent, route):
            return lax.ppermute(sent, "dp", route)

        def around_xy(far):
            return lax.ppermute(far, "section", across), lax.ppermute(far, "section", along)

        def around_d(x_far, y_far):
            d_left = lax.ppermute(y_far[:, :half], "section", across)
            d_right = lax.ppermute(x_far[:, half:], "section", along)
            return d_left, d_right

        def swapped(half_rows):
            return (half_rows, lax.ppermute(half_rows, "dp", swap))

        fars, turns = [], []
        sent = second_sent
        for route in turned:
            far = along_z(sent, route)
            if fars:
                far, x_far, y_far = lax.optimization_barrier((far, *pending))
                turns.append((fars[-1], x_far, y_far))
            far, sent = lax.optimization_barrier((far, sent))
            pending = around_xy(far)
            fars.append(far)
        b_blocks = cast_blocks(feedforward_weights, 0)
        t_blocks, c_blocks = cast_blocks(attention_weights, 1), cast_blocks(feedforward_weights, 1)
        diagonals = [around_d(*turn[1:]) for turn in turns]
        x_far, y_far, *diagonals = lax.optimization_barrier((*pending, *diagonals))
        turns.append((fars[-1], x_far, y_far))
        diagonals.append(around_d(x_far, y_far))
        third_sent = after(third_sent, far)
        c_fars = [along_z(third_sent, route) for route in turned]
        first, b_blocks, t_blocks, c_blocks = lax.optimization_barrier(
            (first, b_blocks, t_blocks, c_blocks)
        )
        turns = [(*turn, *diagonal) for turn, diagonal in zip(turns, diagonals)]
        ordered = first[0, :, share:].reshape(8, -1)[:, : layers * 12 * share]
        ordered = ordered.reshape(8, layers, 12, share)
        vectors = ordered.transpose(1, 2, 0, 3).reshape(layers, 12, width).astype(F32)
        weights = [[("full", (first,), 0)], []]
    else:

        def gathered(piece):
            piece = lax.all_gather(quarter(piece).astype(BF), both, axis=0, tiled=True)
            return ("full", (piece.reshape(4, 1, width, width),), 0)

        vectors = lax.all_gather(vector_params.astype(BF), "dp", axis=2, tiled=True).astype(F32)
        weights = [
            (
                gathered(attention_weights[l]),
                gathered(feedforward_weights[l, 0]),
                gathered(feedforward_weights[l, 1]),
            )
            for l in range(layers)
        ]

    image_ids = lax.dynamic_index_in_dim(image_sizes[:, 0], unit, 0, keepdims=False)
    keep = lax.dynamic_index_in_dim(keep_masks[:, 0], unit, 0, keepdims=False)
    segment, member, inside, table_row = image_layout(image_ids, row_count)
    kept = jnp.sum(jnp.where(member[:, :, None], keep[None], 0), axis=1).astype(F32)
    factors = jnp.where(inside[:, None], kept / (1.0 - drop_rate), 1.0)
    patch_rows = lax.dynamic_index_in_dim(patches, unit, 0, keepdims=False).astype(F32)
    position_rows = jnp.take(positions, table_row, axis=0).astype(F32)
    hidden = patch_rows + jnp.where(inside[:, None], position_rows, 0.0)
    lane = jnp.arange(2 * HD, dtype=jnp.int32) % HD
    coded = lane[None, :] == segment[:, None]
    code_q = coded.astype(BF)
    code_k = jnp.where(coded | (lane[None, :] > image_sizes.shape[2]), 0.0, masked_score).astype(BF)

    saved = []
    output_rows = lax.dynamic_index_in_dim(output_grad, unit, 0, keepdims=False)
    for layer in range(layers):
        vec = vectors[layer]
        factor = factors[:, 2 * layer : 2 * layer + 2]
        a, joined = project(at, hidden, vec, weights[layer][0])
        if tuned and layer == 1:
            c_left, c_right, joined = lax.optimization_barrier((c_left, c_right, joined))
            c_turns = [
                tuple(array[2 * share * n : 2 * share * (n + 1)] for array in (c_all, c_x, c_y, c_left, c_right))
                for n in range(3)
            ]
            c_halves = swapped(assemble(at, c_blocks, c_turns, 0))
            joined = after(joined, c_halves[0])
            weights[1] += [("halves", c_halves, 0), ("halves", c_halves, 1)]
        o, lse = attention(joined, code_q, code_k)
        if tuned and layer == 0:
            o, *c_fars = lax.optimization_barrier((o, *c_fars))
            c_all = jnp.concatenate(c_fars)
            c_x, c_y = around_xy(c_all)
            b_halves = swapped(assemble(at, after(b_blocks, o), turns, 0))
            t_halves = swapped(assemble(at, after(t_blocks, b_halves[0]), turns, 2))
            weights[0] += [("halves", b_halves, 0), ("halves", b_halves, 1)]
            weights[1] += [("halves", t_halves, 0)]
            o = after(o, t_halves[0])
        wa, w1, w2 = weights[layer]
        if tuned and layer == 1:
            hidden, up1, eba1, do1, sums1, kept_feed, x_sent, y_sent = feed_both(
                at, hidden, o, output_rows, vec, factor, wa, w1, w2
            )
            saved.append((saved_hidden, a, joined, o, lse))
            break
        mid, a2, gb, slope, following = feed(at, hidden, o, vec, factor, wa, w1, w2)
        saved.append((hidden, a, joined, o, lse, mid, a2, gb, slope))
        hidden = following
        if tuned and layer == 0:
            c_x, c_y, hidden = lax.optimization_barrier((c_x, c_y, hidden))
            c_left, c_right = around_d(c_x, c_y)
            saved_hidden = hidden

    def pick(index, options):
        value = options[0]
        for n in range(1, len(options)):
            value = jnp.where(index == n, options[n], value)
        return value

    def outward(rows):
        blocks = [rows[:, i * (width // 4) : (i + 1) * (width // 4)] for i in range(4)]
        return pick(s, blocks), lax.ppermute(pick(s ^ 1, blocks), "section", across)

    def ordered_units(mine, theirs):
        return jnp.where(unit == 0, jnp.stack([mine, theirs]), jnp.stack([theirs, mine]))

    def over_units(here):
        return (
            lax.ppermute(here[0, 1], "section", across),
            lax.ppermute(here[1, 1], "section", along),
        )

    def added(kept_part, got):
        return (kept_part.astype(F32) + got.astype(F32)).astype(BF)

    def units_added(here, x_got, y_got):
        return (here[:, 0].astype(F32) + jnp.stack([x_got, y_got]).astype(F32)).astype(BF)

    def over_chips(summed):
        return [
            lax.ppermute(
                lax.dynamic_index_in_dim(summed, (z + k) % 4, 1, keepdims=False), "dp", route
            )
            for k, route in zip((1, 2, 3), around)
        ]

    def chips_added(summed, got):
        total = lax.dynamic_index_in_dim(summed, z, 1, keepdims=False).astype(F32)
        for part in got:
            total = total + part.astype(F32)
        return total.astype(BF)

    def over_sections(total):
        return [lax.ppermute(total, "section", route) for route in (across, along, athwart)]

    def joint(*values):
        return lax.optimization_barrier(values)

    def reduced_plainly(pairs):
        count = len(pairs)
        summed = []
        for xy, (side, route) in enumerate(((s_low, across), (s_high, along))):
            parts = [pair[xy].astype(BF) for pair in pairs]
            mine = [lax.dynamic_slice_in_dim(part, side * half, half, 1) for part in parts]
            other = [lax.dynamic_slice_in_dim(part, (1 - side) * half, half, 1) for part in parts]
            other = lax.ppermute(jnp.concatenate(other, axis=1), "section", route)
            summed.append((jnp.concatenate(mine, axis=1).astype(F32) + other.astype(F32)).astype(BF))
        stacked = jnp.concatenate(summed, axis=1)
        scattered = lax.psum_scatter(stacked, "dp", scatter_dimension=0, tiled=True)
        everyone = lax.all_gather(scattered, "section", axis=0, tiled=False)
        everyone = everyone.reshape(4, share, 2, count, half)
        order = ((0, 0), (1, 0), (0, 1), (2, 1), (2, 0), (3, 0), (1, 1), (3, 1))
        return [
            jnp.concatenate([everyone[dev, :, xy, mat] for dev, xy in order], axis=1).astype(F32)
            for mat in range(count)
        ]

    up = output_rows
    vector_rows = [None] * layers

    def put_rows(layer, attention_sums, feed_sums):
        vector_rows[layer] = jnp.concatenate(
            [attention_sums[0:3], attention_sums[4:5], feed_sums[7:8], feed_sums[0:7]]
        )

    def vectors_updated(vector_grad):
        return (vector_grad,) + adam_update(
            vector_params, vector_first, vector_second, vector_grad, layer_rates, 0.0
        )

    if tuned:
        wa, w1, w2 = weights[1]
        start, a, joined, o, lse = saved[1]
        up, eba, do, feed_sums = up1, eba1, do1, sums1
        do, kept_feed, x_sent, y_sent = joint(do, kept_feed, x_sent, y_sent)
        x_feed = lax.ppermute(x_sent, "section", across)
        y_feed = lax.ppermute(y_sent, "section", along)
        dqkv = attention_back(joined, do, lse, code_q, code_k)
        kept1, x_sent, y_sent = attention_weights_grad(at, a, o, dqkv, eba)
        x_feed, y_feed, kept1, x_sent, y_sent = joint(x_feed, y_feed, kept1, x_sent, y_sent)
        up = after(up, kept1)
        x_got = lax.ppermute(x_sent, "section", across)
        y_got = lax.ppermute(y_sent, "section", along)
        up, attention_sums = project_back(at, up, start, vectors[1], dqkv, wa)
        put_rows(1, attention_sums, feed_sums)
        x_got, y_got, up = joint(x_got, y_got, up)
        summed1 = units_sum((kept1, x_got, y_got), (kept_feed, x_feed, y_feed))
        total1 = lax.psum_scatter(summed1, "dp", scatter_dimension=0, tiled=True)
        up, summed1, hidden = joint(up, summed1, hidden)
        block_mine, block_theirs = outward(hidden)
        wa, w1, w2 = weights[0]
        start, a, joined, o, lse, mid, a2, gb, slope = saved[0]
        up, eba, do, feed_sums, kept2, sent2 = feed_back_whole(
            at, up, mid, a2, vectors[0], factors[:, 0:2], slope, gb, wa, w1, w2
        )
        sent2, kept2, do, block_theirs = joint(sent2, kept2, do, block_theirs)
        got2 = lax.ppermute(sent2, "dp", swap)
        here2 = added(kept2, got2)
        do = after(do, here2)
        x_got, y_got = over_units(here2)
        dqkv = attention_back(joined, do, lse, code_q, code_k)
        x_got, y_got, dqkv, total1 = joint(x_got, y_got, dqkv, total1)
        gradient1 = lax.all_gather(total1[0], "section", axis=0, tiled=False)
        summed2 = units_added(here2, x_got, y_got)
        dqkv = after(dqkv, summed2)
        z_got = over_chips(summed2)
        up, attention_sums = project_back(at, up, start, vectors[0], dqkv, wa)
        put_rows(0, attention_sums, feed_sums)
        rows_all = jnp.concatenate(vector_rows).astype(BF)
        lines = layers * 12 * share // half
        rows_all = rows_all.reshape(lines, half // share, 8, share).transpose(2, 0, 1, 3)
        rows_all = jnp.pad(rows_all.reshape(8, lines, half), ((0, 0), (0, 16 - lines), (0, 0)))
        dqkv, up, gradient1, *z_got = joint(dqkv, up, gradient1, *z_got)
        input_mine, input_theirs = outward(up)
        kept3, sent3 = attention_weights_grad(at, a, o, dqkv, eba, rows_all)
        kept3, sent3, input_theirs = joint(kept3, sent3, input_theirs)
        got3 = lax.ppermute(sent3, "dp", swap)
        here3 = added(kept3, got3)
        x_got, y_got = over_units(here3)
        x_got, y_got, *z_got = joint(x_got, y_got, *z_got)
        summed3 = units_added(here3, x_got, y_got)
        z_got3 = over_chips(summed3)
        total2 = after(chips_added(summed2, z_got), summed3)
        gradient1 = after(gradient1, total2)
        attention_out = adam(
            at, layer_rates, gradient1, attention_weights, attention_first,
            attention_second, 1, 0, None,
        )
        total2, gradient1 = joint(after(total2, attention_out[0]), gradient1)
        g_got2 = over_sections(total2)
        feed_out = adam(
            at, layer_rates, gradient1, feedforward_weights, feedforward_first,
            feedforward_second, 1, 1, None,
        )
        *z_got3, attention_out0, feed_out0 = joint(*z_got3, attention_out[0], feed_out[0])
        attention_out = [attention_out0] + list(attention_out[1:])
        feed_out = [feed_out0] + list(feed_out[1:])
        total3 = chips_added(summed3, z_got3)
        g_got3 = over_sections(total3[:, :, :share])
        vector_grad = total3[0, 0, share : share + lines].astype(F32)
        vector_grad = vector_grad.reshape(layers, 12, share)
        vector_out = vectors_updated(vector_grad)
        gradient2 = jnp.stack([total2] + g_got2)
        gradient2 = after(gradient2, total3)
        feed_out = adam(
            at, layer_rates, gradient2, feedforward_weights, feedforward_first,
            feedforward_second, 0, 0, feed_out,
        )
        *g_got3, feed_out0 = joint(*g_got3, feed_out[0])
        feed_out = [feed_out0] + list(feed_out[1:])
        gradient3 = jnp.stack([total3[:, :, :share]] + g_got3)
        attention_out = adam(
            at, layer_rates, gradient3, attention_weights, attention_first,
            attention_second, 0, 0, attention_out,
        )
    else:
        plain_attention, plain_feed = [None] * layers, [None] * layers
        block_mine, block_theirs = outward(hidden)

        def x_of(array):
            return jnp.where(s_high == 0, array[0], array[2])

        def y_of(array):
            return jnp.where(s_low == 0, array[1], array[3])

        for layer in reversed(range(layers)):
            wa, w1, w2 = weights[layer]
            start, a, joined, o, lse, mid, a2, gb, slope = saved[layer]
            factor = factors[:, 2 * layer : 2 * layer + 2]
            eb, du, up, eba, do, feed_sums = feed_back(
                at, up, mid, vectors[layer], factor, slope, wa, w1, w2
            )
            dqkv = attention_back(joined, do, lse, code_q, code_k)
            up, attention_sums = project_back(at, up, start, vectors[layer], dqkv, wa)
            put_rows(layer, attention_sums, feed_sums)
            all_four = jnp.concatenate([dqkv, eba[None]])
            plain_feed[layer] = jnp.stack(
                reduced_plainly(
                    [(tn(a2, x_of(du)), tn(a2, y_of(du))), (tn(eb, x_of(gb)), tn(eb, y_of(gb)))]
                )
            )
            y_left = jnp.where(s_low == 0, a, o)
            plain_attention[layer] = reduced_plainly(
                [(tn(a, x_of(all_four)), tn(y_left, y_of(all_four)))]
            )[0]
        rows_all = jnp.concatenate(vector_rows)
        rows_all = rows_all + lax.ppermute(rows_all, "section", across)
        rows_all = jnp.pad(rows_all, ((0, 128 - rows_all.shape[0]), (0, 0))).T
        vector_grad = lax.psum_scatter(rows_all, "dp", scatter_dimension=0, tiled=True)
        vector_out = vectors_updated(vector_grad[:, : layers * 12].T.reshape(layers, 12, share))
        input_mine, input_theirs = outward(up)
        gradient = jnp.stack(plain_attention)
        attention_out = (gradient,) + adam_update(
            attention_weights, attention_first, attention_second, gradient, layer_rates, decay_rate
        )
        gradient = jnp.stack(plain_feed)
        feed_out = (gradient,) + adam_update(
            feedforward_weights,
            feedforward_first,
            feedforward_second,
            gradient,
            layer_rates,
            decay_rate,
        )
    outs = [
        ordered_units(block_mine, block_theirs),
        ordered_units(input_mine, input_theirs).astype(F32),
    ]
    for group in zip(vector_out, attention_out, feed_out):
        outs.extend(group)
    return tuple(outs)


def solution(mesh):
    in_specs = (
        P(None, "dp", None),
        P(),
        P(None, "dp", None),
        P(None, "dp", None, None),
        P(None, "dp", None),
        P(None, None, "dp"),
        P(None, "dp", None),
        P(None, None, "dp", None),
        P(None, None, "dp"),
        P(None, "dp", None),
        P(None, None, "dp", None),
        P(None, None, "dp"),
        P(None, "dp", None),
        P(None, None, "dp", None),
        P(),
    )
    out_specs = (
        P(None, "dp", "section"),
        P(None, "dp", "section"),
        P(None, None, "dp"),
        P(None, "dp", None),
        P(None, None, "dp", None),
        P(None, None, "dp"),
        P(None, "dp", None),
        P(None, None, "dp", None),
        P(None, None, "dp"),
        P(None, "dp", None),
        P(None, None, "dp", None),
        P(None, None, "dp"),
        P(None, "dp", None),
        P(None, None, "dp", None),
    )
    return jax.shard_map(shards, mesh=mesh, in_specs=in_specs, out_specs=out_specs, check_vma=False)
```
